32 devices in a mesh: section: 2 (over core), space: 16 (over z, y, x).
Axes of the slice: x: 2, y: 2, z: 4, core: 2. Of those that a mesh axis runs over, the one named last changes fastest.
Arguments:
- fwd_in: bfloat16 [2, 64, 8, 8, 256], P('section', 'space'), may hold values from -6 to 6
- bwd_act: bfloat16 [2, 64, 8, 8, 256], P('section', 'space'), may hold values from -6 to 6
- bwd_grad: bfloat16 [2, 64, 8, 8, 256], P('section', 'space'), may hold values from -6 to 6
- fresh: bfloat16 [64, 8, 8, 256], P('space'), may hold values from -6 to 6
- target: bfloat16 [64, 8, 8, 256], P('space'), may hold values from -6 to 6
- w_first: bfloat16 [2, 27, 128, 128], P('section'), may hold values from -0.109375 to 0.109375
- w_second: bfloat16 [2, 27, 128, 128], P('section'), may hold values from -0.109375 to 0.109375
Outputs:
- fwd_out: bfloat16 [2, 64, 8, 8, 256], P('section', 'space')
- back_act: bfloat16 [2, 64, 8, 8, 256], P('section', 'space')
- back_grad: bfloat16 [2, 64, 8, 8, 256], P('section', 'space')
- grad_first: float32 [2, 3456, 128], P('section', 'space')
- grad_second: float32 [2, 3456, 128], P('section', 'space')
The draws below stay inside these ranges and needn't reach their ends.
All inputs are finite; a program needn't handle non-finite values.
Results may differ from the reference program's by a relative error of at most 0.01.
Values may be sent and summed in bfloat16 or wider, within the bound.
No kernel may reach another device: no remote copies, remote signals or barrier semaphores. Data moves between devices by JAX's collectives and lax.ppermute only.
A program may use at most 64 MiB of HBM per device.

```python
import math
import jax
import jax.numpy as jnp
from jax import lax

C = 128
YW = 8
ZW = 8
SECTIONS = 2
NX = 64


def shard_levels(rng, shape, cuts, smallest, top_value):
    factor_of, own = 1.0, jax.random.fold_in(rng, 6)
    for position, shards_of in cuts:
        steps = jnp.exp(jax.random.uniform(jax.random.fold_in(own, position), (shards_of,), jnp.float32, smallest / len(cuts), top_value / len(cuts)))
        factor_of = factor_of * jnp.repeat(steps, shape[position] // shards_of).reshape([-1 if axis == position else 1 for axis in range(len(shape))])
    return factor_of


def bell_draw(stream_key, extent, deviation, reach, cuts=(), dtype=jnp.bfloat16):
    factor_of = shard_levels(stream_key, extent, cuts, -0.22, 0.18) if cuts else 1.0
    array = jax.random.normal(stream_key, extent, jnp.float32) * deviation * factor_of
    return jnp.minimum(jnp.maximum(array, -reach), reach).astype(dtype)


def setup_inputs(seed: int = 0) -> dict:
    key_list = jax.random.split(jax.random.key(seed), 8)
    fwd_in = bell_draw(key_list[0], (SECTIONS, NX, YW, ZW, 2 * C), 1.0, 6.0, ((0, 2), (1, 16)))
    bwd_act = bell_draw(key_list[1], (SECTIONS, NX, YW, ZW, 2 * C), 1.0, 6.0, ((0, 2), (1, 16)))
    bwd_grad = bell_draw(key_list[2], (SECTIONS, NX, YW, ZW, 2 * C), 1.0, 6.0, ((0, 2), (1, 16)))
    fresh = bell_draw(key_list[3], (NX, YW, ZW, 2 * C), 1.0, 6.0, ((0, 16),))
    target = bell_draw(key_list[4], (NX, YW, ZW, 2 * C), 1.0, 6.0, ((0, 16),))
    w_first = bell_draw(key_list[5], (SECTIONS, 27, C, C), (27 * C) ** -0.5, 0.109375, ((0, 2),))
    w_second = bell_draw(key_list[6], (SECTIONS, 27, C, C), (27 * C) ** -0.5, 0.109375, ((0, 2),))
    return dict(fwd_in=fwd_in, bwd_act=bwd_act, bwd_grad=bwd_grad, fresh=fresh, target=target, w_first=w_first, w_second=w_second)


def smooth_gate(value):
    return 0.5 * value * (1.0 + jax.scipy.special.erf(value * 0.7071067811865476))

def gate_slope(value):
    return 0.5 * (1.0 + jax.scipy.special.erf(value * 0.7071067811865476)) + value * jnp.exp(-0.5 * value * value) * 0.3989422804014327

def conv_real(field, kernel):
    width = kernel.shape[2]
    shaped = kernel.reshape(3, 3, 3, kernel.shape[1], width)
    result = lax.conv_general_dilated(field[None], shaped, (1, 1, 1), [(1, 1), (1, 1), (1, 1)], dimension_numbers=('NDHWC', 'DHWIO', 'NDHWC'), precision=lax.Precision.HIGHEST)
    return result[0]

def section_tick(state, act, grad, first, second):
    width = first.shape[2]
    x_one = state[..., :width].astype(jnp.float32)
    x_two = state[..., width:].astype(jnp.float32)
    y_one = act[..., :width].astype(jnp.float32)
    y_two = act[..., width:].astype(jnp.float32)
    d_one = grad[..., :width].astype(jnp.float32)
    d_two = grad[..., width:]
    first_f = first.astype(jnp.float32)
    second_f = second.astype(jnp.float32)
    h_in = smooth_gate(x_two).astype(jnp.bfloat16)
    new_one = (x_one + conv_real(h_in.astype(jnp.float32), first_f)).astype(jnp.bfloat16)
    h_mid = smooth_gate(new_one.astype(jnp.float32)).astype(jnp.bfloat16)
    new_two = (x_two + conv_real(h_mid.astype(jnp.float32), second_f)).astype(jnp.bfloat16)
    g_out = smooth_gate(y_one).astype(jnp.bfloat16)
    image, pull_second = jax.vjp(conv_real, g_out.astype(jnp.float32), second_f)
    back_two = (y_two - image).astype(jnp.bfloat16)
    g_back = smooth_gate(back_two.astype(jnp.float32)).astype(jnp.bfloat16)
    image_b, pull_first = jax.vjp(conv_real, g_back.astype(jnp.float32), first_f)
    back_one = (y_one - image_b).astype(jnp.bfloat16)
    into_second, grad_second = pull_second(d_two.astype(jnp.float32))
    carry_one = (d_one + gate_slope(y_one) * into_second).astype(jnp.bfloat16)
    into_first, grad_first = pull_first(carry_one.astype(jnp.float32))
    carry_two = (d_two.astype(jnp.float32) + gate_slope(back_two.astype(jnp.float32)) * into_first).astype(jnp.bfloat16)
    forward = jnp.concatenate([new_one, new_two], axis=-1)
    rebuilt = jnp.concatenate([back_one, back_two], axis=-1)
    passed = jnp.concatenate([carry_one, carry_two], axis=-1)
    return (forward, rebuilt, passed, grad_first.reshape(-1, width), grad_second.reshape(-1, width))

def run_section(pack):
    return section_tick(pack[0], pack[1], pack[2], pack[3], pack[4])

def reference(fwd_in, bwd_act, bwd_grad, fresh, target, w_first, w_second):
    fwd_one, rebuilt_one, passed_one, first_one, second_one = lax.map(run_section, (fwd_in, bwd_act, bwd_grad, w_first, w_second))
    state_two = jnp.concatenate([fresh[None], fwd_one[:-1]], axis=0)
    own_grad = (fwd_one[-1].astype(jnp.float32) - target.astype(jnp.float32)).astype(jnp.bfloat16)
    act_two = jnp.concatenate([rebuilt_one[1:], fwd_one[-1:]], axis=0)
    grad_two = jnp.concatenate([passed_one[1:], own_grad[None]], axis=0)
    fwd_two, rebuilt_two, passed_two, first_two, second_two = lax.map(run_section, (state_two, act_two, grad_two, w_first, w_second))
    factor = 1.0 / math.sqrt(NX * YW * ZW)
    return (fwd_two, rebuilt_two, passed_two, (first_one + first_two) * factor, (second_one + second_two) * factor)
```

```python
import math

import jax
import jax.numpy as jnp
from jax import lax
from jax.sharding import PartitionSpec as P


def extended(block, sides, width):
    for axis, dim in sides:
        count = lax.axis_size(axis)
        forward = [(i, i + 1) for i in range(count - 1)]
        backward = [(target, source) for source, target in forward]
        low = lax.ppermute(
            lax.slice_in_dim(block, block.shape[dim] - width, None, axis=dim), axis, forward
        )
        high = lax.ppermute(lax.slice_in_dim(block, 0, width, axis=dim), axis, backward)
        block = jnp.concatenate([low, block, high], axis=dim)
    return block


def from_behind(block, axis, distance):
    devices = range(lax.axis_size(axis))
    route = [(i - distance, i) for i in devices if i - distance in devices]
    return lax.ppermute(block, axis, route)


def smooth_gate(value):
    return 0.5 * value * (1.0 + jax.scipy.special.erf(value * 0.7071067811865476))


def gate_slope(value):
    return (
        0.5 * (1.0 + jax.scipy.special.erf(value * 0.7071067811865476))
        + value * jnp.exp(-0.5 * value * value) * 0.3989422804014327
    )


def pad_sides(field):
    return jnp.pad(field, ((0, 0), (1, 1), (1, 1), (0, 0)))


def joint_extend(fields):
    width = fields[0].shape[-1]
    merged = extended(jnp.concatenate(fields, axis=-1), (("space", 0),), 1)
    padded = pad_sides(merged)
    return tuple((padded[..., index * width : (index + 1) * width] for index in range(len(fields))))


def depth_stack(padded):
    depth = padded.shape[2] - 2
    return jnp.concatenate([padded[:, :, shift : shift + depth, :] for shift in range(3)], axis=-1)


def convolve(padded, weights):
    rows_x = padded.shape[0] - 2
    rows_y = padded.shape[1] - 2
    depth = padded.shape[2] - 2
    width = weights.shape[2]
    stacked = depth_stack(padded)
    wide = weights.reshape(9, 3 * weights.shape[1], width)
    total = jnp.zeros((rows_x * rows_y * depth, width), jnp.float32)
    for across in range(3):
        for down in range(3):
            block = stacked[across : across + rows_x, down : down + rows_y].reshape(
                -1, stacked.shape[-1]
            )
            total = total + jnp.dot(
                block, wide[across * 3 + down], preferred_element_type=jnp.float32
            )
    return total.reshape(rows_x, rows_y, depth, width)


def correlate(padded, incoming):
    rows_x = padded.shape[0] - 2
    rows_y = padded.shape[1] - 2
    stacked = depth_stack(padded)
    flat = incoming.reshape(-1, incoming.shape[-1])
    blocks = []
    for across in range(3):
        for down in range(3):
            block = stacked[across : across + rows_x, down : down + rows_y].reshape(
                -1, stacked.shape[-1]
            )
            blocks.append(
                lax.dot_general(
                    block, flat, (((0,), (0,)), ((), ())), preferred_element_type=jnp.float32
                )
            )
    return jnp.concatenate(blocks, axis=0)


def reduce_blocks(grads):
    count = lax.axis_size("space")
    bits = [1 << level for level in range(count.bit_length() - 1)]
    spot = lax.axis_index("space")
    rows = grads.shape[1]
    ways = 3 if rows % 3 == 0 else 1
    span = rows // ways
    parts = []
    for way in range(ways):
        shift = way % len(bits)
        order = bits[shift:] + bits[:shift]
        part = grads[:, way * span : (way + 1) * span].reshape(
            [2] * len(bits) + [span, grads.shape[2]]
        )
        parts.append((part, order))
    for step in range(len(bits)):
        fresh_parts = []
        for part, order in parts:
            bit = order[step]
            left = sorted(order[step:], reverse=True)
            axis = left.index(bit)
            mine = (spot // bit) % 2
            keep = lax.dynamic_index_in_dim(part, mine, axis, keepdims=False)
            send = lax.dynamic_index_in_dim(part, 1 - mine, axis, keepdims=False)
            got = lax.ppermute(send, "space", [(i, i ^ bit) for i in range(count)])
            total = keep.astype(jnp.float32) + got.astype(jnp.float32)
            if step < len(bits) - 1:
                total = total.astype(jnp.bfloat16)
            fresh_parts.append((total, order))
        parts = fresh_parts
    return jnp.concatenate([part for part, _ in parts], axis=0)


def shards(fwd_in, bwd_act, bwd_grad, fresh, target, w_first, w_second):
    width = w_first.shape[2]
    first = w_first[0]
    second = w_second[0]
    first_back = jnp.transpose(first[::-1], (0, 2, 1))
    second_back = jnp.transpose(second[::-1], (0, 2, 1))
    last_section = lax.axis_size("section") - 1
    place = lax.axis_index("section")

    def tick(state, act, grad):
        x_one = state[..., :width].astype(jnp.float32)
        x_two = state[..., width:].astype(jnp.float32)
        y_one = act[..., :width].astype(jnp.float32)
        y_two = act[..., width:].astype(jnp.float32)
        d_one = grad[..., :width].astype(jnp.float32)
        d_two = grad[..., width:]
        h_in = smooth_gate(x_two).astype(jnp.bfloat16)
        g_out = smooth_gate(y_one).astype(jnp.bfloat16)
        h_pad, g_pad, d_pad = joint_extend((h_in, g_out, d_two))
        new_one = (x_one + convolve(h_pad, first)).astype(jnp.bfloat16)
        back_two = (y_two - convolve(g_pad, second)).astype(jnp.bfloat16)
        carry_one = (d_one + gate_slope(y_one) * convolve(d_pad, second_back)).astype(jnp.bfloat16)
        h_mid = smooth_gate(new_one.astype(jnp.float32)).astype(jnp.bfloat16)
        g_back = smooth_gate(back_two.astype(jnp.float32)).astype(jnp.bfloat16)
        m_pad, b_pad, c_pad = joint_extend((h_mid, g_back, carry_one))
        new_two = (x_two + convolve(m_pad, second)).astype(jnp.bfloat16)
        back_one = (y_one - convolve(b_pad, first)).astype(jnp.bfloat16)
        carry_two = (
            d_two.astype(jnp.float32)
            + gate_slope(back_two.astype(jnp.float32)) * convolve(c_pad, first_back)
        ).astype(jnp.bfloat16)
        forward = jnp.concatenate([new_one, new_two], axis=-1)
        rebuilt = jnp.concatenate([back_one, back_two], axis=-1)
        passed = jnp.concatenate([carry_one, carry_two], axis=-1)
        return (forward, rebuilt, passed, (b_pad, carry_one), (g_pad, d_two))

    fwd_one, rebuilt_one, passed_one, first_pair_one, second_pair_one = tick(
        fwd_in[0], bwd_act[0], bwd_grad[0]
    )
    lifted = from_behind(fwd_one, "section", 1)
    lowered = from_behind(jnp.stack([rebuilt_one, passed_one]), "section", -1)
    state_two = jnp.where(place == 0, fresh, lifted)
    own_grad = (fwd_one.astype(jnp.float32) - target.astype(jnp.float32)).astype(jnp.bfloat16)
    act_two = jnp.where(place == last_section, fwd_one, lowered[0])
    grad_two = jnp.where(place == last_section, own_grad, lowered[1])
    fwd_two, rebuilt_two, passed_two, first_pair_two, second_pair_two = tick(
        state_two, act_two, grad_two
    )
    cell_total = fwd_in.shape[1] * lax.axis_size("space") * fwd_in.shape[2] * fwd_in.shape[3]
    factor = 1.0 / math.sqrt(cell_total)
    first_sum = correlate(first_pair_one[0], first_pair_one[1]) + correlate(
        first_pair_two[0], first_pair_two[1]
    )
    second_sum = correlate(second_pair_one[0], second_pair_one[1]) + correlate(
        second_pair_two[0], second_pair_two[1]
    )
    count = lax.axis_size("space")
    blocks = jnp.concatenate(
        [(part * factor).astype(jnp.bfloat16).reshape(count, -1, width) for part in (first_sum, second_sum)],
        axis=1,
    )
    total = reduce_blocks(blocks)
    rows = total.shape[0] // 2
    first_total, second_total = total[:rows], total[rows:]
    return (
        fwd_two[None],
        rebuilt_two[None],
        passed_two[None],
        first_total[None],
        second_total[None],
    )


def solution(mesh):
    placed = (
        P("section", "space", None, None, None),
        P("section", "space", None, None, None),
        P("section", "space", None, None, None),
        P("space", None, None, None),
        P("space", None, None, None),
        P("section", None, None, None),
        P("section", None, None, None),
    )
    return jax.shard_map(
        shards,
        mesh=mesh,
        in_specs=placed,
        out_specs=(
            P("section", "space", None, None, None),
            P("section", "space", None, None, None),
            P("section", "space", None, None, None),
            P("section", "space", None),
            P("section", "space", None),
        ),
        check_vma=False,
    )
```

```python
import functools
import math

import jax
import jax.numpy as jnp
from jax import lax
from jax.experimental import pallas as pl
from jax.experimental.pallas import tpu as pltpu
from jax.sharding import PartitionSpec as P

VMEM = pltpu.CompilerParams(vmem_limit_bytes=48 * 1024 * 1024)
F32 = jnp.float32
BF16 = jnp.bfloat16


def half_erf(value):
    return 0.5 * (1.0 + lax.erf(value * 0.7071067811865476))


def smooth_gate(value):
    return value * half_erf(value)


def gate_slope(value, half):
    return half + value * jnp.exp(-0.5 * value * value) * 0.3989422804014327


def fill_shifts(stack, field, ydim, zdim):
    rows, width = field.shape
    cells = field.reshape(rows // zdim, zdim, width)
    depth = lax.broadcasted_iota(jnp.int32, cells.shape, 1)
    before = jnp.where(depth == 0, 0.0, pltpu.roll(cells, 1, 1))
    after = jnp.where(depth == zdim - 1, 0.0, pltpu.roll(cells, zdim - 1, 1))
    for across, moved in enumerate((before, cells, after)):
        moved = moved.reshape(rows // (ydim * zdim), ydim, zdim, width)
        blank = jnp.zeros_like(moved[:, :1])
        shifted = (
            jnp.concatenate([blank, moved[:, :-1]], axis=1),
            moved,
            jnp.concatenate([moved[:, 1:], blank], axis=1),
        )
        for down in range(3):
            at = (3 * down + across) * width
            stack[0:rows, at : at + width] = shifted[down].reshape(rows, width).astype(BF16)


def convolve(stack, weights, rows, plane):
    total = None
    for step in range(3):
        part = jnp.dot(
            stack[step * plane : step * plane + rows, :],
            weights[step],
            preferred_element_type=F32,
        )
        total = part if total is None else total + part
    return total


def pack_edges(state, act, grad, low, high, plane):
    width = state.shape[1] // 2
    cells = state.shape[0]
    left, right = slice(0, width), slice(width, 2 * width)
    for index, (source, half) in enumerate(((state, right), (act, left), (grad, right))):
        at = index * 2 * plane
        low[at : at + 2 * plane, :] = source[0 : 2 * plane, half]
        high[at : at + 2 * plane, :] = source[cells - 2 * plane : cells, half]
    for index, (source, half) in enumerate(((state, left), (act, right), (grad, left))):
        at = (6 + index) * plane
        low[at : at + plane, :] = source[0:plane, half]
        high[at : at + plane, :] = source[cells - plane : cells, half]


def edges_kernel(plane, state, act, grad, low, high):
    pack_edges(state, act, grad, low, high, plane)


def first_kernel(ydim, zdim, flags, state, act, grad, below, above, first, second, second_back,
                 new_one, back_two, mid, back, carry, gate, stack):
    plane = ydim * zdim
    cells, double = state.shape
    width = double // 2
    inner = cells + 2 * plane
    outer = cells + 4 * plane
    left, right = slice(0, width), slice(width, double)

    def two(source, half, index):
        at = index * 2 * plane
        return jnp.concatenate(
            [below[at : at + 2 * plane, :], source[:, half], above[at : at + 2 * plane, :]], axis=0
        ).astype(F32)

    def one(source, half, index):
        at = (6 + index) * plane
        return jnp.concatenate(
            [below[at : at + plane, :], source[:, half], above[at : at + plane, :]], axis=0
        ).astype(F32)

    low_flag, high_flag = flags[0], flags[1]

    def store_masked(ref, value):
        ref[0:plane, :] = (value[0:plane].astype(F32) * low_flag).astype(BF16)
        ref[plane : plane + cells, :] = value[plane : plane + cells]
        ref[plane + cells : inner, :] = (value[plane + cells :].astype(F32) * high_flag).astype(BF16)

    core = slice(plane, plane + cells)
    fill_shifts(stack, smooth_gate(two(state, right, 0)), ydim, zdim)
    f_one = (one(state, left, 0) + convolve(stack, first, inner, plane)).astype(BF16)
    new_one[...] = f_one[core]
    store_masked(mid, smooth_gate(f_one.astype(F32)).astype(BF16))

    y_one = two(act, left, 1)
    half = half_erf(y_one)
    gated = y_one * half
    gate[...] = gated[plane : plane + inner].astype(BF16)
    fill_shifts(stack, gated, ydim, zdim)
    r_two = (one(act, right, 1) - convolve(stack, second, inner, plane)).astype(BF16)
    back_two[...] = r_two[core]
    store_masked(back, smooth_gate(r_two.astype(F32)).astype(BF16))

    fill_shifts(stack, two(grad, right, 2), ydim, zdim)
    slope = gate_slope(y_one[plane : plane + inner], half[plane : plane + inner])
    e_one = (one(grad, left, 2) + slope * convolve(stack, second_back, inner, plane)).astype(BF16)
    store_masked(carry, e_one)


def second_kernel(ydim, zdim, state, act, grad, new_one, back_two, mid, back, carry, first, second,
                  first_back, forward, rebuilt, passed, stack):
    plane = ydim * zdim
    cells, double = state.shape
    width = double // 2
    left, right = slice(0, width), slice(width, double)
    forward[:, left] = new_one[...]
    rebuilt[:, right] = back_two[...]
    passed[:, left] = carry[plane : plane + cells, :]

    fill_shifts(stack, back[...].astype(F32), ydim, zdim)
    rebuilt[:, left] = (
        act[:, left].astype(F32) - convolve(stack, first, cells, plane)
    ).astype(BF16)
    fill_shifts(stack, carry[...].astype(F32), ydim, zdim)
    r_two = back_two[...].astype(F32)
    passed[:, right] = (
        grad[:, right].astype(F32)
        + gate_slope(r_two, half_erf(r_two)) * convolve(stack, first_back, cells, plane)
    ).astype(BF16)
    fill_shifts(stack, mid[...].astype(F32), ydim, zdim)
    forward[:, right] = (
        state[:, right].astype(F32) + convolve(stack, second, cells, plane)
    ).astype(BF16)


def correlate(stack, field, cotangent, ydim, zdim, emit):
    plane = ydim * zdim
    cells, width = cotangent.shape
    fill_shifts(stack, cotangent, ydim, zdim)
    for step in range(3):
        product = lax.dot_general(
            field[step * plane : step * plane + cells, :],
            stack[0:cells, :],
            (((0,), (0,)), ((), ())),
            preferred_element_type=F32,
        )
        for place in range(9):
            emit(9 * step + 8 - place, product[:, place * width : (place + 1) * width])


def corr_kernel(ydim, zdim, factor, last, *refs):
    if last:
        grad, back, carry, gate, so_far, out, stack = refs
    else:
        grad, back, carry, gate, out, stack = refs
    plane = ydim * zdim
    cells, double = grad.shape
    width = double // 2

    def store(which):
        def emit(k, block):
            at = slice(k * width, (k + 1) * width)
            if last:
                out[which, at, :] = ((block + so_far[which, at, :]) * factor).astype(out.dtype)
            else:
                out[which, at, :] = block

        return emit

    own = carry[plane : plane + cells, :].astype(F32)
    correlate(stack, back, own, ydim, zdim, store(0))
    correlate(stack, gate, grad[:, width:].astype(F32), ydim, zdim, store(1))


def whole(count):
    return [pl.BlockSpec(memory_space=pltpu.VMEM)] * count


def reduce_blocks(grads):
    count = lax.axis_size("space")
    bits = [1 << level for level in range(count.bit_length() - 1)]
    spot = lax.axis_index("space")
    rows = grads.shape[1]
    ways = 3 if rows % 3 == 0 else 1
    span = rows // ways
    parts = []
    for way in range(ways):
        shift = way % len(bits)
        order = bits[shift:] + bits[:shift]
        part = grads[:, way * span : (way + 1) * span].reshape(
            [2] * len(bits) + [span, grads.shape[2]]
        )
        parts.append((part, order))
    for step in range(len(bits)):
        fresh_parts = []
        for part, order in parts:
            bit = order[step]
            left = sorted(order[step:], reverse=True)
            axis = left.index(bit)
            mine = (spot // bit) % 2
            keep = lax.dynamic_index_in_dim(part, mine, axis, keepdims=False)
            send = lax.dynamic_index_in_dim(part, 1 - mine, axis, keepdims=False)
            got = lax.ppermute(send, "space", [(i, i ^ bit) for i in range(count)])
            total = keep.astype(jnp.float32) + got.astype(jnp.float32)
            if step < len(bits) - 1:
                total = total.astype(jnp.bfloat16)
            fresh_parts.append((total, order))
        parts = fresh_parts
    return jnp.concatenate([part for part, _ in parts], axis=0)


def shards(fwd_in, bwd_act, bwd_grad, fresh, target, w_first, w_second):
    width = w_first.shape[2]
    layers, ydim, zdim = fwd_in.shape[1:4]
    plane = ydim * zdim
    cells = layers * plane
    shape = fwd_in.shape[1:]
    flat = lambda block: block.reshape(cells, 2 * width)
    first = w_first[0].reshape(3, 9 * width, width)
    second = w_second[0].reshape(3, 9 * width, width)
    first_back = jnp.transpose(w_first[0][::-1], (0, 2, 1)).reshape(3, 9 * width, width)
    second_back = jnp.transpose(w_second[0][::-1], (0, 2, 1)).reshape(3, 9 * width, width)
    last_section = lax.axis_size("section") - 1
    place = lax.axis_index("section")
    count = lax.axis_size("space")
    spot = lax.axis_index("space")
    flags = jnp.stack([spot > 0, spot < count - 1]).astype(F32)
    up = [(i, i + 1) for i in range(count - 1)]
    down = [(i + 1, i) for i in range(count - 1)]
    array = jax.ShapeDtypeStruct
    edge = array((9 * plane, width), BF16)
    tile = array((cells, width), BF16)
    wide = array((cells + 2 * plane, width), BF16)
    state_shape = array((cells, 2 * width), BF16)
    offsets = 27 * width

    def exchange(low, high):
        below = lax.ppermute(high, "space", up)
        above = lax.ppermute(low, "space", down)
        return below, above

    def edges(state, act, grad):
        return pl.pallas_call(
            functools.partial(edges_kernel, plane),
            out_shape=(edge, edge),
            in_specs=whole(3),
            out_specs=tuple(whole(2)),
            compiler_params=VMEM,
            name="edges",
        )(state, act, grad)

    def tick_first(state, act, grad, below, above):
        return pl.pallas_call(
            functools.partial(first_kernel, ydim, zdim),
            out_shape=(tile, tile, wide, wide, wide, wide),
            in_specs=[pl.BlockSpec(memory_space=pltpu.SMEM)] + whole(8),
            out_specs=tuple(whole(6)),
            scratch_shapes=[pltpu.VMEM((cells + 4 * plane, 9 * width), BF16)],
            compiler_params=VMEM,
            name="tick_first",
        )(flags, state, act, grad, below, above, first, second, second_back)

    def tick_second(state, act, grad, made):
        new_one, back_two, mid, back, carry, _ = made
        return pl.pallas_call(
            functools.partial(second_kernel, ydim, zdim),
            out_shape=(state_shape,) * 3,
            in_specs=whole(11),
            out_specs=tuple(whole(3)),
            scratch_shapes=[pltpu.VMEM((cells + 2 * plane, 9 * width), BF16)],
            compiler_params=VMEM,
            name="tick_second",
        )(state, act, grad, new_one, back_two, mid, back, carry, first, second, first_back)

    def weight_grads(grad, made, so_far, factor):
        last = so_far is not None
        extra = (so_far,) if last else ()
        return pl.pallas_call(
            functools.partial(corr_kernel, ydim, zdim, factor, last),
            out_shape=array((2, offsets, width), BF16 if last else F32),
            in_specs=whole(4 + len(extra)),
            out_specs=whole(1)[0],
            scratch_shapes=[pltpu.VMEM((cells, 9 * width), BF16)],
            compiler_params=VMEM,
            name="weight_grads",
        )(grad, made[3], made[4], made[5], *extra)

    state, act, grad = flat(fwd_in), flat(bwd_act), flat(bwd_grad)
    below, above = exchange(*edges(state, act, grad))
    made_one = tick_first(state, act, grad, below, above)
    forward, rebuilt, passed = tick_second(state, act, grad, made_one)
    lifted = lax.ppermute(forward, "section", [(s, s + 1) for s in range(last_section)])
    lowered = lax.ppermute(
        jnp.stack([rebuilt, passed]), "section", [(s + 1, s) for s in range(last_section)]
    )
    own_grad = (forward.astype(F32) - flat(target).astype(F32)).astype(BF16)
    state_two = jnp.where(place == 0, flat(fresh), lifted)
    act_two = jnp.where(place == last_section, forward, lowered[0])
    grad_two = jnp.where(place == last_section, own_grad, lowered[1])
    below, above = exchange(*edges(state_two, act_two, grad_two))
    so_far = weight_grads(grad, made_one, None, None)
    made_two = tick_first(state_two, act_two, grad_two, below, above)
    cell_total = cells * count
    sums = weight_grads(grad_two, made_two, so_far, 1.0 / math.sqrt(cell_total))
    forward, rebuilt, passed = tick_second(state_two, act_two, grad_two, made_two)
    blocks = jnp.concatenate([sums[0].reshape(count, -1, width), sums[1].reshape(count, -1, width)], axis=1)
    total = reduce_blocks(blocks)
    rows = total.shape[0] // 2
    return (
        forward.reshape((1,) + shape),
        rebuilt.reshape((1,) + shape),
        passed.reshape((1,) + shape),
        total[:rows][None],
        total[rows:][None],
    )


def solution(mesh):
    placed = (
        P("section", "space", None, None, None),
        P("section", "space", None, None, None),
        P("section", "space", None, None, None),
        P("space", None, None, None),
        P("space", None, None, None),
        P("section", None, None, None),
        P("section", None, None, None),
    )
    return jax.shard_map(
        shards,
        mesh=mesh,
        in_specs=placed,
        out_specs=(
            P("section", "space", None, None, None),
            P("section", "space", None, None, None),
            P("section", "space", None, None, None),
            P("section", "space", None),
            P("section", "space", None),
        ),
        check_vma=False,
    )
```

```python
import functools
import math

import jax
import jax.numpy as jnp
from jax import lax
from jax.experimental import pallas as pl
from jax.experimental.pallas import tpu as pltpu
from jax.sharding import PartitionSpec as P

VMEM = pltpu.CompilerParams(vmem_limit_bytes=20 * 1024 * 1024)
F32 = jnp.float32
BF16 = jnp.bfloat16


def half_erf(value):
    return 0.5 * (1.0 + lax.erf(value * 0.7071067811865476))


def smooth_gate(value):
    return value * half_erf(value)


def gate_slope(value, half):
    return half + value * jnp.exp(-0.5 * value * value) * 0.3989422804014327


def fill_shifts(stack, field, ydim, zdim):
    rows, width = field.shape
    cells = field.reshape(rows // zdim, zdim, width)
    depth = lax.broadcasted_iota(jnp.int32, cells.shape, 1)
    before = jnp.where(depth == 0, 0.0, pltpu.roll(cells, 1, 1))
    after = jnp.where(depth == zdim - 1, 0.0, pltpu.roll(cells, zdim - 1, 1))
    for across, moved in enumerate((before, cells, after)):
        moved = moved.reshape(rows // (ydim * zdim), ydim, zdim, width)
        blank = jnp.zeros_like(moved[:, :1])
        shifted = (
            jnp.concatenate([blank, moved[:, :-1]], axis=1),
            moved,
            jnp.concatenate([moved[:, 1:], blank], axis=1),
        )
        for down in range(3):
            at = (3 * down + across) * width
            stack[0:rows, at : at + width] = shifted[down].reshape(rows, width).astype(BF16)


def convolve(stack, weights, rows, plane):
    total = None
    for step in range(3):
        part = jnp.dot(
            stack[step * plane : step * plane + rows, :],
            weights[step],
            preferred_element_type=F32,
        )
        total = part if total is None else total + part
    return total


def pack_edges(state, act, grad, low, high, plane):
    width = state.shape[1] // 2
    cells = state.shape[0]
    left, right = slice(0, width), slice(width, 2 * width)
    for index, (source, half) in enumerate(((state, right), (act, left), (grad, right))):
        at = index * 2 * plane
        low[at : at + 2 * plane, :] = source[0 : 2 * plane, half]
        high[at : at + 2 * plane, :] = source[cells - 2 * plane : cells, half]
    for index, (source, half) in enumerate(((state, left), (act, right), (grad, left))):
        at = (6 + index) * plane
        low[at : at + plane, :] = source[0:plane, half]
        high[at : at + plane, :] = source[cells - plane : cells, half]


def edges_kernel(plane, state, act, grad, low, high, sems):
    width = state.shape[1] // 2
    cells = state.shape[0]
    left, right = pl.ds(0, width), pl.ds(width, width)
    moves = []
    for index, (source, half) in enumerate(((state, right), (act, left), (grad, right))):
        moves.append((source, half, 2 * plane, index * 2 * plane))
    for index, (source, half) in enumerate(((state, left), (act, right), (grad, left))):
        moves.append((source, half, plane, (6 + index) * plane))
    copies = []
    for source, half, size, at in moves:
        for start, out in ((0, low), (cells - size, high)):
            copies.append(
                pltpu.make_async_copy(
                    source.at[pl.ds(start, size), half],
                    out.at[pl.ds(at, size), :],
                    sems.at[len(copies)],
                )
            )
    for copy in copies:
        copy.start()
    for copy in copies:
        copy.wait()


def join_kernel(plane, places, forward, lifted, lowered, fresh, target, state, act, grad, low, high):
    first_place, last_place = places[0] == 0, places[0] == places[1]
    state[...] = jnp.where(first_place, fresh[...], lifted[0])
    own = forward[...]
    act[...] = jnp.where(last_place, own, lowered[0])
    error = (own.astype(F32) - target[...].astype(F32)).astype(BF16)
    grad[...] = jnp.where(last_place, error, lowered[1])
    pack_edges(state, act, grad, low, high, plane)


def first_kernel(ydim, zdim, flags, state, act, grad, below, above, first, second, second_back,
                 new_one, back_two, mid, back, carry, gate, stack):
    plane = ydim * zdim
    cells, double = state.shape
    width = double // 2
    inner = cells + 2 * plane
    outer = cells + 4 * plane
    left, right = slice(0, width), slice(width, double)

    def two(source, half, index):
        at = index * 2 * plane
        return jnp.concatenate(
            [below[at : at + 2 * plane, :], source[:, half], above[at : at + 2 * plane, :]], axis=0
        ).astype(F32)

    def one(source, half, index):
        at = (6 + index) * plane
        return jnp.concatenate(
            [below[at : at + plane, :], source[:, half], above[at : at + plane, :]], axis=0
        ).astype(F32)

    low_flag, high_flag = flags[0], flags[1]

    def store_masked(ref, value):
        ref[0:plane, :] = (value[0:plane].astype(F32) * low_flag).astype(BF16)
        ref[plane : plane + cells, :] = value[plane : plane + cells]
        ref[plane + cells : inner, :] = (value[plane + cells :].astype(F32) * high_flag).astype(BF16)

    core = slice(plane, plane + cells)
    fill_shifts(stack, smooth_gate(two(state, right, 0)), ydim, zdim)
    f_one = (one(state, left, 0) + convolve(stack, first, inner, plane)).astype(BF16)
    new_one[...] = f_one[core]
    store_masked(mid, smooth_gate(f_one.astype(F32)).astype(BF16))

    y_one = two(act, left, 1)
    half = half_erf(y_one)
    gated = y_one * half
    gate[...] = gated[plane : plane + inner].astype(BF16)
    fill_shifts(stack, gated, ydim, zdim)
    r_two = (one(act, right, 1) - convolve(stack, second, inner, plane)).astype(BF16)
    back_two[...] = r_two[core]
    store_masked(back, smooth_gate(r_two.astype(F32)).astype(BF16))

    fill_shifts(stack, two(grad, right, 2), ydim, zdim)
    slope = gate_slope(y_one[plane : plane + inner], half[plane : plane + inner])
    e_one = (one(grad, left, 2) + slope * convolve(stack, second_back, inner, plane)).astype(BF16)
    store_masked(carry, e_one)


def second_kernel(ydim, zdim, state, act, grad, new_one, back_two, mid, back, carry, first, second,
                  first_back, forward, rebuilt, passed, stack):
    plane = ydim * zdim
    cells, double = state.shape
    width = double // 2
    left, right = slice(0, width), slice(width, double)
    forward[:, left] = new_one[...]
    rebuilt[:, right] = back_two[...]
    passed[:, left] = carry[plane : plane + cells, :]

    fill_shifts(stack, back[...].astype(F32), ydim, zdim)
    rebuilt[:, left] = (
        act[:, left].astype(F32) - convolve(stack, first, cells, plane)
    ).astype(BF16)
    fill_shifts(stack, carry[...].astype(F32), ydim, zdim)
    r_two = back_two[...].astype(F32)
    passed[:, right] = (
        grad[:, right].astype(F32)
        + gate_slope(r_two, half_erf(r_two)) * convolve(stack, first_back, cells, plane)
    ).astype(BF16)
    fill_shifts(stack, mid[...].astype(F32), ydim, zdim)
    forward[:, right] = (
        state[:, right].astype(F32) + convolve(stack, second, cells, plane)
    ).astype(BF16)


def tick_kernel(ydim, zdim, paired, places, flags, state_in, act_in, grad_in, below, above, first,
                second, first_back, second_back, forward, sent, back, carry, gate, state, act, grad,
                new_one, back_two, mid, rebuilt, stack, sems):
    copies = [
        pltpu.make_async_copy(source, target, sems.at[index])
        for index, (source, target) in enumerate(
            ((state_in, state), (act_in, act), (grad_in, grad))
        )
    ]
    for copy in copies:
        copy.start()
    for copy in copies:
        copy.wait()
    first_kernel(ydim, zdim, flags, state, act, grad, below, above, first, second, second_back,
                 new_one, back_two, mid, back, carry, gate, stack)
    second_kernel(ydim, zdim, state, act, grad, new_one, back_two, mid, back, carry, first, second,
                  first_back, forward, rebuilt, sent.at[1], stack)
    if paired:
        sent[0] = jnp.where(places[0] == 0, forward[...], rebuilt[...])
    else:
        sent[0] = rebuilt[...]


def correlate(stack, field, cotangent, ydim, zdim, emit):
    plane = ydim * zdim
    cells, width = cotangent.shape
    fill_shifts(stack, cotangent, ydim, zdim)
    for step in range(3):
        product = lax.dot_general(
            field[step * plane : step * plane + cells, :],
            stack[0:cells, :],
            (((0,), (0,)), ((), ())),
            preferred_element_type=F32,
        )
        for place in range(9):
            emit(9 * step + 8 - place, product[:, place * width : (place + 1) * width])


def both_grads(ydim, zdim, grad, back, carry, gate, stack, put):
    plane = ydim * zdim
    cells, double = grad.shape
    width = double // 2

    def store(which):
        return lambda k, block: put(which, slice(k * width, (k + 1) * width), block)

    own = carry[plane : plane + cells, :].astype(F32)
    correlate(stack, back, own, ydim, zdim, store(0))
    correlate(stack, gate, grad[:, width:].astype(F32), ydim, zdim, store(1))


def corr_kernel(ydim, zdim, grad, back, carry, gate, out, stack):
    def put(which, at, block):
        out[which, at, :] = block

    both_grads(ydim, zdim, grad, back, carry, gate, stack, put)


def ways_of(count, rows):
    bits = [1 << level for level in range(count.bit_length() - 1)]
    ways = 3
    span = 2 * rows // ways
    return [(way * span, span, bits[way % len(bits) :] + bits[: way % len(bits)]) for way in range(ways)]


def last_kernel(ydim, zdim, factor, count, direct, spot, flags, state, act, grad, below, above, first,
                second, second_back, so_far, new_one, back_two, mid, back, carry, *refs):
    refs, (gate, stack, sums) = refs[:-3], refs[-3:]
    first_kernel(ydim, zdim, flags, state, act, grad, below, above, first, second, second_back,
                 new_one, back_two, mid, back, carry, gate, stack)

    def put(which, at, block):
        sums[which, at, :] = (block + so_far[which, at, :]) * factor

    both_grads(ydim, zdim, grad, back, carry, gate, stack, put)
    if not direct:
        refs[0][...] = sums[...].astype(BF16)
        return
    rows = sums.shape[1] // count
    for index, (start, span, order) in enumerate(ways_of(count, rows)):
        mine = (spot[0] // order[0]) % 2
        for kept in range(2):
            side = mine if kept else 1 - mine
            out = refs[2 * index + (0 if kept else 1)]
            for j in range(count // 2):
                fixed = sum(
                    bit for level, bit in enumerate(order[1:]) if (j >> (len(order) - 2 - level)) & 1
                )
                block = fixed + side * order[0]
                pieces = []
                for which in range(2):
                    lower = max(start, which * rows)
                    upper = min(start + span, (which + 1) * rows)
                    if lower < upper:
                        at = pl.multiple_of(block * rows + (lower - which * rows), 8)
                        pieces.append(sums[which, pl.ds(at, upper - lower), :])
                value = pieces[0] if len(pieces) == 1 else jnp.concatenate(pieces, axis=0)
                out[j] = value.astype(BF16)


def whole(count):
    return [pl.BlockSpec(memory_space=pltpu.VMEM)] * count


def split_blocks(sums, count):
    blocks = jnp.concatenate([part.reshape(count, -1, part.shape[-1]) for part in sums], axis=1)
    spot = lax.axis_index("space")
    halves = []
    for start, span, order in ways_of(count, blocks.shape[1] // 2):
        part = blocks[:, start : start + span]
        part = part.reshape([2] * len(order) + list(part.shape[1:]))
        levels = [len(order) - bit.bit_length() for bit in order]
        part = jnp.transpose(part, levels + [len(order), len(order) + 1])
        part = part.reshape((2, count // 2) + part.shape[-2:])
        mine = (spot // order[0]) % 2
        for side in (mine, 1 - mine):
            halves.append(lax.dynamic_index_in_dim(part, side, 0, keepdims=False))
    return halves


def reduce_blocks(halves, count, rows):
    spot = lax.axis_index("space")
    ways = [
        (halves[2 * way], halves[2 * way + 1], order)
        for way, (_, _, order) in enumerate(ways_of(count, rows))
    ]
    for step in range(count.bit_length() - 1):
        later = []
        for keep, send, order in ways:
            bit = order[step]
            got = lax.ppermute(send, "space", [(i, i ^ bit) for i in range(count)])
            total = keep.astype(F32) + got.astype(F32)
            if step + 1 < len(order):
                total = total.astype(BF16)
                total = total.reshape((2, total.shape[0] // 2) + total.shape[1:])
                mine = (spot // order[step + 1]) % 2
                keep = lax.dynamic_index_in_dim(total, mine, 0, keepdims=False)
                send = lax.dynamic_index_in_dim(total, 1 - mine, 0, keepdims=False)
            else:
                keep, send = total[0], None
            later.append((keep, send, order))
        ways = later
    return jnp.concatenate([keep for keep, _, _ in ways], axis=0)


def shards(fwd_in, bwd_act, bwd_grad, fresh, target, w_first, w_second):
    width = w_first.shape[2]
    layers, ydim, zdim = fwd_in.shape[1:4]
    plane = ydim * zdim
    cells = layers * plane
    shape = fwd_in.shape[1:]
    flat = lambda block: block.reshape(cells, 2 * width)
    first = w_first[0].reshape(3, 9 * width, width)
    second = w_second[0].reshape(3, 9 * width, width)
    first_back = jnp.transpose(w_first[0][::-1], (0, 2, 1)).reshape(3, 9 * width, width)
    second_back = jnp.transpose(w_second[0][::-1], (0, 2, 1)).reshape(3, 9 * width, width)
    last_section = lax.axis_size("section") - 1
    place = lax.axis_index("section")
    count = lax.axis_size("space")
    spot = lax.axis_index("space")
    flags = jnp.stack([spot > 0, spot < count - 1]).astype(F32)
    up = [(i, i + 1) for i in range(count - 1)]
    down = [(i + 1, i) for i in range(count - 1)]
    array = jax.ShapeDtypeStruct
    edge = array((9 * plane, width), BF16)
    tile = array((cells, width), BF16)
    wide = array((cells + 2 * plane, width), BF16)
    state_shape = array((cells, 2 * width), BF16)
    offsets = 27 * width

    def exchange(low, high):
        below = lax.ppermute(high, "space", up)
        above = lax.ppermute(low, "space", down)
        return below, above

    state, act, grad = flat(fwd_in), flat(bwd_act), flat(bwd_grad)
    smem = pl.BlockSpec(memory_space=pltpu.SMEM)
    hbm = pl.BlockSpec(memory_space=pltpu.HBM)
    scratch = lambda like: pltpu.VMEM(like.shape, like.dtype)
    inner_stack = pltpu.VMEM((cells + 2 * plane, 9 * width), BF16)
    outer_stack = pltpu.VMEM((cells + 4 * plane, 9 * width), BF16)
    places = jnp.stack([place, jnp.full_like(place, last_section)]).astype(jnp.int32)

    low, high = pl.pallas_call(
        functools.partial(edges_kernel, plane),
        out_shape=(edge, edge),
        in_specs=[hbm] * 3,
        out_specs=(hbm, hbm),
        scratch_shapes=[pltpu.SemaphoreType.DMA((12,))],
        compiler_params=VMEM,
        name="edges",
    )(state, act, grad)
    below, above = exchange(low, high)

    paired = last_section == 1
    forward, sent, back, carry, gate = pl.pallas_call(
        functools.partial(tick_kernel, ydim, zdim, paired),
        out_shape=(state_shape, array((2, cells, 2 * width), BF16), wide, wide, wide),
        in_specs=[smem] * 2 + [hbm] * 3 + whole(6),
        out_specs=tuple(whole(5)),
        scratch_shapes=[scratch(state_shape)] * 3
        + [scratch(tile), scratch(tile), scratch(wide), scratch(state_shape), outer_stack]
        + [pltpu.SemaphoreType.DMA((3,))],
        compiler_params=VMEM,
        name="tick_one",
    )(places, flags, state, act, grad, below, above, first, second, first_back, second_back)
    if paired:
        lifted = lowered = lax.ppermute(sent, "section", [(0, 1), (1, 0)])
    else:
        lifted = lax.ppermute(forward[None], "section", [(s, s + 1) for s in range(last_section)])
        lowered = lax.ppermute(sent, "section", [(s + 1, s) for s in range(last_section)])

    state_two, act_two, grad_two, low, high = pl.pallas_call(
        functools.partial(join_kernel, plane),
        out_shape=(state_shape,) * 3 + (edge, edge),
        in_specs=[smem] + whole(5),
        out_specs=tuple(whole(5)),
        compiler_params=VMEM,
        name="join",
    )(places, forward, lifted, lowered, flat(fresh), flat(target))
    below, above = exchange(low, high)

    so_far = pl.pallas_call(
        functools.partial(corr_kernel, ydim, zdim),
        out_shape=array((2, offsets, width), F32),
        in_specs=whole(4),
        out_specs=whole(1)[0],
        scratch_shapes=[pltpu.VMEM((cells, 9 * width), BF16)],
        compiler_params=VMEM,
        name="weight_grads",
    )(grad, back, carry, gate)

    rows = offsets // count
    direct = rows % 24 == 0
    if direct:
        span = 2 * rows // 3
        outs = (array((count // 2, span, width), BF16),) * 6
    else:
        outs = (array((2, offsets, width), BF16),)
    factor = 1.0 / math.sqrt(cells * count)
    made = pl.pallas_call(
        functools.partial(last_kernel, ydim, zdim, factor, count, direct),
        out_shape=(tile, tile, wide, wide, wide) + outs,
        in_specs=[smem] * 2 + whole(9),
        out_specs=tuple(whole(5 + len(outs))),
        scratch_shapes=[scratch(wide), outer_stack, pltpu.VMEM((2, offsets, width), F32)],
        compiler_params=VMEM,
        name="tick_two_first",
    )(spot.astype(jnp.int32).reshape(1), flags, state_two, act_two, grad_two, below, above, first,
      second, second_back, so_far)
    forward, rebuilt, passed = pl.pallas_call(
        functools.partial(second_kernel, ydim, zdim),
        out_shape=(state_shape,) * 3,
        in_specs=whole(11),
        out_specs=tuple(whole(3)),
        scratch_shapes=[inner_stack],
        compiler_params=VMEM,
        cost_estimate=pl.CostEstimate(flops=2 * 81 * cells * width * width, bytes_accessed=4000000, transcendentals=0),
        name="tick_two_second",
    )(state_two, act_two, grad_two, *made[:5], first, second, first_back)
    halves = made[5:] if direct else split_blocks(made[5], count)
    total = reduce_blocks(halves, count, rows)
    return (
        forward.reshape((1,) + shape),
        rebuilt.reshape((1,) + shape),
        passed.reshape((1,) + shape),
        total[:rows][None],
        total[rows:][None],
    )


def solution(mesh):
    placed = (
        P("section", "space", None, None, None),
        P("section", "space", None, None, None),
        P("section", "space", None, None, None),
        P("space", None, None, None),
        P("space", None, None, None),
        P("section", None, None, None),
        P("section", None, None, None),
    )
    return jax.shard_map(
        shards,
        mesh=mesh,
        in_specs=placed,
        out_specs=(
            P("section", "space", None, None, None),
            P("section", "space", None, None, None),
            P("section", "space", None, None, None),
            P("section", "space", None),
            P("section", "space", None),
        ),
        check_vma=False,
    )
```

```python
import functools
import math

import jax
import jax.numpy as jnp
from jax import lax
from jax.experimental import pallas as pl
from jax.experimental.pallas import tpu as pltpu
from jax.sharding import PartitionSpec as P

VMEM = pltpu.CompilerParams(vmem_limit_bytes=65408 * 1024)
F32 = jnp.float32
BF16 = jnp.bfloat16


class Copies:
    def __init__(self, sems):
        self.sems, self.used, self.open = sems, 0, {}

    def start(self, name, source, target):
        copy = pltpu.make_async_copy(source, target, self.sems.at[self.used])
        self.used += 1
        copy.start()
        self.open[name] = copy

    def need(self, *names):
        for name in names:
            if name in self.open:
                self.open.pop(name).wait()

    def finish(self):
        self.need(*list(self.open))


def half_erf(value):
    return 0.5 * (1.0 + lax.erf(value * 0.7071067811865476))


def smooth_gate(value):
    return value * half_erf(value)


def gate_slope(value, half):
    return half + value * jnp.exp(-0.5 * value * value) * 0.3989422804014327


def fill_shifts(stack, field, ydim, zdim):
    rows, width = field.shape
    cells = field.reshape(rows // zdim, zdim, width)
    depth = lax.broadcasted_iota(jnp.int32, cells.shape, 1)
    before = jnp.where(depth == 0, 0.0, pltpu.roll(cells, 1, 1))
    after = jnp.where(depth == zdim - 1, 0.0, pltpu.roll(cells, zdim - 1, 1))
    for across, moved in enumerate((before, cells, after)):
        moved = moved.reshape(rows // (ydim * zdim), ydim, zdim, width)
        blank = jnp.zeros_like(moved[:, :1])
        shifted = (
            jnp.concatenate([blank, moved[:, :-1]], axis=1),
            moved,
            jnp.concatenate([moved[:, 1:], blank], axis=1),
        )
        for down in range(3):
            at = (3 * down + across) * width
            stack[0:rows, at : at + width] = shifted[down].reshape(rows, width).astype(BF16)


def convolve(stack, weights, rows, plane):
    total = None
    for step in range(3):
        part = jnp.dot(
            stack[step * plane : step * plane + rows, :],
            weights[step],
            preferred_element_type=F32,
        )
        total = part if total is None else total + part
    return total


def pack_edges(state, act, grad, low, high, plane):
    width = state.shape[1] // 2
    cells = state.shape[0]
    left, right = slice(0, width), slice(width, 2 * width)
    for index, (source, half) in enumerate(((state, right), (act, left), (grad, right))):
        at = index * 2 * plane
        low[at : at + 2 * plane, :] = source[0 : 2 * plane, half]
        high[at : at + 2 * plane, :] = source[cells - 2 * plane : cells, half]
    for index, (source, half) in enumerate(((state, left), (act, right), (grad, left))):
        at = (6 + index) * plane
        low[at : at + plane, :] = source[0:plane, half]
        high[at : at + plane, :] = source[cells - plane : cells, half]


def edges_kernel(plane, state, act, grad, low, high, sems):
    width = state.shape[1] // 2
    cells = state.shape[0]
    left, right = pl.ds(0, width), pl.ds(width, width)
    moves = []
    for index, (source, half) in enumerate(((state, right), (act, left), (grad, right))):
        moves.append((source, half, 2 * plane, index * 2 * plane))
    for index, (source, half) in enumerate(((state, left), (act, right), (grad, left))):
        moves.append((source, half, plane, (6 + index) * plane))
    copies = []
    for source, half, size, at in moves:
        for start, out in ((0, low), (cells - size, high)):
            copies.append(
                pltpu.make_async_copy(
                    source.at[pl.ds(start, size), half],
                    out.at[pl.ds(at, size), :],
                    sems.at[len(copies)],
                )
            )
    for copy in copies:
        copy.start()
    for copy in copies:
        copy.wait()


def join_kernel(plane, places, forward_in, lifted_in, lowered_in, fresh_in, target_in, state_out,
                act_out, grad_out, low_out, high_out, forward, lifted, lowered, fresh, target, state,
                act, grad, low, high, sems):
    copies = Copies(sems)
    copies.start("lifted", lifted_in.at[0], lifted)
    copies.start("lowered", lowered_in, lowered)
    copies.start("fresh", fresh_in, fresh)
    copies.start("forward", forward_in, forward)
    copies.start("target", target_in, target)
    copies.finish()
    first_place, last_place = places[0] == 0, places[0] == places[1]
    state[...] = jnp.where(first_place, fresh[...], lifted[...])
    own = forward[...]
    act[...] = jnp.where(last_place, own, lowered[0])
    error = (own.astype(F32) - target[...].astype(F32)).astype(BF16)
    grad[...] = jnp.where(last_place, error, lowered[1])
    pack_edges(state, act, grad, low, high, plane)
    for index, (source, out) in enumerate(
        ((low, low_out), (high, high_out), (state, state_out), (act, act_out), (grad, grad_out))
    ):
        copies.start(index, source, out)
    copies.finish()


def flip_kernel(first_in, second_in, first_out, second_out, source, flipped, sems):
    copies = Copies(sems)
    copies.start(0, first_in, source.at[0])
    copies.start(1, second_in, source.at[1])
    offsets = source.shape[1]
    for which, out in enumerate((first_out, second_out)):
        copies.need(which)
        for k in range(offsets):
            flipped[which, offsets - 1 - k] = jnp.transpose(source[which, k])
        copies.start(2 + which, flipped.at[which], out)
    copies.finish()


def first_kernel(ydim, zdim, copies, made, flags, state, act, grad, below, above, first, second, second_back,
                 new_one, back_two, mid, back, carry, gate, stack):
    plane = ydim * zdim
    cells, double = state.shape
    width = double // 2
    inner = cells + 2 * plane
    outer = cells + 4 * plane
    left, right = slice(0, width), slice(width, double)

    def two(source, half, index):
        at = index * 2 * plane
        return jnp.concatenate(
            [below[at : at + 2 * plane, :], source[:, half], above[at : at + 2 * plane, :]], axis=0
        ).astype(F32)

    def one(source, half, index):
        at = (6 + index) * plane
        return jnp.concatenate(
            [below[at : at + plane, :], source[:, half], above[at : at + plane, :]], axis=0
        ).astype(F32)

    low_flag, high_flag = flags[0], flags[1]

    def store_masked(ref, value):
        ref[0:plane, :] = (value[0:plane].astype(F32) * low_flag).astype(BF16)
        ref[plane : plane + cells, :] = value[plane : plane + cells]
        ref[plane + cells : inner, :] = (value[plane + cells :].astype(F32) * high_flag).astype(BF16)

    core = slice(plane, plane + cells)
    copies.need("below", "above", "state")
    fill_shifts(stack, smooth_gate(two(state, right, 0)), ydim, zdim)
    copies.need("first")
    f_one = (one(state, left, 0) + convolve(stack, first, inner, plane)).astype(BF16)
    new_one[...] = f_one[core]
    store_masked(mid, smooth_gate(f_one.astype(F32)).astype(BF16))

    made("new_one", "mid")

    copies.need("act")
    y_one = two(act, left, 1)
    half = half_erf(y_one)
    gated = y_one * half
    gate[...] = gated[plane : plane + inner].astype(BF16)
    fill_shifts(stack, gated, ydim, zdim)
    copies.need("second")
    r_two = (one(act, right, 1) - convolve(stack, second, inner, plane)).astype(BF16)
    back_two[...] = r_two[core]
    store_masked(back, smooth_gate(r_two.astype(F32)).astype(BF16))

    made("gate", "back_two", "back")

    copies.need("grad")
    fill_shifts(stack, two(grad, right, 2), ydim, zdim)
    slope = gate_slope(y_one[plane : plane + inner], half[plane : plane + inner])
    copies.need("second_back")
    e_one = (one(grad, left, 2) + slope * convolve(stack, second_back, inner, plane)).astype(BF16)
    store_masked(carry, e_one)
    made("carry")


def second_kernel(ydim, zdim, copies, made, state, act, grad, new_one, back_two, mid, back, carry,
                  first, second, first_back, forward, rebuilt, passed, stack):
    plane = ydim * zdim
    cells, double = state.shape
    width = double // 2
    left, right = slice(0, width), slice(width, double)

    copies.need("back", "act", "back_two")
    fill_shifts(stack, back[...].astype(F32), ydim, zdim)
    rebuilt[:, right] = back_two[...]
    copies.need("first")
    rebuilt[:, left] = (
        act[:, left].astype(F32) - convolve(stack, first, cells, plane)
    ).astype(BF16)
    made("rebuilt")
    copies.need("carry", "grad")
    fill_shifts(stack, carry[...].astype(F32), ydim, zdim)
    passed[:, left] = carry[plane : plane + cells, :]
    r_two = back_two[...].astype(F32)
    copies.need("first_back")
    passed[:, right] = (
        grad[:, right].astype(F32)
        + gate_slope(r_two, half_erf(r_two)) * convolve(stack, first_back, cells, plane)
    ).astype(BF16)
    made("passed")
    copies.need("mid", "state", "new_one")
    fill_shifts(stack, mid[...].astype(F32), ydim, zdim)
    forward[:, left] = new_one[...]
    copies.need("second")
    forward[:, right] = (
        state[:, right].astype(F32) + convolve(stack, second, cells, plane)
    ).astype(BF16)
    made("forward")


def second_alone(ydim, zdim, *refs):
    names = ("state", "act", "grad", "new_one", "back_two", "mid", "back", "carry", "first", "second",
             "first_back")
    sources, outs, local, results = refs[:11], refs[11:14], refs[14:25], refs[25:28]
    stack, sems = refs[28:]
    copies = Copies(sems)
    order = ("back", "act", "back_two", "first", "carry", "grad", "first_back", "mid", "state", "new_one",
             "second")
    for name in order:
        copies.start(name, sources[names.index(name)], local[names.index(name)])
    where = {"forward": 0, "rebuilt": 1, "passed": 2}

    def made(name):
        copies.start("out_" + name, results[where[name]], outs[where[name]])

    second_kernel(ydim, zdim, copies, made, *local, *results, stack)
    copies.finish()


def tick_kernel(ydim, zdim, paired, places, flags, state_in, act_in, grad_in, below_in, above_in,
                first_in, second_in, first_back_in, second_back_in, forward_out, sent_out, back_out,
                carry_out, gate_out, forward, sent, back, carry, gate, state, act, grad, below, above,
                first, second, first_back, second_back, new_one, back_two, mid, rebuilt, stack, sems):
    copies = Copies(sems)
    for name, source, target in (
        ("below", below_in, below),
        ("above", above_in, above),
        ("state", state_in, state),
        ("first", first_in, first),
        ("act", act_in, act),
        ("second", second_in, second),
        ("grad", grad_in, grad),
        ("second_back", second_back_in, second_back),
        ("first_back", first_back_in, first_back),
    ):
        copies.start(name, source, target)
    stores = {
        "back": (back, back_out),
        "carry": (carry, carry_out),
        "gate": (gate, gate_out),
        "forward": (forward, forward_out),
        "passed": (sent.at[1], sent_out.at[1]),
    }

    def made(*names):
        for name in names:
            if name in stores:
                copies.start("out_" + name, *stores[name])

    first_kernel(ydim, zdim, copies, made, flags, state, act, grad, below, above, first, second,
                 second_back, new_one, back_two, mid, back, carry, gate, stack)
    second_kernel(ydim, zdim, copies, made, state, act, grad, new_one, back_two, mid, back, carry, first,
                  second, first_back, forward, rebuilt, sent.at[1], stack)
    if paired:
        sent[0] = jnp.where(places[0] == 0, forward[...], rebuilt[...])
    else:
        sent[0] = rebuilt[...]
    copies.start("out_sent", sent.at[0], sent_out.at[0])
    copies.finish()


def correlate(stack, field, cotangent, ydim, zdim, emit):
    plane = ydim * zdim
    cells, width = cotangent.shape
    fill_shifts(stack, cotangent, ydim, zdim)
    for step in range(3):
        product = lax.dot_general(
            field[step * plane : step * plane + cells, :],
            stack[0:cells, :],
            (((0,), (0,)), ((), ())),
            preferred_element_type=F32,
        )
        for place in range(9):
            emit(9 * step + 8 - place, product[:, place * width : (place + 1) * width])


def both_grads(ydim, zdim, grad, back, carry, gate, stack, put):
    plane = ydim * zdim
    cells, double = grad.shape
    width = double // 2

    def store(which):
        return lambda k, block: put(which, slice(k * width, (k + 1) * width), block)

    own = carry[plane : plane + cells, :].astype(F32)
    correlate(stack, back, own, ydim, zdim, store(0))
    correlate(stack, gate, grad[:, width:].astype(F32), ydim, zdim, store(1))


def corr_kernel(ydim, zdim, grad_in, back_in, carry_in, gate_in, out_ref, grad, back, carry, gate, out,
                stack, sems):
    copies = Copies(sems)
    for name, source, target in (
        ("carry", carry_in, carry), ("back", back_in, back), ("grad", grad_in, grad), ("gate", gate_in, gate)
    ):
        copies.start(name, source, target)
    copies.finish()

    def put(which, at, block):
        out[which, at, :] = block

    both_grads(ydim, zdim, grad, back, carry, gate, stack, put)
    copies.start("out", out, out_ref)
    copies.finish()


def ways_of(count, rows):
    bits = [1 << level for level in range(count.bit_length() - 1)]
    ways = 3
    span = 2 * rows // ways
    return [(way * span, span, bits[way % len(bits) :] + bits[: way % len(bits)]) for way in range(ways)]


def last_kernel(ydim, zdim, factor, count, direct, spot, flags, *args):
    names = ("state", "act", "grad", "below", "above", "first", "second", "second_back", "so_far")
    made_names = ("new_one", "back_two", "mid", "back", "carry")
    n_outs = 6 if direct else 1
    sources, args = args[:9], args[9:]
    outs, args = args[:5], args[5:]
    final_outs, args = args[:n_outs], args[n_outs:]
    local, args = args[:9], args[9:]
    results, args = args[:5], args[5:]
    refs, args = args[:n_outs], args[n_outs:]
    gate, stack, sums, sems = args
    copies = Copies(sems)
    for name in ("below", "above", "state", "first", "act", "second", "grad", "second_back", "so_far"):
        copies.start(name, sources[names.index(name)], local[names.index(name)])

    def made(*done):
        for name in done:
            if name in made_names:
                index = made_names.index(name)
                copies.start("out_" + name, results[index], outs[index])

    first_kernel(ydim, zdim, copies, made, flags, *local[:8], *results, gate, stack)
    back, carry = results[3], results[4]
    grad, so_far = local[2], local[8]
    copies.need("so_far")

    def put(which, at, block):
        sums[which, at, :] = (block + so_far[which, at, :]) * factor

    both_grads(ydim, zdim, grad, back, carry, gate, stack, put)
    if not direct:
        refs[0][...] = sums[...].astype(BF16)
        copies.start("out", refs[0], final_outs[0])
        copies.finish()
        return
    rows = sums.shape[1] // count
    for index, (start, span, order) in enumerate(ways_of(count, rows)):
        mine = (spot[0] // order[0]) % 2
        for kept in (0, 1):
            side = mine if kept else 1 - mine
            out = refs[2 * index + (0 if kept else 1)]
            for j in range(count // 2):
                fixed = sum(
                    bit for level, bit in enumerate(order[1:]) if (j >> (len(order) - 2 - level)) & 1
                )
                block = fixed + side * order[0]
                pieces = []
                for which in range(2):
                    lower = max(start, which * rows)
                    upper = min(start + span, (which + 1) * rows)
                    if lower < upper:
                        at = pl.multiple_of(block * rows + (lower - which * rows), 8)
                        pieces.append(sums[which, pl.ds(at, upper - lower), :])
                value = pieces[0] if len(pieces) == 1 else jnp.concatenate(pieces, axis=0)
                out[j] = value.astype(BF16)
            at = 2 * index + (0 if kept else 1)
            copies.start(("half", at), out, final_outs[at])
    copies.finish()


def split_blocks(sums, count):
    blocks = jnp.concatenate([part.reshape(count, -1, part.shape[-1]) for part in sums], axis=1)
    spot = lax.axis_index("space")
    halves = []
    for start, span, order in ways_of(count, blocks.shape[1] // 2):
        part = blocks[:, start : start + span]
        part = part.reshape([2] * len(order) + list(part.shape[1:]))
        levels = [len(order) - bit.bit_length() for bit in order]
        part = jnp.transpose(part, levels + [len(order), len(order) + 1])
        part = part.reshape((2, count // 2) + part.shape[-2:])
        mine = (spot // order[0]) % 2
        for side in (mine, 1 - mine):
            halves.append(lax.dynamic_index_in_dim(part, side, 0, keepdims=False))
    return halves


def reduce_blocks(halves, count, rows):
    spot = lax.axis_index("space")
    ways = [
        (halves[2 * way], halves[2 * way + 1], order)
        for way, (_, _, order) in enumerate(ways_of(count, rows))
    ]
    for step in range(count.bit_length() - 1):
        later = []
        for keep, send, order in ways:
            bit = order[step]
            got = lax.ppermute(send, "space", [(i, i ^ bit) for i in range(count)])
            total = keep.astype(F32) + got.astype(F32)
            if step + 1 < len(order):
                total = total.astype(BF16)
                total = total.reshape((2, total.shape[0] // 2) + total.shape[1:])
                mine = (spot // order[step + 1]) % 2
                keep = lax.dynamic_index_in_dim(total, mine, 0, keepdims=False)
                send = lax.dynamic_index_in_dim(total, 1 - mine, 0, keepdims=False)
            else:
                keep, send = total[0], None
            later.append((keep, send, order))
        ways = later
    return jnp.concatenate([keep for keep, _, _ in ways], axis=0)


def shards(fwd_in, bwd_act, bwd_grad, fresh, target, w_first, w_second):
    width = w_first.shape[2]
    layers, ydim, zdim = fwd_in.shape[1:4]
    plane = ydim * zdim
    cells = layers * plane
    shape = fwd_in.shape[1:]
    flat = lambda block: block.reshape(cells, 2 * width)
    first = w_first[0].reshape(3, 9 * width, width)
    second = w_second[0].reshape(3, 9 * width, width)
    last_section = lax.axis_size("section") - 1
    place = lax.axis_index("section")
    count = lax.axis_size("space")
    spot = lax.axis_index("space")
    flags = jnp.stack([spot > 0, spot < count - 1]).astype(F32)
    up = [(i, i + 1) for i in range(count - 1)]
    down = [(i + 1, i) for i in range(count - 1)]
    array = jax.ShapeDtypeStruct
    edge = array((9 * plane, width), BF16)
    tile = array((cells, width), BF16)
    wide = array((cells + 2 * plane, width), BF16)
    state_shape = array((cells, 2 * width), BF16)
    offsets = 27 * width

    def exchange(low, high):
        below = lax.ppermute(high, "space", up)
        above = lax.ppermute(low, "space", down)
        return below, above

    state, act, grad = flat(fwd_in), flat(bwd_act), flat(bwd_grad)
    smem = pl.BlockSpec(memory_space=pltpu.SMEM)
    hbm = pl.BlockSpec(memory_space=pltpu.HBM)
    inner_stack = array((cells + 2 * plane, 9 * width), BF16)
    outer_stack = array((cells + 4 * plane, 9 * width), BF16)
    small_stack = array((cells, 9 * width), BF16)
    weight = array((3, 9 * width, width), BF16)
    raw_weight = array((27, width, width), BF16)
    sums_shape = array((2, offsets, width), F32)
    places = jnp.stack([place, jnp.full_like(place, last_section)]).astype(jnp.int32)

    def call(kernel, name, scalars, inputs, outs, scratch, copies, flops=0):
        return pl.pallas_call(
            kernel,
            out_shape=tuple(outs),
            in_specs=[smem] * len(scalars) + [hbm] * len(inputs),
            out_specs=(hbm,) * len(outs),
            scratch_shapes=[pltpu.VMEM(like.shape, like.dtype) for like in scratch]
            + [pltpu.SemaphoreType.DMA((copies,))],
            compiler_params=VMEM,
            cost_estimate=pl.CostEstimate(
                flops=flops, bytes_accessed=sum(x.size * 2 for x in inputs), transcendentals=0
            ),
            name=name,
        )(*scalars, *inputs)

    work = 2 * 27 * cells * width * width
    low, high = call(functools.partial(edges_kernel, plane), "edges", (), (state, act, grad), (edge,) * 2, (), 12)
    below, above = exchange(low, high)
    first_back, second_back = call(
        flip_kernel, "flip", (), (w_first[0], w_second[0]), (raw_weight,) * 2,
        (array((2,) + raw_weight.shape, BF16),) * 2, 4,
    )
    first_back, second_back = first_back.reshape(weight.shape), second_back.reshape(weight.shape)

    paired = last_section == 1
    pair_shape = array((2, cells, 2 * width), BF16)
    tick_outs = (state_shape, pair_shape, wide, wide, wide)
    forward, sent, back, carry, gate = call(
        functools.partial(tick_kernel, ydim, zdim, paired), "tick_one", (places, flags),
        (state, act, grad, below, above, first, second, first_back, second_back), tick_outs,
        tick_outs + (state_shape,) * 3 + (edge,) * 2 + (weight,) * 4
        + (tile, tile, wide, state_shape, outer_stack), 15, 8 * work,
    )
    if paired:
        lifted = lowered = lax.ppermute(sent, "section", [(0, 1), (1, 0)])
    else:
        lifted = lax.ppermute(forward[None], "section", [(s, s + 1) for s in range(last_section)])
        lowered = lax.ppermute(sent, "section", [(s + 1, s) for s in range(last_section)])

    join_outs = (state_shape,) * 3 + (edge, edge)
    state_two, act_two, grad_two, low, high = call(
        functools.partial(join_kernel, plane), "join", (places,),
        (forward, lifted, lowered, flat(fresh), flat(target)), join_outs,
        (state_shape, state_shape, pair_shape, state_shape, state_shape) + join_outs, 10,
    )
    below, above = exchange(low, high)
    (so_far,) = call(
        functools.partial(corr_kernel, ydim, zdim), "weight_grads", (), (grad, back, carry, gate),
        (sums_shape,), (state_shape, wide, wide, wide, sums_shape, small_stack), 5, 2 * work,
    )

    rows = offsets // count
    direct = rows % 24 == 0
    if direct:
        span = 2 * rows // 3
        outs = (array((count // 2, span, width), BF16),) * 6
    else:
        outs = (array((2, offsets, width), BF16),)
    factor = 1.0 / math.sqrt(cells * count)
    kept = (tile, tile, wide, wide, wide)
    made = call(
        functools.partial(last_kernel, ydim, zdim, factor, count, direct), "tick_two_first",
        (spot.astype(jnp.int32).reshape(1), flags),
        (state_two, act_two, grad_two, below, above, first, second, second_back, so_far), kept + outs,
        (state_shape,) * 3 + (edge,) * 2 + (weight,) * 3 + (sums_shape,) + kept + outs
        + (wide, outer_stack, sums_shape), 20, 6 * work,
    )
    forward, rebuilt, passed = call(
        functools.partial(second_alone, ydim, zdim), "tick_two_second", (),
        (state_two, act_two, grad_two, *made[:5], first, second, first_back), (state_shape,) * 3,
        (state_shape,) * 3 + kept + (weight,) * 3 + (state_shape,) * 3 + (inner_stack,), 14, 3 * work,
    )
    halves = made[5:] if direct else split_blocks(made[5], count)
    total = reduce_blocks(halves, count, rows)
    return (
        forward.reshape((1,) + shape),
        rebuilt.reshape((1,) + shape),
        passed.reshape((1,) + shape),
        total[:rows][None],
        total[rows:][None],
    )


def solution(mesh):
    placed = (
        P("section", "space", None, None, None),
        P("section", "space", None, None, None),
        P("section", "space", None, None, None),
        P("space", None, None, None),
        P("space", None, None, None),
        P("section", None, None, None),
        P("section", None, None, None),
    )
    return jax.shard_map(
        shards,
        mesh=mesh,
        in_specs=placed,
        out_specs=(
            P("section", "space", None, None, None),
            P("section", "space", None, None, None),
            P("section", "space", None, None, None),
            P("section", "space", None),
            P("section", "space", None),
        ),
        check_vma=False,
    )
```

```python
import functools
import math

import jax
import jax.numpy as jnp
from jax import lax
from jax.experimental import pallas as pl
from jax.experimental.pallas import tpu as pltpu
from jax.sharding import PartitionSpec as P

F32 = jnp.float32
BF16 = jnp.bfloat16


class Copies:
    def __init__(self, sems):
        self.sems, self.used, self.open = sems, 0, {}

    def start(self, name, source, target):
        copy = pltpu.make_async_copy(source, target, self.sems.at[self.used])
        self.used += 1
        copy.start()
        self.open[name] = copy

    def need(self, *names):
        for name in names:
            if name in self.open:
                self.open.pop(name).wait()

    def finish(self):
        self.need(*list(self.open))


def half_erf(value):
    return 0.5 * (1.0 + lax.erf(value * 0.7071067811865476))


def smooth_gate(value):
    return value * half_erf(value)


def gate_slope(value, half):
    return half + value * jnp.exp(-0.5 * value * value) * 0.3989422804014327


def fill_shifts(stack, field, ydim, zdim):
    rows, width = field.shape
    cells = field.reshape(rows // zdim, zdim, width)
    depth = lax.broadcasted_iota(jnp.int32, cells.shape, 1)
    before = jnp.where(depth == 0, 0.0, pltpu.roll(cells, 1, 1))
    after = jnp.where(depth == zdim - 1, 0.0, pltpu.roll(cells, zdim - 1, 1))
    for across, moved in enumerate((before, cells, after)):
        moved = moved.reshape(rows // (ydim * zdim), ydim, zdim, width)
        blank = jnp.zeros_like(moved[:, :1])
        shifted = (
            jnp.concatenate([blank, moved[:, :-1]], axis=1),
            moved,
            jnp.concatenate([moved[:, 1:], blank], axis=1),
        )
        for down in range(3):
            at = (3 * down + across) * width
            stack[0:rows, at : at + width] = shifted[down].reshape(rows, width).astype(BF16)


def convolve(stack, weights, rows, plane):
    total = None
    for step in range(3):
        part = jnp.dot(
            stack[step * plane : step * plane + rows, :],
            weights[step],
            preferred_element_type=F32,
        )
        total = part if total is None else total + part
    return total


def pack_edges(state, act, grad, low, high, plane):
    width = state.shape[1] // 2
    cells = state.shape[0]
    left, right = slice(0, width), slice(width, 2 * width)
    for index, (source, half) in enumerate(((state, right), (act, left), (grad, right))):
        at = index * 2 * plane
        low[at : at + 2 * plane, :] = source[0 : 2 * plane, half]
        high[at : at + 2 * plane, :] = source[cells - 2 * plane : cells, half]
    for index, (source, half) in enumerate(((state, left), (act, right), (grad, left))):
        at = (6 + index) * plane
        low[at : at + plane, :] = source[0:plane, half]
        high[at : at + plane, :] = source[cells - plane : cells, half]


def edges_kernel(plane, state, act, grad, low_out, high_out, low, high, sems):
    width = state.shape[1] // 2
    cells = state.shape[0]
    left, right = pl.ds(0, width), pl.ds(width, width)
    moves = []
    for index, (source, half) in enumerate(((state, right), (act, left), (grad, right))):
        moves.append((source, half, 2 * plane, index * 2 * plane))
    for index, (source, half) in enumerate(((state, left), (act, right), (grad, left))):
        moves.append((source, half, plane, (6 + index) * plane))
    copies = Copies(sems)
    for side, (out, result) in enumerate(((high, high_out), (low, low_out))):
        for index, (source, half, size, at) in enumerate(moves):
            start = 0 if side else cells - size
            copies.start((side, index), source.at[pl.ds(start, size), half], out.at[pl.ds(at, size), :])
    for side, (out, result) in enumerate(((high, high_out), (low, low_out))):
        copies.need(*[(side, index) for index in range(len(moves))])
        copies.start(side, out, result)
    copies.finish()


def join_kernel(plane, places, forward, lifted, lowered, fresh, target, state, act, grad, low, high):
    first_place, last_place = places[0] == 0, places[0] == places[1]
    state[...] = jnp.where(first_place, fresh[...], lifted[0])
    own = forward[...]
    act[...] = jnp.where(last_place, own, lowered[0])
    error = (own.astype(F32) - target[...].astype(F32)).astype(BF16)
    grad[...] = jnp.where(last_place, error, lowered[1])
    pack_edges(state, act, grad, low, high, plane)


def flip_kernel(first, second, state_in, act_in, grad_in, first_back, second_back, state, act, grad):
    state[...] = state_in[...]
    act[...] = act_in[...]
    grad[...] = grad_in[...]
    offsets = first.shape[0]
    for source, out in ((first, first_back), (second, second_back)):
        for k in range(offsets):
            out[offsets - 1 - k] = jnp.transpose(source[k])


def first_kernel(ydim, zdim, copies, made, flags, state, act, grad, below, above, first, second, second_back,
                 new_one, back_two, mid, back, carry, gate, stack):
    plane = ydim * zdim
    cells, double = state.shape
    width = double // 2
    inner = cells + 2 * plane
    outer = cells + 4 * plane
    left, right = slice(0, width), slice(width, double)

    def two(source, half, index):
        at = index * 2 * plane
        return jnp.concatenate(
            [below[at : at + 2 * plane, :], source[:, half], above[at : at + 2 * plane, :]], axis=0
        ).astype(F32)

    def one(source, half, index):
        at = (6 + index) * plane
        return jnp.concatenate(
            [below[at : at + plane, :], source[:, half], above[at : at + plane, :]], axis=0
        ).astype(F32)

    low_flag, high_flag = flags[0], flags[1]

    def store_masked(ref, value):
        ref[0:plane, :] = (value[0:plane].astype(F32) * low_flag).astype(BF16)
        ref[plane : plane + cells, :] = value[plane : plane + cells]
        ref[plane + cells : inner, :] = (value[plane + cells :].astype(F32) * high_flag).astype(BF16)

    core = slice(plane, plane + cells)
    copies.need("below", "above", "state")
    fill_shifts(stack, smooth_gate(two(state, right, 0)), ydim, zdim)
    copies.need("first")
    f_one = (one(state, left, 0) + convolve(stack, first, inner, plane)).astype(BF16)
    new_one[...] = f_one[core]
    store_masked(mid, smooth_gate(f_one.astype(F32)).astype(BF16))

    made("new_one", "mid")

    copies.need("act")
    y_one = two(act, left, 1)
    half = half_erf(y_one)
    gated = y_one * half
    gate[...] = gated[plane : plane + inner].astype(BF16)
    fill_shifts(stack, gated, ydim, zdim)
    copies.need("second")
    r_two = (one(act, right, 1) - convolve(stack, second, inner, plane)).astype(BF16)
    back_two[...] = r_two[core]
    store_masked(back, smooth_gate(r_two.astype(F32)).astype(BF16))

    made("gate", "back_two", "back")

    copies.need("grad")
    fill_shifts(stack, two(grad, right, 2), ydim, zdim)
    slope = gate_slope(y_one[plane : plane + inner], half[plane : plane + inner])
    copies.need("second_back")
    e_one = (one(grad, left, 2) + slope * convolve(stack, second_back, inner, plane)).astype(BF16)
    store_masked(carry, e_one)
    made("carry")


def second_kernel(ydim, zdim, copies, made, state, act, grad, new_one, back_two, mid, back, carry,
                  first, second, first_back, forward, rebuilt, passed, stack):
    plane = ydim * zdim
    cells, double = state.shape
    width = double // 2
    left, right = slice(0, width), slice(width, double)

    copies.need("back", "act", "back_two")
    fill_shifts(stack, back[...].astype(F32), ydim, zdim)
    rebuilt[:, right] = back_two[...]
    copies.need("first")
    rebuilt[:, left] = (
        act[:, left].astype(F32) - convolve(stack, first, cells, plane)
    ).astype(BF16)
    made("rebuilt")
    copies.need("carry", "grad")
    fill_shifts(stack, carry[...].astype(F32), ydim, zdim)
    passed[:, left] = carry[plane : plane + cells, :]
    r_two = back_two[...].astype(F32)
    copies.need("first_back")
    passed[:, right] = (
        grad[:, right].astype(F32)
        + gate_slope(r_two, half_erf(r_two)) * convolve(stack, first_back, cells, plane)
    ).astype(BF16)
    made("passed")
    copies.need("mid", "state", "new_one")
    fill_shifts(stack, mid[...].astype(F32), ydim, zdim)
    forward[:, left] = new_one[...]
    copies.need("second")
    forward[:, right] = (
        state[:, right].astype(F32) + convolve(stack, second, cells, plane)
    ).astype(BF16)
    made("forward")


def tick_kernel(ydim, zdim, paired, places, flags, state, act, grad, below, above, first, second,
                first_back, second_back, forward, sent, back, carry, gate, new_one, back_two, mid,
                rebuilt, stack):
    copies = Copies(None)
    ignore = lambda *names: None
    first_kernel(ydim, zdim, copies, ignore, flags, state, act, grad, below, above, first, second,
                 second_back, new_one, back_two, mid, back, carry, gate, stack)
    second_kernel(ydim, zdim, copies, ignore, state, act, grad, new_one, back_two, mid, back, carry,
                  first, second, first_back, forward, rebuilt, sent.at[1], stack)
    if paired:
        sent[0] = jnp.where(places[0] == 0, forward[...], rebuilt[...])
    else:
        sent[0] = rebuilt[...]


def correlate(stack, field, cotangent, ydim, zdim, emit):
    plane = ydim * zdim
    cells, width = cotangent.shape
    fill_shifts(stack, cotangent, ydim, zdim)
    for step in range(3):
        product = lax.dot_general(
            field[step * plane : step * plane + cells, :],
            stack[0:cells, :],
            (((0,), (0,)), ((), ())),
            preferred_element_type=F32,
        )
        for place in range(9):
            emit(9 * step + 8 - place, product[:, place * width : (place + 1) * width])


def both_grads(ydim, zdim, grad, back, carry, gate, stack, put):
    plane = ydim * zdim
    cells, double = grad.shape
    width = double // 2

    def store(which):
        return lambda k, block: put(which, slice(k * width, (k + 1) * width), block)

    own = carry[plane : plane + cells, :].astype(F32)
    correlate(stack, back, own, ydim, zdim, store(0))
    correlate(stack, gate, grad[:, width:].astype(F32), ydim, zdim, store(1))


def corr_kernel(ydim, zdim, grad, back, carry, gate, out, stack):
    def put(which, at, block):
        out[which, at, :] = block

    both_grads(ydim, zdim, grad, back, carry, gate, stack, put)


def ways_of(count, rows):
    bits = [1 << level for level in range(count.bit_length() - 1)]
    ways = 3
    span = 2 * rows // ways
    return [(way * span, span, bits[way % len(bits) :] + bits[: way % len(bits)]) for way in range(ways)]


def last_kernel(ydim, zdim, factor, count, direct, spot, flags, state, act, grad, below, above, first,
                second, first_back, second_back, so_far, *args):
    n_outs = 6 if direct else 1
    results_out, args = args[:3], args[3:]
    final_outs, args = args[:n_outs], args[n_outs:]
    results, args = args[:3], args[3:]
    refs, args = args[:n_outs], args[n_outs:]
    new_one, back_two, mid, back, carry, gate, stack, sums, sems = args
    copies = Copies(sems)
    ignore = lambda *names: None
    first_kernel(ydim, zdim, copies, ignore, flags, state, act, grad, below, above, first, second,
                 second_back, new_one, back_two, mid, back, carry, gate, stack)

    def put(which, at, block):
        sums[which, at, :] = (block + so_far[which, at, :]) * factor

    both_grads(ydim, zdim, grad, back, carry, gate, stack, put)
    if not direct:
        refs[0][...] = sums[...].astype(BF16)
        copies.start("out", refs[0], final_outs[0])
    rows = sums.shape[1] // count
    for index, (start, span, order) in enumerate(ways_of(count, rows) if direct else ()):
        mine = (spot[0] // order[0]) % 2
        for kept in (0, 1):
            side = mine if kept else 1 - mine
            out = refs[2 * index + (0 if kept else 1)]
            for j in range(count // 2):
                fixed = sum(
                    bit for level, bit in enumerate(order[1:]) if (j >> (len(order) - 2 - level)) & 1
                )
                block = fixed + side * order[0]
                pieces = []
                for which in range(2):
                    lower = max(start, which * rows)
                    upper = min(start + span, (which + 1) * rows)
                    if lower < upper:
                        at = pl.multiple_of(block * rows + (lower - which * rows), 8)
                        pieces.append(sums[which, pl.ds(at, upper - lower), :])
                value = pieces[0] if len(pieces) == 1 else jnp.concatenate(pieces, axis=0)
                out[j] = value.astype(BF16)
            at = 2 * index + (0 if kept else 1)
            copies.start(("half", at), out, final_outs[at])

    where = {"forward": 0, "rebuilt": 1, "passed": 2}

    def made(name):
        copies.start("out_" + name, results[where[name]], results_out[where[name]])

    second_kernel(ydim, zdim, copies, made, state, act, grad, new_one, back_two, mid, back, carry, first,
                  second, first_back, *results, stack)
    copies.finish()


def split_blocks(sums, count):
    blocks = jnp.concatenate([part.reshape(count, -1, part.shape[-1]) for part in sums], axis=1)
    spot = lax.axis_index("space")
    halves = []
    for start, span, order in ways_of(count, blocks.shape[1] // 2):
        part = blocks[:, start : start + span]
        part = part.reshape([2] * len(order) + list(part.shape[1:]))
        levels = [len(order) - bit.bit_length() for bit in order]
        part = jnp.transpose(part, levels + [len(order), len(order) + 1])
        part = part.reshape((2, count // 2) + part.shape[-2:])
        mine = (spot // order[0]) % 2
        for side in (mine, 1 - mine):
            halves.append(lax.dynamic_index_in_dim(part, side, 0, keepdims=False))
    return halves


def reduce_blocks(halves, count, rows):
    spot = lax.axis_index("space")
    ways = [
        (halves[2 * way], halves[2 * way + 1], order)
        for way, (_, _, order) in enumerate(ways_of(count, rows))
    ]
    for step in range(count.bit_length() - 1):
        later = []
        for keep, send, order in ways:
            bit = order[step]
            got = lax.ppermute(send, "space", [(i, i ^ bit) for i in range(count)])
            total = keep.astype(F32) + got.astype(F32)
            if step + 1 < len(order):
                total = total.astype(BF16)
                total = total.reshape((2, total.shape[0] // 2) + total.shape[1:])
                mine = (spot // order[step + 1]) % 2
                keep = lax.dynamic_index_in_dim(total, mine, 0, keepdims=False)
                send = lax.dynamic_index_in_dim(total, 1 - mine, 0, keepdims=False)
            else:
                keep, send = total[0], None
            later.append((keep, send, order))
        ways = later
    return jnp.concatenate([keep for keep, _, _ in ways], axis=0)


def shards(fwd_in, bwd_act, bwd_grad, fresh, target, w_first, w_second):
    width = w_first.shape[2]
    layers, ydim, zdim = fwd_in.shape[1:4]
    plane = ydim * zdim
    cells = layers * plane
    shape = fwd_in.shape[1:]
    flat = lambda block: block.reshape(cells, 2 * width)
    first = w_first[0].reshape(3, 9 * width, width)
    second = w_second[0].reshape(3, 9 * width, width)
    last_section = lax.axis_size("section") - 1
    place = lax.axis_index("section")
    count = lax.axis_size("space")
    spot = lax.axis_index("space")
    flags = jnp.stack([spot > 0, spot < count - 1]).astype(F32)
    up = [(i, i + 1) for i in range(count - 1)]
    down = [(i + 1, i) for i in range(count - 1)]
    array = jax.ShapeDtypeStruct
    edge = array((9 * plane, width), BF16)
    tile = array((cells, width), BF16)
    wide = array((cells + 2 * plane, width), BF16)
    state_shape = array((cells, 2 * width), BF16)
    offsets = 27 * width

    def exchange(low, high):
        below = lax.ppermute(high, "space", up)
        above = lax.ppermute(low, "space", down)
        return below, above

    state, act, grad = flat(fwd_in), flat(bwd_act), flat(bwd_grad)
    smem = pl.BlockSpec(memory_space=pltpu.SMEM)
    hbm = pl.BlockSpec(memory_space=pltpu.HBM)
    outer_stack = array((cells + 4 * plane, 9 * width), BF16)
    small_stack = array((cells, 9 * width), BF16)
    weight = array((3, 9 * width, width), BF16)
    raw_weight = array((27, width, width), BF16)
    sums_shape = array((2, offsets, width), F32)
    places = jnp.stack([place, jnp.full_like(place, last_section)]).astype(jnp.int32)

    vmem = pl.BlockSpec(memory_space=pltpu.VMEM)

    def call(kernel, name, scalars, inputs, outs, scratch, grant, copies=0, places=(vmem, vmem), flops=0):
        semaphores = [pltpu.SemaphoreType.DMA((copies,))] if copies else []
        return pl.pallas_call(
            kernel,
            out_shape=tuple(outs),
            in_specs=[smem] * len(scalars) + [places[0]] * len(inputs),
            out_specs=(places[1],) * len(outs),
            scratch_shapes=[pltpu.VMEM(like.shape, like.dtype) for like in scratch] + semaphores,
            compiler_params=pltpu.CompilerParams(vmem_limit_bytes=grant),
            cost_estimate=pl.CostEstimate(
                flops=flops, bytes_accessed=sum(x.size * 2 for x in inputs), transcendentals=0
            ),
            name=name,
        )(*scalars, *inputs)

    work = 2 * 27 * cells * width * width
    low, high = call(
        functools.partial(edges_kernel, plane), "edges", (), (state, act, grad), (edge,) * 2,
        (edge,) * 2, 65408 * 1024, 14, (hbm, hbm),
    )
    below, above = exchange(low, high)
    first_back, second_back, state, act, grad = call(
        flip_kernel, "flip", (), (w_first[0], w_second[0], state, act, grad),
        (raw_weight,) * 2 + (state_shape,) * 3, (), 16 * 1024 * 1024,
    )
    first_back, second_back = first_back.reshape(weight.shape), second_back.reshape(weight.shape)

    paired = last_section == 1
    pair_shape = array((2, cells, 2 * width), BF16)
    tick_outs = (state_shape, pair_shape, wide, wide, wide)
    forward, sent, back, carry, gate = call(
        functools.partial(tick_kernel, ydim, zdim, paired), "tick_one", (places, flags),
        (state, act, grad, below, above, first, second, first_back, second_back), tick_outs,
        (tile, tile, wide, state_shape, outer_stack), 16 * 1024 * 1024, flops=8 * work,
    )
    if paired:
        lifted = lowered = lax.ppermute(sent, "section", [(0, 1), (1, 0)])
    else:
        lifted = lax.ppermute(forward[None], "section", [(s, s + 1) for s in range(last_section)])
        lowered = lax.ppermute(sent, "section", [(s + 1, s) for s in range(last_section)])

    join_outs = (state_shape,) * 3 + (edge, edge)
    state_two, act_two, grad_two, low, high = call(
        functools.partial(join_kernel, plane), "join", (places,),
        (forward, lifted, lowered, flat(fresh), flat(target)), join_outs,
        (), 16 * 1024 * 1024,
    )
    below, above = exchange(low, high)
    (so_far,) = call(
        functools.partial(corr_kernel, ydim, zdim), "weight_grads", (), (flat(bwd_grad), back, carry, gate),
        (sums_shape,), (small_stack,), 16 * 1024 * 1024, flops=2 * work,
    )

    rows = offsets // count
    direct = rows % 24 == 0
    if direct:
        span = 2 * rows // 3
        outs = (array((count // 2, span, width), BF16),) * 6
    else:
        outs = (array((2, offsets, width), BF16),)
    factor = 1.0 / math.sqrt(cells * count)
    results = (state_shape,) * 3
    made = call(
        functools.partial(last_kernel, ydim, zdim, factor, count, direct), "tick_two",
        (spot.astype(jnp.int32).reshape(1), flags),
        (state_two, act_two, grad_two, below, above, first, second, first_back, second_back, so_far),
        results + outs,
        results + outs + (tile, tile, wide, wide, wide, wide, outer_stack, sums_shape),
        48 * 1024 * 1024, 9, (vmem, hbm), 9 * work,
    )
    forward, rebuilt, passed = made[:3]
    halves = made[3:] if direct else split_blocks(made[3], count)
    total = reduce_blocks(halves, count, rows)
    return (
        forward.reshape((1,) + shape),
        rebuilt.reshape((1,) + shape),
        passed.reshape((1,) + shape),
        total[:rows][None],
        total[rows:][None],
    )


def solution(mesh):
    placed = (
        P("section", "space", None, None, None),
        P("section", "space", None, None, None),
        P("section", "space", None, None, None),
        P("space", None, None, None),
        P("space", None, None, None),
        P("section", None, None, None),
        P("section", None, None, None),
    )
    return jax.shard_map(
        shards,
        mesh=mesh,
        in_specs=placed,
        out_specs=(
            P("section", "space", None, None, None),
            P("section", "space", None, None, None),
            P("section", "space", None, None, None),
            P("section", "space", None),
            P("section", "space", None),
        ),
        check_vma=False,
    )
```

```python
import functools
import math

import jax
import jax.numpy as jnp
from jax import lax
from jax.experimental import pallas as pl
from jax.experimental.pallas import tpu as pltpu
from jax.sharding import PartitionSpec as P

F32 = jnp.float32
BF16 = jnp.bfloat16


class Copies:
    def __init__(self, sems):
        self.sems, self.used, self.open = sems, 0, {}

    def start(self, name, source, target):
        copy = pltpu.make_async_copy(source, target, self.sems.at[self.used])
        self.used += 1
        copy.start()
        self.open[name] = copy

    def need(self, *names):
        for name in names:
            if name in self.open:
                self.open.pop(name).wait()

    def finish(self):
        self.need(*list(self.open))


def half_erf(value):
    return 0.5 * (1.0 + lax.erf(value * 0.7071067811865476))


def smooth_gate(value):
    return value * half_erf(value)


def gate_slope(value, half):
    return half + value * jnp.exp(-0.5 * value * value) * 0.3989422804014327


def fill_shifts(stack, field, ydim, zdim):
    rows, width = field.shape
    cells = field.reshape(rows // zdim, zdim, width)
    depth = lax.broadcasted_iota(jnp.int32, cells.shape, 1)
    before = jnp.where(depth == 0, 0.0, pltpu.roll(cells, 1, 1))
    after = jnp.where(depth == zdim - 1, 0.0, pltpu.roll(cells, zdim - 1, 1))
    for across, moved in enumerate((before, cells, after)):
        moved = moved.reshape(rows // (ydim * zdim), ydim, zdim, width)
        blank = jnp.zeros_like(moved[:, :1])
        shifted = (
            jnp.concatenate([blank, moved[:, :-1]], axis=1),
            moved,
            jnp.concatenate([moved[:, 1:], blank], axis=1),
        )
        for down in range(3):
            at = (3 * down + across) * width
            stack[0:rows, at : at + width] = shifted[down].reshape(rows, width).astype(BF16)


def convolve(stack, weights, rows, plane):
    total = None
    for step in range(3):
        part = jnp.dot(
            stack[step * plane : step * plane + rows, :],
            weights[step],
            preferred_element_type=F32,
        )
        total = part if total is None else total + part
    return total


def pack_edges(state, act, grad, low, high, plane):
    width = state.shape[1] // 2
    cells = state.shape[0]
    left, right = slice(0, width), slice(width, 2 * width)
    for index, (source, half) in enumerate(((state, right), (act, left), (grad, right))):
        at = index * 2 * plane
        low[at : at + 2 * plane, :] = source[0 : 2 * plane, half]
        high[at : at + 2 * plane, :] = source[cells - 2 * plane : cells, half]
    for index, (source, half) in enumerate(((state, left), (act, right), (grad, left))):
        at = (6 + index) * plane
        low[at : at + plane, :] = source[0:plane, half]
        high[at : at + plane, :] = source[cells - plane : cells, half]


def edges_kernel(plane, state, act, grad, low_out, high_out, low, high, sems):
    width = state.shape[1] // 2
    cells = state.shape[0]
    left, right = pl.ds(0, width), pl.ds(width, width)
    moves = []
    for index, (source, half) in enumerate(((state, right), (act, left), (grad, right))):
        moves.append((source, half, 2 * plane, index * 2 * plane))
    for index, (source, half) in enumerate(((state, left), (act, right), (grad, left))):
        moves.append((source, half, plane, (6 + index) * plane))
    copies = Copies(sems)
    for side, (out, result) in enumerate(((high, high_out), (low, low_out))):
        for index, (source, half, size, at) in enumerate(moves):
            start = 0 if side else cells - size
            copies.start((side, index), source.at[pl.ds(start, size), half], out.at[pl.ds(at, size), :])
    for side, (out, result) in enumerate(((high, high_out), (low, low_out))):
        copies.need(*[(side, index) for index in range(len(moves))])
        copies.start(side, out, result)
    copies.finish()


def join_kernel(plane, places, forward, lifted, lowered, fresh, target, state, act, grad, low, high):
    first_place, last_place = places[0] == 0, places[0] == places[1]
    state[...] = jnp.where(first_place, fresh[...], lifted[0])
    own = forward[...]
    act[...] = jnp.where(last_place, own, lowered[0])
    error = (own.astype(F32) - target[...].astype(F32)).astype(BF16)
    grad[...] = jnp.where(last_place, error, lowered[1])
    pack_edges(state, act, grad, low, high, plane)


def flip_kernel(first, second, state_in, act_in, grad_in, first_back, second_back, state, act, grad):
    state[...] = state_in[...]
    act[...] = act_in[...]
    grad[...] = grad_in[...]
    offsets = first.shape[0]
    for source, out in ((first, first_back), (second, second_back)):
        for k in range(offsets):
            out[offsets - 1 - k] = jnp.transpose(source[k])


def first_kernel(ydim, zdim, copies, made, flags, state, act, grad, below, above, first, second, second_back,
                 new_one, back_two, mid, back, carry, gate, stack):
    plane = ydim * zdim
    cells, double = state.shape
    width = double // 2
    inner = cells + 2 * plane
    outer = cells + 4 * plane
    left, right = slice(0, width), slice(width, double)

    def two(source, half, index):
        at = index * 2 * plane
        return jnp.concatenate(
            [below[at : at + 2 * plane, :], source[:, half], above[at : at + 2 * plane, :]], axis=0
        ).astype(F32)

    def one(source, half, index):
        at = (6 + index) * plane
        return jnp.concatenate(
            [below[at : at + plane, :], source[:, half], above[at : at + plane, :]], axis=0
        ).astype(F32)

    low_flag, high_flag = flags[0], flags[1]

    def store_masked(ref, value):
        ref[0:plane, :] = (value[0:plane].astype(F32) * low_flag).astype(BF16)
        ref[plane : plane + cells, :] = value[plane : plane + cells]
        ref[plane + cells : inner, :] = (value[plane + cells :].astype(F32) * high_flag).astype(BF16)

    core = slice(plane, plane + cells)
    copies.need("below", "above", "state")
    fill_shifts(stack, smooth_gate(two(state, right, 0)), ydim, zdim)
    copies.need("first")
    f_one = (one(state, left, 0) + convolve(stack, first, inner, plane)).astype(BF16)
    new_one[...] = f_one[core]
    store_masked(mid, smooth_gate(f_one.astype(F32)).astype(BF16))

    made("new_one", "mid")

    copies.need("act")
    y_one = two(act, left, 1)
    half = half_erf(y_one)
    gated = y_one * half
    gate[...] = gated[plane : plane + inner].astype(BF16)
    fill_shifts(stack, gated, ydim, zdim)
    copies.need("second")
    r_two = (one(act, right, 1) - convolve(stack, second, inner, plane)).astype(BF16)
    back_two[...] = r_two[core]
    store_masked(back, smooth_gate(r_two.astype(F32)).astype(BF16))

    made("gate", "back_two", "back")

    copies.need("grad")
    fill_shifts(stack, two(grad, right, 2), ydim, zdim)
    slope = gate_slope(y_one[plane : plane + inner], half[plane : plane + inner])
    copies.need("second_back")
    e_one = (one(grad, left, 2) + slope * convolve(stack, second_back, inner, plane)).astype(BF16)
    store_masked(carry, e_one)
    made("carry")


def second_kernel(ydim, zdim, copies, made, state, act, grad, new_one, back_two, mid, back, carry,
                  first, second, first_back, forward, rebuilt, passed, stack):
    plane = ydim * zdim
    cells, double = state.shape
    width = double // 2
    left, right = slice(0, width), slice(width, double)

    copies.need("back", "act", "back_two")
    fill_shifts(stack, back[...].astype(F32), ydim, zdim)
    rebuilt[:, right] = back_two[...]
    copies.need("first")
    rebuilt[:, left] = (
        act[:, left].astype(F32) - convolve(stack, first, cells, plane)
    ).astype(BF16)
    made("rebuilt")
    copies.need("carry", "grad")
    fill_shifts(stack, carry[...].astype(F32), ydim, zdim)
    passed[:, left] = carry[plane : plane + cells, :]
    r_two = back_two[...].astype(F32)
    copies.need("first_back")
    passed[:, right] = (
        grad[:, right].astype(F32)
        + gate_slope(r_two, half_erf(r_two)) * convolve(stack, first_back, cells, plane)
    ).astype(BF16)
    made("passed")
    copies.need("mid", "state", "new_one")
    fill_shifts(stack, mid[...].astype(F32), ydim, zdim)
    forward[:, left] = new_one[...]
    copies.need("second")
    forward[:, right] = (
        state[:, right].astype(F32) + convolve(stack, second, cells, plane)
    ).astype(BF16)
    made("forward")


def tick_kernel(ydim, zdim, paired, places, flags, state, act, grad, below, above, first, second,
                first_back, second_back, forward, sent, back, carry, gate, new_one, back_two, mid,
                rebuilt, stack):
    copies = Copies(None)
    ignore = lambda *names: None
    first_kernel(ydim, zdim, copies, ignore, flags, state, act, grad, below, above, first, second,
                 second_back, new_one, back_two, mid, back, carry, gate, stack)
    second_kernel(ydim, zdim, copies, ignore, state, act, grad, new_one, back_two, mid, back, carry,
                  first, second, first_back, forward, rebuilt, sent.at[1], stack)
    if paired:
        sent[0] = jnp.where(places[0] == 0, forward[...], rebuilt[...])
    else:
        sent[0] = rebuilt[...]


def correlate(stack, field, cotangent, ydim, zdim, emit):
    plane = ydim * zdim
    cells, width = cotangent.shape
    fill_shifts(stack, cotangent, ydim, zdim)
    for step in range(3):
        product = lax.dot_general(
            field[step * plane : step * plane + cells, :],
            stack[0:cells, :],
            (((0,), (0,)), ((), ())),
            preferred_element_type=F32,
        )
        for place in range(9):
            emit(9 * step + 8 - place, product[:, place * width : (place + 1) * width])


def both_grads(ydim, zdim, grad, back, carry, gate, stack, put):
    plane = ydim * zdim
    cells, double = grad.shape
    width = double // 2

    def store(which):
        return lambda k, block: put(which, slice(k * width, (k + 1) * width), block)

    own = carry[plane : plane + cells, :].astype(F32)
    correlate(stack, back, own, ydim, zdim, store(0))
    correlate(stack, gate, grad[:, width:].astype(F32), ydim, zdim, store(1))


def corr_kernel(ydim, zdim, grad, back, carry, gate, out, stack):
    def put(which, at, block):
        out[which, at, :] = block

    both_grads(ydim, zdim, grad, back, carry, gate, stack, put)


def ways_of(count, rows):
    bits = [1 << level for level in range(count.bit_length() - 1)]
    turning, last = bits[:-1], bits[-1:]
    ways = 3
    span = 2 * rows // ways
    orders = [turning[way % len(turning) :] + turning[: way % len(turning)] + last for way in range(ways)]
    return [(way * span, span, order) for way, order in enumerate(orders)]


def last_kernel(ydim, zdim, factor, count, direct, spot, flags, state, act, grad, below, above, first,
                second, first_back, second_back, so_far, *args):
    n_outs = 6 if direct else 1
    results_out, args = args[:3], args[3:]
    final_outs, args = args[:n_outs], args[n_outs:]
    results, args = args[:3], args[3:]
    refs, args = args[:n_outs], args[n_outs:]
    new_one, back_two, mid, back, carry, gate, stack, sums, sems = args
    copies = Copies(sems)
    copies.start("so_far", so_far, sums)
    ignore = lambda *names: None
    first_kernel(ydim, zdim, copies, ignore, flags, state, act, grad, below, above, first, second,
                 second_back, new_one, back_two, mid, back, carry, gate, stack)
    copies.need("so_far")

    def put(which, at, block):
        sums[which, at, :] = (block + sums[which, at, :]) * factor

    both_grads(ydim, zdim, grad, back, carry, gate, stack, put)
    if not direct:
        refs[0][...] = sums[...].astype(BF16)
        copies.start("out", refs[0], final_outs[0])
    rows = sums.shape[1] // count
    for index, (start, span, order) in enumerate(ways_of(count, rows) if direct else ()):
        mine = (spot[0] // order[0]) % 2
        for kept in (0, 1):
            side = mine if kept else 1 - mine
            out = refs[2 * index + (0 if kept else 1)]
            for j in range(count // 2):
                fixed = sum(
                    bit for level, bit in enumerate(order[1:]) if (j >> (len(order) - 2 - level)) & 1
                )
                block = fixed + side * order[0]
                pieces = []
                for which in range(2):
                    lower = max(start, which * rows)
                    upper = min(start + span, (which + 1) * rows)
                    if lower < upper:
                        at = pl.multiple_of(block * rows + (lower - which * rows), 8)
                        pieces.append(sums[which, pl.ds(at, upper - lower), :])
                value = pieces[0] if len(pieces) == 1 else jnp.concatenate(pieces, axis=0)
                out[j] = value.astype(BF16)
            at = 2 * index + (0 if kept else 1)
            copies.start(("half", at), out, final_outs[at])

    where = {"forward": 0, "rebuilt": 1, "passed": 2}

    def made(name):
        copies.start("out_" + name, results[where[name]], results_out[where[name]])

    second_kernel(ydim, zdim, copies, made, state, act, grad, new_one, back_two, mid, back, carry, first,
                  second, first_back, *results, stack)
    copies.finish()


def split_blocks(sums, count):
    blocks = jnp.concatenate([part.reshape(count, -1, part.shape[-1]) for part in sums], axis=1)
    spot = lax.axis_index("space")
    halves = []
    for start, span, order in ways_of(count, blocks.shape[1] // 2):
        part = blocks[:, start : start + span]
        part = part.reshape([2] * len(order) + list(part.shape[1:]))
        levels = [len(order) - bit.bit_length() for bit in order]
        part = jnp.transpose(part, levels + [len(order), len(order) + 1])
        part = part.reshape((2, count // 2) + part.shape[-2:])
        mine = (spot // order[0]) % 2
        for side in (mine, 1 - mine):
            halves.append(lax.dynamic_index_in_dim(part, side, 0, keepdims=False))
    return halves


def reduce_blocks(halves, count, rows):
    spot = lax.axis_index("space")
    ways = [
        (halves[2 * way], halves[2 * way + 1], order)
        for way, (_, _, order) in enumerate(ways_of(count, rows))
    ]
    def halved(total, bit):
        total = total.astype(BF16)
        total = total.reshape((2, total.shape[0] // 2) + total.shape[1:])
        mine = (spot // bit) % 2
        keep = lax.dynamic_index_in_dim(total, mine, 0, keepdims=False)
        return keep, lax.dynamic_index_in_dim(total, 1 - mine, 0, keepdims=False)

    def swapped(send, bit):
        return lax.ppermute(send, "space", [(i, i ^ bit) for i in range(count)]).astype(F32)

    depth = count.bit_length() - 1
    for step in range(depth - 1):
        later = []
        for keep, send, order in ways:
            total = keep.astype(F32) + swapped(send, order[step])
            later.append((*halved(total, order[step + 1]), order))
        ways = later
    keep = jnp.concatenate([keep[0] for keep, _, _ in ways], axis=0)
    send = jnp.concatenate([send[0] for _, send, _ in ways], axis=0)
    return keep.astype(F32) + swapped(send, ways[0][2][-1])


def shards(fwd_in, bwd_act, bwd_grad, fresh, target, w_first, w_second):
    width = w_first.shape[2]
    layers, ydim, zdim = fwd_in.shape[1:4]
    plane = ydim * zdim
    cells = layers * plane
    shape = fwd_in.shape[1:]
    flat = lambda block: block.reshape(cells, 2 * width)
    first = w_first[0].reshape(3, 9 * width, width)
    second = w_second[0].reshape(3, 9 * width, width)
    last_section = lax.axis_size("section") - 1
    place = lax.axis_index("section")
    count = lax.axis_size("space")
    spot = lax.axis_index("space")
    flags = jnp.stack([spot > 0, spot < count - 1]).astype(F32)
    up = [(i, i + 1) for i in range(count - 1)]
    down = [(i + 1, i) for i in range(count - 1)]
    array = jax.ShapeDtypeStruct
    edge = array((9 * plane, width), BF16)
    tile = array((cells, width), BF16)
    wide = array((cells + 2 * plane, width), BF16)
    state_shape = array((cells, 2 * width), BF16)
    offsets = 27 * width

    def exchange(low, high):
        below = lax.ppermute(high, "space", up)
        above = lax.ppermute(low, "space", down)
        return below, above

    state, act, grad = flat(fwd_in), flat(bwd_act), flat(bwd_grad)
    smem = pl.BlockSpec(memory_space=pltpu.SMEM)
    hbm = pl.BlockSpec(memory_space=pltpu.HBM)
    outer_stack = array((cells + 4 * plane, 9 * width), BF16)
    small_stack = array((cells, 9 * width), BF16)
    weight = array((3, 9 * width, width), BF16)
    raw_weight = array((27, width, width), BF16)
    sums_shape = array((2, offsets, width), F32)
    places = jnp.stack([place, jnp.full_like(place, last_section)]).astype(jnp.int32)

    vmem = pl.BlockSpec(memory_space=pltpu.VMEM)

    def call(kernel, name, scalars, inputs, outs, scratch, grant, copies=0, places=(vmem, vmem), flops=0,
             far=0):
        semaphores = [pltpu.SemaphoreType.DMA((copies,))] if copies else []
        return pl.pallas_call(
            kernel,
            out_shape=tuple(outs),
            in_specs=[smem] * len(scalars) + [places[0]] * (len(inputs) - far) + [hbm] * far,
            out_specs=(places[1],) * len(outs),
            scratch_shapes=[pltpu.VMEM(like.shape, like.dtype) for like in scratch] + semaphores,
            compiler_params=pltpu.CompilerParams(vmem_limit_bytes=grant),
            cost_estimate=pl.CostEstimate(
                flops=flops, bytes_accessed=sum(x.size * 2 for x in inputs), transcendentals=0
            ),
            name=name,
        )(*scalars, *inputs)

    work = 2 * 27 * cells * width * width
    low, high = call(
        functools.partial(edges_kernel, plane), "edges", (), (state, act, grad), (edge,) * 2,
        (edge,) * 2, 65408 * 1024, 14, (hbm, hbm),
    )
    below, above = exchange(low, high)
    first_back, second_back, state, act, grad = call(
        flip_kernel, "flip", (), (w_first[0], w_second[0], state, act, grad),
        (raw_weight,) * 2 + (state_shape,) * 3, (), 16 * 1024 * 1024,
    )
    first_back, second_back = first_back.reshape(weight.shape), second_back.reshape(weight.shape)

    paired = last_section == 1
    pair_shape = array((2, cells, 2 * width), BF16)
    tick_outs = (state_shape, pair_shape, wide, wide, wide)
    forward, sent, back, carry, gate = call(
        functools.partial(tick_kernel, ydim, zdim, paired), "tick_one", (places, flags),
        (state, act, grad, below, above, first, second, first_back, second_back), tick_outs,
        (tile, tile, wide, state_shape, outer_stack), 16 * 1024 * 1024, flops=8 * work,
    )
    if paired:
        lifted = lowered = lax.ppermute(sent, "section", [(0, 1), (1, 0)])
    else:
        lifted = lax.ppermute(forward[None], "section", [(s, s + 1) for s in range(last_section)])
        lowered = lax.ppermute(sent, "section", [(s + 1, s) for s in range(last_section)])

    join_outs = (state_shape,) * 3 + (edge, edge)
    state_two, act_two, grad_two, low, high = call(
        functools.partial(join_kernel, plane), "join", (places,),
        (forward, lifted, lowered, flat(fresh), flat(target)), join_outs,
        (), 16 * 1024 * 1024,
    )
    below, above = exchange(low, high)
    (so_far,) = call(
        functools.partial(corr_kernel, ydim, zdim), "weight_grads", (), (flat(bwd_grad), back, carry, gate),
        (sums_shape,), (small_stack,), 16 * 1024 * 1024, flops=2 * work,
    )

    rows = offsets // count
    direct = rows % 24 == 0
    if direct:
        span = 2 * rows // 3
        outs = (array((count // 2, span, width), BF16),) * 6
    else:
        outs = (array((2, offsets, width), BF16),)
    factor = 1.0 / math.sqrt(cells * count)
    results = (state_shape,) * 3
    made = call(
        functools.partial(last_kernel, ydim, zdim, factor, count, direct), "tick_two",
        (spot.astype(jnp.int32).reshape(1), flags),
        (state_two, act_two, grad_two, below, above, first, second, first_back, second_back, so_far),
        results + outs,
        results + outs + (tile, tile, wide, wide, wide, wide, outer_stack, sums_shape),
        48 * 1024 * 1024, 10, (vmem, hbm), 9 * work, 1,
    )
    forward, rebuilt, passed = made[:3]
    halves = made[3:] if direct else split_blocks(made[3], count)
    total = reduce_blocks(halves, count, rows)
    return (
        forward.reshape((1,) + shape),
        rebuilt.reshape((1,) + shape),
        passed.reshape((1,) + shape),
        total[:rows][None],
        total[rows:][None],
    )


def solution(mesh):
    placed = (
        P("section", "space", None, None, None),
        P("section", "space", None, None, None),
        P("section", "space", None, None, None),
        P("space", None, None, None),
        P("space", None, None, None),
        P("section", None, None, None),
        P("section", None, None, None),
    )
    return jax.shard_map(
        shards,
        mesh=mesh,
        in_specs=placed,
        out_specs=(
            P("section", "space", None, None, None),
            P("section", "space", None, None, None),
            P("section", "space", None, None, None),
            P("section", "space", None),
            P("section", "space", None),
        ),
        check_vma=False,
    )
```

```python
import functools
import math

import jax
import jax.numpy as jnp
from jax import lax
from jax.experimental import pallas as pl
from jax.experimental.pallas import tpu as pltpu
from jax.sharding import PartitionSpec as P

F32 = jnp.float32
BF16 = jnp.bfloat16


class Copies:
    def __init__(self, sems):
        self.sems, self.used, self.open = sems, 0, {}

    def start(self, name, source, target):
        copy = pltpu.make_async_copy(source, target, self.sems.at[self.used])
        self.used += 1
        copy.start()
        self.open[name] = copy

    def need(self, *names):
        for name in names:
            if name in self.open:
                self.open.pop(name).wait()

    def finish(self):
        self.need(*list(self.open))


def half_erf(value):
    return 0.5 * (1.0 + lax.erf(value * 0.7071067811865476))


def smooth_gate(value):
    return value * half_erf(value)


def gate_slope(value, half):
    return half + value * jnp.exp(-0.5 * value * value) * 0.3989422804014327


def fill_shifts(stack, field, ydim, zdim):
    rows, width = field.shape
    cells = field.reshape(rows // zdim, zdim, width)
    depth = lax.broadcasted_iota(jnp.int32, cells.shape, 1)
    before = jnp.where(depth == 0, 0.0, pltpu.roll(cells, 1, 1))
    after = jnp.where(depth == zdim - 1, 0.0, pltpu.roll(cells, zdim - 1, 1))
    for across, moved in enumerate((before, cells, after)):
        moved = moved.reshape(rows // (ydim * zdim), ydim, zdim, width)
        blank = jnp.zeros_like(moved[:, :1])
        shifted = (
            jnp.concatenate([blank, moved[:, :-1]], axis=1),
            moved,
            jnp.concatenate([moved[:, 1:], blank], axis=1),
        )
        for down in range(3):
            at = (3 * down + across) * width
            stack[0:rows, at : at + width] = shifted[down].reshape(rows, width).astype(BF16)


def convolve(stack, weights, rows, plane):
    total = None
    for step in range(3):
        part = jnp.dot(
            stack[step * plane : step * plane + rows, :],
            weights[step],
            preferred_element_type=F32,
        )
        total = part if total is None else total + part
    return total


def pack_edges(odd, state, act, grad, near, far, plane):
    width = state.shape[1] // 2
    cells = state.shape[0]
    left, right = slice(0, width), slice(width, 2 * width)

    def put(at, size, source, half):
        low = source[0:size, half]
        high = source[cells - size : cells, half]
        near[at : at + size, :] = jnp.where(odd, low, high)
        far[at : at + size, :] = jnp.where(odd, high, low)

    for index, (source, half) in enumerate(((state, right), (act, left), (grad, right))):
        put(index * 2 * plane, 2 * plane, source, half)
    for index, (source, half) in enumerate(((state, left), (act, right), (grad, left))):
        put((6 + index) * plane, plane, source, half)


def edges_kernel(plane, state, act, grad, near_out, far_out, near, far, sems):
    width = state.shape[1] // 2
    cells = state.shape[0]
    left, right = pl.ds(0, width), pl.ds(width, width)
    moves = []
    for index, (source, half) in enumerate(((state, right), (act, left), (grad, right))):
        moves.append((source, half, 2 * plane, index * 2 * plane))
    for index, (source, half) in enumerate(((state, left), (act, right), (grad, left))):
        moves.append((source, half, plane, (6 + index) * plane))
    copies = Copies(sems)
    odd = lax.rem(lax.axis_index("space"), 2)
    for side, (out, high) in enumerate(((near, 1 - odd), (far, odd))):
        for index, (source, half, size, at) in enumerate(moves):
            start = pl.multiple_of(high * (cells - size), plane)
            copies.start((side, index), source.at[pl.ds(start, size), half], out.at[pl.ds(at, size), :])
    for side, (out, result) in enumerate(((near, near_out), (far, far_out))):
        copies.need(*[(side, index) for index in range(len(moves))])
        copies.start(side, out, result)
    copies.finish()


def join_kernel(plane, forward, lifted, lowered, fresh, target, state, act, grad, near, far):
    place = lax.axis_index("section")
    first_place, last_place = place == 0, place == lax.axis_size("section") - 1
    state[...] = jnp.where(first_place, fresh[...], lifted[0])
    own = forward[...]
    act[...] = jnp.where(last_place, own, lowered[0])
    error = (own.astype(F32) - target[...].astype(F32)).astype(BF16)
    grad[...] = jnp.where(last_place, error, lowered[1])
    pack_edges(lax.rem(lax.axis_index("space"), 2) == 1, state, act, grad, near, far, plane)


def flip_kernel(first, second, state_in, act_in, grad_in, first_back, second_back, state, act, grad):
    state[...] = state_in[...]
    act[...] = act_in[...]
    grad[...] = grad_in[...]
    offsets = first.shape[0]
    for source, out in ((first, first_back), (second, second_back)):
        for k in range(offsets):
            out[offsets - 1 - k] = jnp.transpose(source[k])


def first_kernel(ydim, zdim, copies, made, state, act, grad, near, far, first, second, second_back,
                 new_one, back_two, mid, back, carry, gate, stack):
    plane = ydim * zdim
    cells, double = state.shape
    width = double // 2
    inner = cells + 2 * plane
    outer = cells + 4 * plane
    left, right = slice(0, width), slice(width, double)

    spot = lax.axis_index("space")
    odd = lax.rem(spot, 2) == 1

    def around(source, half, at, size):
        one_side, other_side = near[at : at + size, :], far[at : at + size, :]
        below = jnp.where(odd, one_side, other_side)
        above = jnp.where(odd, other_side, one_side)
        return jnp.concatenate([below, source[:, half], above], axis=0).astype(F32)

    def two(source, half, index):
        return around(source, half, index * 2 * plane, 2 * plane)

    def one(source, half, index):
        return around(source, half, (6 + index) * plane, plane)

    inside_low, inside_high = spot > 0, spot < lax.axis_size("space") - 1

    def store_masked(ref, value):
        blank = jnp.zeros((plane, width), BF16)
        ref[0:plane, :] = jnp.where(inside_low, value[0:plane], blank)
        ref[plane : plane + cells, :] = value[plane : plane + cells]
        ref[plane + cells : inner, :] = jnp.where(inside_high, value[plane + cells :], blank)

    core = slice(plane, plane + cells)
    copies.need("near", "far", "state")
    fill_shifts(stack, smooth_gate(two(state, right, 0)), ydim, zdim)
    copies.need("first")
    f_one = (one(state, left, 0) + convolve(stack, first, inner, plane)).astype(BF16)
    new_one[...] = f_one[core]
    store_masked(mid, smooth_gate(f_one.astype(F32)).astype(BF16))

    made("new_one", "mid")

    copies.need("act")
    y_one = two(act, left, 1)
    half = half_erf(y_one)
    gated = y_one * half
    gate[...] = gated[plane : plane + inner].astype(BF16)
    fill_shifts(stack, gated, ydim, zdim)
    copies.need("second")
    r_two = (one(act, right, 1) - convolve(stack, second, inner, plane)).astype(BF16)
    back_two[...] = r_two[core]
    store_masked(back, smooth_gate(r_two.astype(F32)).astype(BF16))

    made("gate", "back_two", "back")

    copies.need("grad")
    fill_shifts(stack, two(grad, right, 2), ydim, zdim)
    slope = gate_slope(y_one[plane : plane + inner], half[plane : plane + inner])
    copies.need("second_back")
    e_one = (one(grad, left, 2) + slope * convolve(stack, second_back, inner, plane)).astype(BF16)
    store_masked(carry, e_one)
    made("carry")


def second_kernel(ydim, zdim, copies, made, state, act, grad, new_one, back_two, mid, back, carry,
                  first, second, first_back, forward, rebuilt, passed, stack):
    plane = ydim * zdim
    cells, double = state.shape
    width = double // 2
    left, right = slice(0, width), slice(width, double)

    copies.need("back", "act", "back_two")
    fill_shifts(stack, back[...].astype(F32), ydim, zdim)
    rebuilt[:, right] = back_two[...]
    copies.need("first")
    rebuilt[:, left] = (
        act[:, left].astype(F32) - convolve(stack, first, cells, plane)
    ).astype(BF16)
    made("rebuilt")
    copies.need("carry", "grad")
    fill_shifts(stack, carry[...].astype(F32), ydim, zdim)
    passed[:, left] = carry[plane : plane + cells, :]
    r_two = back_two[...].astype(F32)
    copies.need("first_back")
    passed[:, right] = (
        grad[:, right].astype(F32)
        + gate_slope(r_two, half_erf(r_two)) * convolve(stack, first_back, cells, plane)
    ).astype(BF16)
    made("passed")
    copies.need("mid", "state", "new_one")
    fill_shifts(stack, mid[...].astype(F32), ydim, zdim)
    forward[:, left] = new_one[...]
    copies.need("second")
    forward[:, right] = (
        state[:, right].astype(F32) + convolve(stack, second, cells, plane)
    ).astype(BF16)
    made("forward")


def tick_kernel(ydim, zdim, paired, state, act, grad, near, far, first, second,
                first_back, second_back, forward, sent, back, carry, gate, new_one, back_two, mid,
                rebuilt, stack):
    copies = Copies(None)
    ignore = lambda *names: None
    first_kernel(ydim, zdim, copies, ignore, state, act, grad, near, far, first, second,
                 second_back, new_one, back_two, mid, back, carry, gate, stack)
    second_kernel(ydim, zdim, copies, ignore, state, act, grad, new_one, back_two, mid, back, carry,
                  first, second, first_back, forward, rebuilt, sent.at[1], stack)
    if paired:
        sent[0] = jnp.where(lax.axis_index("section") == 0, forward[...], rebuilt[...])
    else:
        sent[0] = rebuilt[...]


def correlate(stack, field, cotangent, ydim, zdim, emit):
    plane = ydim * zdim
    cells, width = cotangent.shape
    fill_shifts(stack, cotangent, ydim, zdim)
    for step in range(3):
        product = lax.dot_general(
            field[step * plane : step * plane + cells, :],
            stack[0:cells, :],
            (((0,), (0,)), ((), ())),
            preferred_element_type=F32,
        )
        for place in range(9):
            emit(9 * step + 8 - place, product[:, place * width : (place + 1) * width])


def both_grads(ydim, zdim, grad, back, carry, gate, stack, put):
    plane = ydim * zdim
    cells, double = grad.shape
    width = double // 2

    def store(which):
        return lambda k, block: put(which, slice(k * width, (k + 1) * width), block)

    own = carry[plane : plane + cells, :].astype(F32)
    correlate(stack, back, own, ydim, zdim, store(0))
    correlate(stack, gate, grad[:, width:].astype(F32), ydim, zdim, store(1))


def corr_kernel(ydim, zdim, grad, back, carry, gate, out, stack):
    def put(which, at, block):
        out[which, at, :] = block

    both_grads(ydim, zdim, grad, back, carry, gate, stack, put)


def ways_of(count, rows):
    bits = [1 << level for level in range(count.bit_length() - 1)]
    turning, last = bits[:-1], bits[-1:]
    ways = 3
    span = 2 * rows // ways
    orders = [turning[way % len(turning) :] + turning[: way % len(turning)] + last for way in range(ways)]
    return [(way * span, span, order) for way, order in enumerate(orders)]


def last_kernel(ydim, zdim, factor, count, direct, state, act, grad, near, far, first,
                second, first_back, second_back, so_far, *args):
    n_outs = 6 if direct else 1
    results_out, args = args[:3], args[3:]
    final_outs, args = args[:n_outs], args[n_outs:]
    results, args = args[:3], args[3:]
    refs, args = args[:n_outs], args[n_outs:]
    new_one, back_two, mid, back, carry, gate, stack, sums, sems = args
    copies = Copies(sems)
    copies.start("so_far", so_far, sums)
    ignore = lambda *names: None
    first_kernel(ydim, zdim, copies, ignore, state, act, grad, near, far, first, second,
                 second_back, new_one, back_two, mid, back, carry, gate, stack)
    copies.need("so_far")

    def put(which, at, block):
        sums[which, at, :] = (block + sums[which, at, :]) * factor

    both_grads(ydim, zdim, grad, back, carry, gate, stack, put)
    if not direct:
        refs[0][...] = sums[...].astype(BF16)
        copies.start("out", refs[0], final_outs[0])
    rows = sums.shape[1] // count
    for index, (start, span, order) in enumerate(ways_of(count, rows) if direct else ()):
        mine = lax.rem(lax.div(lax.axis_index("space"), order[0]), 2)
        for kept in (0, 1):
            side = mine if kept else 1 - mine
            out = refs[2 * index + (0 if kept else 1)]
            for j in range(count // 2):
                fixed = sum(
                    bit for level, bit in enumerate(order[1:]) if (j >> (len(order) - 2 - level)) & 1
                )
                block = fixed + side * order[0]
                pieces = []
                for which in range(2):
                    lower = max(start, which * rows)
                    upper = min(start + span, (which + 1) * rows)
                    if lower < upper:
                        at = pl.multiple_of(block * rows + (lower - which * rows), 8)
                        pieces.append(sums[which, pl.ds(at, upper - lower), :])
                value = pieces[0] if len(pieces) == 1 else jnp.concatenate(pieces, axis=0)
                out[j] = value.astype(BF16)
            at = 2 * index + (0 if kept else 1)
            copies.start(("half", at), out, final_outs[at])

    where = {"forward": 0, "rebuilt": 1, "passed": 2}

    def made(name):
        copies.start("out_" + name, results[where[name]], results_out[where[name]])

    second_kernel(ydim, zdim, copies, made, state, act, grad, new_one, back_two, mid, back, carry, first,
                  second, first_back, *results, stack)
    copies.finish()


def split_blocks(sums, count):
    blocks = jnp.concatenate([part.reshape(count, -1, part.shape[-1]) for part in sums], axis=1)
    spot = lax.axis_index("space")
    halves = []
    for start, span, order in ways_of(count, blocks.shape[1] // 2):
        part = blocks[:, start : start + span]
        part = part.reshape([2] * len(order) + list(part.shape[1:]))
        levels = [len(order) - bit.bit_length() for bit in order]
        part = jnp.transpose(part, levels + [len(order), len(order) + 1])
        part = part.reshape((2, count // 2) + part.shape[-2:])
        mine = (spot // order[0]) % 2
        for side in (mine, 1 - mine):
            halves.append(lax.dynamic_index_in_dim(part, side, 0, keepdims=False))
    return halves


def reduce_blocks(halves, count, rows):
    spot = lax.axis_index("space")
    ways = [
        (halves[2 * way], halves[2 * way + 1], order)
        for way, (_, _, order) in enumerate(ways_of(count, rows))
    ]
    def halved(total, bit):
        total = total.astype(BF16)
        total = total.reshape((2, total.shape[0] // 2) + total.shape[1:])
        mine = (spot // bit) % 2
        keep = lax.dynamic_index_in_dim(total, mine, 0, keepdims=False)
        return keep, lax.dynamic_index_in_dim(total, 1 - mine, 0, keepdims=False)

    def swapped(send, bit):
        return lax.ppermute(send, "space", [(i, i ^ bit) for i in range(count)]).astype(F32)

    depth = count.bit_length() - 1
    for step in range(depth - 1):
        later = []
        for keep, send, order in ways:
            total = keep.astype(F32) + swapped(send, order[step])
            later.append((*halved(total, order[step + 1]), order))
        ways = later
    keep = jnp.concatenate([keep[0] for keep, _, _ in ways], axis=0)
    send = jnp.concatenate([send[0] for _, send, _ in ways], axis=0)
    return keep.astype(F32) + swapped(send, ways[0][2][-1])


def shards(fwd_in, bwd_act, bwd_grad, fresh, target, w_first, w_second):
    width = w_first.shape[2]
    layers, ydim, zdim = fwd_in.shape[1:4]
    plane = ydim * zdim
    cells = layers * plane
    shape = fwd_in.shape[1:]
    flat = lambda block: block.reshape(cells, 2 * width)
    first = w_first[0].reshape(3, 9 * width, width)
    second = w_second[0].reshape(3, 9 * width, width)
    last_section = lax.axis_size("section") - 1
    place = lax.axis_index("section")
    count = lax.axis_size("space")
    beside = [(i, i ^ 1) for i in range(count) if i ^ 1 < count]
    across = [pair for i in range(1, count - 1, 2) for pair in ((i, i + 1), (i + 1, i))]
    array = jax.ShapeDtypeStruct
    edge = array((9 * plane, width), BF16)
    tile = array((cells, width), BF16)
    wide = array((cells + 2 * plane, width), BF16)
    state_shape = array((cells, 2 * width), BF16)
    offsets = 27 * width

    def exchange(near, far):
        far = lax.ppermute(far, "space", across)
        near = lax.ppermute(near, "space", beside)
        return near, far

    state, act, grad = flat(fwd_in), flat(bwd_act), flat(bwd_grad)
    hbm = pl.BlockSpec(memory_space=pltpu.HBM)
    outer_stack = array((cells + 4 * plane, 9 * width), BF16)
    small_stack = array((cells, 9 * width), BF16)
    weight = array((3, 9 * width, width), BF16)
    raw_weight = array((27, width, width), BF16)
    sums_shape = array((2, offsets, width), F32)

    vmem = pl.BlockSpec(memory_space=pltpu.VMEM)

    def call(kernel, name, inputs, outs, scratch, grant, copies=0, places=(vmem, vmem), flops=0,
             far=0):
        semaphores = [pltpu.SemaphoreType.DMA((copies,))] if copies else []
        return pl.pallas_call(
            kernel,
            out_shape=tuple(outs),
            in_specs=[places[0]] * (len(inputs) - far) + [hbm] * far,
            out_specs=(places[1],) * len(outs),
            scratch_shapes=[pltpu.VMEM(like.shape, like.dtype) for like in scratch] + semaphores,
            compiler_params=pltpu.CompilerParams(vmem_limit_bytes=grant),
            cost_estimate=pl.CostEstimate(
                flops=flops, bytes_accessed=sum(x.size * 2 for x in inputs), transcendentals=0
            ),
            name=name,
        )(*inputs)

    work = 2 * 27 * cells * width * width
    near, far = call(
        functools.partial(edges_kernel, plane), "edges", (state, act, grad), (edge,) * 2,
        (edge,) * 2, 65408 * 1024, 14, (hbm, hbm),
    )
    near, far = exchange(near, far)
    first_back, second_back, state, act, grad = call(
        flip_kernel, "flip", (w_first[0], w_second[0], state, act, grad),
        (raw_weight,) * 2 + (state_shape,) * 3, (), 16 * 1024 * 1024,
    )
    first_back, second_back = first_back.reshape(weight.shape), second_back.reshape(weight.shape)

    paired = last_section == 1
    pair_shape = array((2, cells, 2 * width), BF16)
    tick_outs = (state_shape, pair_shape, wide, wide, wide)
    forward, sent, back, carry, gate = call(
        functools.partial(tick_kernel, ydim, zdim, paired), "tick_one",
        (state, act, grad, near, far, first, second, first_back, second_back), tick_outs,
        (tile, tile, wide, state_shape, outer_stack), 16 * 1024 * 1024, flops=8 * work,
    )
    if paired:
        lifted = lowered = lax.ppermute(sent, "section", [(0, 1), (1, 0)])
    else:
        lifted = lax.ppermute(forward[None], "section", [(s, s + 1) for s in range(last_section)])
        lowered = lax.ppermute(sent, "section", [(s + 1, s) for s in range(last_section)])

    join_outs = (state_shape,) * 3 + (edge, edge)
    state_two, act_two, grad_two, near, far = call(
        functools.partial(join_kernel, plane), "join",
        (forward, lifted, lowered, flat(fresh), flat(target)), join_outs,
        (), 16 * 1024 * 1024,
    )
    near, far = exchange(near, far)
    (so_far,) = call(
        functools.partial(corr_kernel, ydim, zdim), "weight_grads", (flat(bwd_grad), back, carry, gate),
        (sums_shape,), (small_stack,), 16 * 1024 * 1024, flops=2 * work,
    )

    rows = offsets // count
    direct = rows % 24 == 0
    if direct:
        span = 2 * rows // 3
        outs = (array((count // 2, span, width), BF16),) * 6
    else:
        outs = (array((2, offsets, width), BF16),)
    factor = 1.0 / math.sqrt(cells * count)
    results = (state_shape,) * 3
    made = call(
        functools.partial(last_kernel, ydim, zdim, factor, count, direct), "tick_two",
        (state_two, act_two, grad_two, near, far, first, second, first_back, second_back, so_far),
        results + outs,
        results + outs + (tile, tile, wide, wide, wide, wide, outer_stack, sums_shape),
        48 * 1024 * 1024, 10, (vmem, hbm), 9 * work, 1,
    )
    forward, rebuilt, passed = made[:3]
    halves = made[3:] if direct else split_blocks(made[3], count)
    total = reduce_blocks(halves, count, rows)
    return (
        forward.reshape((1,) + shape),
        rebuilt.reshape((1,) + shape),
        passed.reshape((1,) + shape),
        total[:rows][None],
        total[rows:][None],
    )


def solution(mesh):
    placed = (
        P("section", "space", None, None, None),
        P("section", "space", None, None, None),
        P("section", "space", None, None, None),
        P("space", None, None, None),
        P("space", None, None, None),
        P("section", None, None, None),
        P("section", None, None, None),
    )
    return jax.shard_map(
        shards,
        mesh=mesh,
        in_specs=placed,
        out_specs=(
            P("section", "space", None, None, None),
            P("section", "space", None, None, None),
            P("section", "space", None, None, None),
            P("section", "space", None),
            P("section", "space", None),
        ),
        check_vma=False,
    )
```

```python
import functools
import math

import jax
import jax.numpy as jnp
from jax import lax
from jax.experimental import pallas as pl
from jax.experimental.pallas import tpu as pltpu
from jax.sharding import PartitionSpec as P

F32 = jnp.float32
BF16 = jnp.bfloat16


class Copies:
    def __init__(self, sems):
        self.sems, self.used, self.open = sems, 0, {}

    def start(self, name, source, target):
        copy = pltpu.make_async_copy(source, target, self.sems.at[self.used])
        self.used += 1
        copy.start()
        self.open[name] = copy

    def need(self, *names):
        for name in names:
            if name in self.open:
                self.open.pop(name).wait()

    def finish(self):
        self.need(*list(self.open))


def half_erf(value):
    return 0.5 * (1.0 + lax.erf(value * 0.7071067811865476))


def smooth_gate(value):
    return value * half_erf(value)


def gate_slope(value, half):
    return half + value * jnp.exp(-0.5 * value * value) * 0.3989422804014327


def fill_shifts(stack, field, ydim, zdim):
    rows, width = field.shape
    cells = field.reshape(rows // zdim, zdim, width)
    depth = lax.broadcasted_iota(jnp.int32, cells.shape, 1)
    before = jnp.where(depth == 0, 0.0, pltpu.roll(cells, 1, 1))
    after = jnp.where(depth == zdim - 1, 0.0, pltpu.roll(cells, zdim - 1, 1))
    for across, moved in enumerate((before, cells, after)):
        moved = moved.reshape(rows // (ydim * zdim), ydim, zdim, width)
        blank = jnp.zeros_like(moved[:, :1])
        shifted = (
            jnp.concatenate([blank, moved[:, :-1]], axis=1),
            moved,
            jnp.concatenate([moved[:, 1:], blank], axis=1),
        )
        for down in range(3):
            at = (3 * down + across) * width
            stack[0:rows, at : at + width] = shifted[down].reshape(rows, width).astype(BF16)


def convolve(stack, weights, rows, plane):
    total = None
    for step in range(3):
        part = jnp.dot(
            stack[step * plane : step * plane + rows, :],
            weights[step],
            preferred_element_type=F32,
        )
        total = part if total is None else total + part
    return total


def pack_edges(odd, state, act, grad, near, far, plane):
    width = state.shape[1] // 2
    cells = state.shape[0]
    left, right = slice(0, width), slice(width, 2 * width)

    def put(at, size, source, half):
        low = source[0:size, half]
        high = source[cells - size : cells, half]
        near[at : at + size, :] = jnp.where(odd, low, high)
        far[at : at + size, :] = jnp.where(odd, high, low)

    for index, (source, half) in enumerate(((state, right), (act, left), (grad, right))):
        put(index * 2 * plane, 2 * plane, source, half)
    for index, (source, half) in enumerate(((state, left), (act, right), (grad, left))):
        put((6 + index) * plane, plane, source, half)


def edges_kernel(plane, state, act, grad, near_out, far_out, near, far, sems):
    width = state.shape[1] // 2
    cells = state.shape[0]
    left, right = pl.ds(0, width), pl.ds(width, width)
    moves = []
    for index, (source, half) in enumerate(((state, right), (act, left), (grad, right))):
        moves.append((source, half, 2 * plane, index * 2 * plane))
    for index, (source, half) in enumerate(((state, left), (act, right), (grad, left))):
        moves.append((source, half, plane, (6 + index) * plane))
    copies = Copies(sems)
    odd = lax.rem(lax.axis_index("space"), 2)
    for side, (out, high) in enumerate(((near, 1 - odd), (far, odd))):
        for index, (source, half, size, at) in enumerate(moves):
            start = pl.multiple_of(high * (cells - size), plane)
            copies.start((side, index), source.at[pl.ds(start, size), half], out.at[pl.ds(at, size), :])
    for side, (out, result) in enumerate(((near, near_out), (far, far_out))):
        copies.need(*[(side, index) for index in range(len(moves))])
        copies.start(side, out, result)
    copies.finish()


def join_kernel(plane, forward, lifted, lowered, fresh, target, state, act, grad, near, far):
    place = lax.axis_index("section")
    first_place, last_place = place == 0, place == lax.axis_size("section") - 1
    state[...] = jnp.where(first_place, fresh[...], lifted[0])
    own = forward[...]
    act[...] = jnp.where(last_place, own, lowered[0])
    error = (own.astype(F32) - target[...].astype(F32)).astype(BF16)
    grad[...] = jnp.where(last_place, error, lowered[1])
    pack_edges(lax.rem(lax.axis_index("space"), 2) == 1, state, act, grad, near, far, plane)


def own_kernel(ydim, zdim, state, act, grad, first, second, second_back, partial, stack):
    own_sums(ydim, zdim, gated_fields(state, act, grad), (first, second, second_back), partial, stack)


def flip_kernel(first, second, state_in, act_in, grad_in, first_back, second_back, state, act, grad):
    state[...] = state_in[...]
    act[...] = act_in[...]
    grad[...] = grad_in[...]
    offsets = first.shape[0]
    for source, out in ((first, first_back), (second, second_back)):
        for k in range(offsets):
            out[offsets - 1 - k] = jnp.transpose(source[k])


def own_sums(ydim, zdim, fields, weights, partial, stack):
    plane = ydim * zdim
    for index, (field, weight) in enumerate(zip(fields, weights)):
        fill_shifts(stack, field, ydim, zdim)
        cells = field.shape[0]
        partial[index] = jnp.zeros(partial.shape[1:], F32)
        for step in range(3):
            at = (2 - step) * plane
            partial[index, at : at + cells, :] += jnp.dot(
                stack[0:cells, :], weight[step], preferred_element_type=F32
            )


def gated_fields(state, act, grad):
    width = state.shape[1] // 2
    return (
        smooth_gate(state[:, width:].astype(F32)),
        smooth_gate(act[:, :width].astype(F32)),
        grad[:, width:].astype(F32),
    )


def halo_sums(index, partial, stack, weights, plane):
    total = partial[index]
    inner = total.shape[0]
    low = jnp.dot(stack[0 : 2 * plane, :], weights[0], preferred_element_type=F32)
    both = jnp.dot(stack[plane : 3 * plane, :], weights[1], preferred_element_type=F32)
    high = jnp.dot(stack[2 * plane : 4 * plane, :], weights[2], preferred_element_type=F32)
    return jnp.concatenate(
        [
            total[0:plane] + low[0:plane] + both[0:plane],
            total[plane : 2 * plane] + low[plane:],
            total[2 * plane : inner - 2 * plane],
            total[inner - 2 * plane : inner - plane] + high[0:plane],
            total[inner - plane :] + high[plane:] + both[plane:],
        ],
        axis=0,
    )


def first_kernel(ydim, zdim, copies, made, state, act, grad, near, far, first, second, second_back, partial,
                 new_one, back_two, mid, back, carry, gate, stack):
    plane = ydim * zdim
    cells, double = state.shape
    width = double // 2
    inner = cells + 2 * plane
    outer = cells + 4 * plane
    left, right = slice(0, width), slice(width, double)

    spot = lax.axis_index("space")
    odd = lax.rem(spot, 2) == 1

    def around(source, half, at, size):
        one_side, other_side = near[at : at + size, :], far[at : at + size, :]
        below = jnp.where(odd, one_side, other_side)
        above = jnp.where(odd, other_side, one_side)
        return jnp.concatenate([below, source[:, half], above], axis=0).astype(F32)

    def two(source, half, index):
        return around(source, half, index * 2 * plane, 2 * plane)

    def outside(field):
        return jnp.concatenate([field[0 : 2 * plane], field[2 * plane + cells :]], axis=0)

    def one(source, half, index):
        return around(source, half, (6 + index) * plane, plane)

    inside_low, inside_high = spot > 0, spot < lax.axis_size("space") - 1

    def store_masked(ref, value):
        blank = jnp.zeros((plane, width), BF16)
        ref[0:plane, :] = jnp.where(inside_low, value[0:plane], blank)
        ref[plane : plane + cells, :] = value[plane : plane + cells]
        ref[plane + cells : inner, :] = jnp.where(inside_high, value[plane + cells :], blank)

    core = slice(plane, plane + cells)
    copies.need("near", "far", "state")
    fill_shifts(stack, smooth_gate(outside(two(state, right, 0))), ydim, zdim)
    copies.need("first")
    f_one = (one(state, left, 0) + halo_sums(0, partial, stack, first, plane)).astype(BF16)
    new_one[...] = f_one[core]
    store_masked(mid, smooth_gate(f_one.astype(F32)).astype(BF16))

    made("new_one", "mid")

    copies.need("act")
    y_one = two(act, left, 1)
    half = half_erf(y_one)
    gated = y_one * half
    gate[...] = gated[plane : plane + inner].astype(BF16)
    fill_shifts(stack, outside(gated), ydim, zdim)
    copies.need("second")
    r_two = (one(act, right, 1) - halo_sums(1, partial, stack, second, plane)).astype(BF16)
    back_two[...] = r_two[core]
    store_masked(back, smooth_gate(r_two.astype(F32)).astype(BF16))

    made("gate", "back_two", "back")

    copies.need("grad")
    fill_shifts(stack, outside(two(grad, right, 2)), ydim, zdim)
    slope = gate_slope(y_one[plane : plane + inner], half[plane : plane + inner])
    copies.need("second_back")
    e_one = (one(grad, left, 2) + slope * halo_sums(2, partial, stack, second_back, plane)).astype(BF16)
    store_masked(carry, e_one)
    made("carry")


def second_kernel(ydim, zdim, copies, made, state, act, grad, new_one, back_two, mid, back, carry,
                  first, second, first_back, forward, rebuilt, passed, stack):
    plane = ydim * zdim
    cells, double = state.shape
    width = double // 2
    left, right = slice(0, width), slice(width, double)

    copies.need("back", "act", "back_two")
    fill_shifts(stack, back[...].astype(F32), ydim, zdim)
    rebuilt[:, right] = back_two[...]
    copies.need("first")
    rebuilt[:, left] = (
        act[:, left].astype(F32) - convolve(stack, first, cells, plane)
    ).astype(BF16)
    made("rebuilt")
    copies.need("carry", "grad")
    fill_shifts(stack, carry[...].astype(F32), ydim, zdim)
    passed[:, left] = carry[plane : plane + cells, :]
    r_two = back_two[...].astype(F32)
    copies.need("first_back")
    passed[:, right] = (
        grad[:, right].astype(F32)
        + gate_slope(r_two, half_erf(r_two)) * convolve(stack, first_back, cells, plane)
    ).astype(BF16)
    made("passed")
    copies.need("mid", "state", "new_one")
    fill_shifts(stack, mid[...].astype(F32), ydim, zdim)
    forward[:, left] = new_one[...]
    copies.need("second")
    forward[:, right] = (
        state[:, right].astype(F32) + convolve(stack, second, cells, plane)
    ).astype(BF16)
    made("forward")


def tick_kernel(ydim, zdim, paired, state, act, grad, near, far, first, second,
                first_back, second_back, partial, forward, sent, back, carry, gate, new_one, back_two, mid,
                rebuilt, stack):
    copies = Copies(None)
    ignore = lambda *names: None
    first_kernel(ydim, zdim, copies, ignore, state, act, grad, near, far, first, second,
                 second_back, partial, new_one, back_two, mid, back, carry, gate, stack)
    second_kernel(ydim, zdim, copies, ignore, state, act, grad, new_one, back_two, mid, back, carry,
                  first, second, first_back, forward, rebuilt, sent.at[1], stack)
    if paired:
        sent[0] = jnp.where(lax.axis_index("section") == 0, forward[...], rebuilt[...])
    else:
        sent[0] = rebuilt[...]


def correlate(stack, field, cotangent, ydim, zdim, emit):
    plane = ydim * zdim
    cells, width = cotangent.shape
    fill_shifts(stack, cotangent, ydim, zdim)
    for step in range(3):
        product = lax.dot_general(
            field[step * plane : step * plane + cells, :],
            stack[0:cells, :],
            (((0,), (0,)), ((), ())),
            preferred_element_type=F32,
        )
        for place in range(9):
            emit(9 * step + 8 - place, product[:, place * width : (place + 1) * width])


def both_grads(ydim, zdim, grad, back, carry, gate, stack, put):
    plane = ydim * zdim
    cells, double = grad.shape
    width = double // 2

    def store(which):
        return lambda k, block: put(which, slice(k * width, (k + 1) * width), block)

    own = carry[plane : plane + cells, :].astype(F32)
    correlate(stack, back, own, ydim, zdim, store(0))
    correlate(stack, gate, grad[:, width:].astype(F32), ydim, zdim, store(1))


def corr_kernel(ydim, zdim, grad, back, carry, gate, out, stack):
    def put(which, at, block):
        out[which, at, :] = block

    both_grads(ydim, zdim, grad, back, carry, gate, stack, put)


def ways_of(count, rows):
    bits = [1 << level for level in range(count.bit_length() - 1)]
    turning, last = bits[:-1], bits[-1:]
    ways = 3
    span = 2 * rows // ways
    orders = [turning[way % len(turning) :] + turning[: way % len(turning)] + last for way in range(ways)]
    return [(way * span, span, order) for way, order in enumerate(orders)]


def last_kernel(ydim, zdim, factor, count, direct, state, act, grad, near, far, first,
                second, first_back, second_back, partial, so_far, *args):
    n_outs = 6 if direct else 1
    results_out, args = args[:3], args[3:]
    final_outs, args = args[:n_outs], args[n_outs:]
    results, args = args[:3], args[3:]
    refs, args = args[:n_outs], args[n_outs:]
    new_one, back_two, mid, back, carry, gate, stack, sums, sems = args
    copies = Copies(sems)
    copies.start("so_far", so_far, sums)
    ignore = lambda *names: None
    first_kernel(ydim, zdim, copies, ignore, state, act, grad, near, far, first, second,
                 second_back, partial, new_one, back_two, mid, back, carry, gate, stack)
    copies.need("so_far")

    def put(which, at, block):
        sums[which, at, :] = (block + sums[which, at, :]) * factor

    both_grads(ydim, zdim, grad, back, carry, gate, stack, put)
    if not direct:
        refs[0][...] = sums[...].astype(BF16)
        copies.start("out", refs[0], final_outs[0])
    rows = sums.shape[1] // count
    for index, (start, span, order) in enumerate(ways_of(count, rows) if direct else ()):
        mine = lax.rem(lax.div(lax.axis_index("space"), order[0]), 2)
        for kept in (0, 1):
            side = mine if kept else 1 - mine
            out = refs[2 * index + (0 if kept else 1)]
            for j in range(count // 2):
                fixed = sum(
                    bit for level, bit in enumerate(order[1:]) if (j >> (len(order) - 2 - level)) & 1
                )
                block = fixed + side * order[0]
                pieces = []
                for which in range(2):
                    lower = max(start, which * rows)
                    upper = min(start + span, (which + 1) * rows)
                    if lower < upper:
                        at = pl.multiple_of(block * rows + (lower - which * rows), 8)
                        pieces.append(sums[which, pl.ds(at, upper - lower), :])
                value = pieces[0] if len(pieces) == 1 else jnp.concatenate(pieces, axis=0)
                out[j] = value.astype(BF16)
            at = 2 * index + (0 if kept else 1)
            copies.start(("half", at), out, final_outs[at])

    where = {"forward": 0, "rebuilt": 1, "passed": 2}

    def made(name):
        copies.start("out_" + name, results[where[name]], results_out[where[name]])

    second_kernel(ydim, zdim, copies, made, state, act, grad, new_one, back_two, mid, back, carry, first,
                  second, first_back, *results, stack)
    copies.finish()


def split_blocks(sums, count):
    blocks = jnp.concatenate([part.reshape(count, -1, part.shape[-1]) for part in sums], axis=1)
    spot = lax.axis_index("space")
    halves = []
    for start, span, order in ways_of(count, blocks.shape[1] // 2):
        part = blocks[:, start : start + span]
        part = part.reshape([2] * len(order) + list(part.shape[1:]))
        levels = [len(order) - bit.bit_length() for bit in order]
        part = jnp.transpose(part, levels + [len(order), len(order) + 1])
        part = part.reshape((2, count // 2) + part.shape[-2:])
        mine = (spot // order[0]) % 2
        for side in (mine, 1 - mine):
            halves.append(lax.dynamic_index_in_dim(part, side, 0, keepdims=False))
    return halves


def reduce_blocks(halves, count, rows):
    spot = lax.axis_index("space")
    ways = [
        (halves[2 * way], halves[2 * way + 1], order)
        for way, (_, _, order) in enumerate(ways_of(count, rows))
    ]
    def halved(total, bit):
        total = total.astype(BF16)
        total = total.reshape((2, total.shape[0] // 2) + total.shape[1:])
        mine = (spot // bit) % 2
        keep = lax.dynamic_index_in_dim(total, mine, 0, keepdims=False)
        return keep, lax.dynamic_index_in_dim(total, 1 - mine, 0, keepdims=False)

    def swapped(send, bit):
        return lax.ppermute(send, "space", [(i, i ^ bit) for i in range(count)]).astype(F32)

    depth = count.bit_length() - 1
    for step in range(depth - 1):
        later = []
        for keep, send, order in ways:
            total = keep.astype(F32) + swapped(send, order[step])
            later.append((*halved(total, order[step + 1]), order))
        ways = later
    keep = jnp.concatenate([keep[0] for keep, _, _ in ways], axis=0)
    send = jnp.concatenate([send[0] for _, send, _ in ways], axis=0)
    return keep.astype(F32) + swapped(send, ways[0][2][-1])


def shards(fwd_in, bwd_act, bwd_grad, fresh, target, w_first, w_second):
    width = w_first.shape[2]
    layers, ydim, zdim = fwd_in.shape[1:4]
    plane = ydim * zdim
    cells = layers * plane
    shape = fwd_in.shape[1:]
    flat = lambda block: block.reshape(cells, 2 * width)
    first = w_first[0].reshape(3, 9 * width, width)
    second = w_second[0].reshape(3, 9 * width, width)
    last_section = lax.axis_size("section") - 1
    place = lax.axis_index("section")
    count = lax.axis_size("space")
    beside = [(i, i ^ 1) for i in range(count) if i ^ 1 < count]
    across = [pair for i in range(1, count - 1, 2) for pair in ((i, i + 1), (i + 1, i))]
    array = jax.ShapeDtypeStruct
    edge = array((9 * plane, width), BF16)
    tile = array((cells, width), BF16)
    wide = array((cells + 2 * plane, width), BF16)
    state_shape = array((cells, 2 * width), BF16)
    offsets = 27 * width

    def exchange(near, far):
        far = lax.ppermute(far, "space", across)
        near = lax.ppermute(near, "space", beside)
        return near, far

    state, act, grad = flat(fwd_in), flat(bwd_act), flat(bwd_grad)
    hbm = pl.BlockSpec(memory_space=pltpu.HBM)
    outer_stack = array((cells + 4 * plane, 9 * width), BF16)
    small_stack = array((cells, 9 * width), BF16)
    weight = array((3, 9 * width, width), BF16)
    raw_weight = array((27, width, width), BF16)
    sums_shape = array((2, offsets, width), F32)

    vmem = pl.BlockSpec(memory_space=pltpu.VMEM)

    def call(kernel, name, inputs, outs, scratch, grant, copies=0, places=(vmem, vmem), flops=0,
             far=0):
        semaphores = [pltpu.SemaphoreType.DMA((copies,))] if copies else []
        return pl.pallas_call(
            kernel,
            out_shape=tuple(outs),
            in_specs=[places[0]] * (len(inputs) - far) + [hbm] * far,
            out_specs=(places[1],) * len(outs),
            scratch_shapes=[pltpu.VMEM(like.shape, like.dtype) for like in scratch] + semaphores,
            compiler_params=pltpu.CompilerParams(vmem_limit_bytes=grant),
            cost_estimate=pl.CostEstimate(
                flops=flops, bytes_accessed=sum(x.size * 2 for x in inputs), transcendentals=0
            ),
            name=name,
        )(*inputs)

    work = 2 * 27 * cells * width * width
    near, far = call(
        functools.partial(edges_kernel, plane), "edges", (state, act, grad), (edge,) * 2,
        (edge,) * 2, 65408 * 1024, 14, (hbm, hbm),
    )
    near, far = exchange(near, far)
    first_back, second_back, state, act, grad = call(
        flip_kernel, "flip", (w_first[0], w_second[0], state, act, grad),
        (raw_weight,) * 2 + (state_shape,) * 3, (), 16 * 1024 * 1024,
    )
    first_back, second_back = first_back.reshape(weight.shape), second_back.reshape(weight.shape)

    partial_shape = array((3, cells + 2 * plane, width), F32)

    def own(state, act, grad):
        (partial,) = call(
            functools.partial(own_kernel, ydim, zdim), "own_sums",
            (state, act, grad, first, second, second_back), (partial_shape,), (small_stack,),
            16 * 1024 * 1024, flops=2 * work,
        )
        return partial

    partial = own(state, act, grad)
    paired = last_section == 1
    pair_shape = array((2, cells, 2 * width), BF16)
    tick_outs = (state_shape, pair_shape, wide, wide, wide)
    forward, sent, back, carry, gate = call(
        functools.partial(tick_kernel, ydim, zdim, paired), "tick_one",
        (state, act, grad, near, far, first, second, first_back, second_back, partial), tick_outs,
        (tile, tile, wide, state_shape, outer_stack), 16 * 1024 * 1024, flops=8 * work,
    )
    if paired:
        lifted = lowered = lax.ppermute(sent, "section", [(0, 1), (1, 0)])
    else:
        lifted = lax.ppermute(forward[None], "section", [(s, s + 1) for s in range(last_section)])
        lowered = lax.ppermute(sent, "section", [(s + 1, s) for s in range(last_section)])

    join_outs = (state_shape,) * 3 + (edge, edge)
    state_two, act_two, grad_two, near, far = call(
        functools.partial(join_kernel, plane), "join",
        (forward, lifted, lowered, flat(fresh), flat(target)), join_outs,
        (), 16 * 1024 * 1024,
    )
    near, far = exchange(near, far)
    (so_far,) = call(
        functools.partial(corr_kernel, ydim, zdim), "weight_grads", (flat(bwd_grad), back, carry, gate),
        (sums_shape,), (small_stack,), 16 * 1024 * 1024, flops=2 * work,
    )

    partial = own(state_two, act_two, grad_two)
    rows = offsets // count
    direct = rows % 24 == 0
    if direct:
        span = 2 * rows // 3
        outs = (array((count // 2, span, width), BF16),) * 6
    else:
        outs = (array((2, offsets, width), BF16),)
    factor = 1.0 / math.sqrt(cells * count)
    results = (state_shape,) * 3
    made = call(
        functools.partial(last_kernel, ydim, zdim, factor, count, direct), "tick_two",
        (state_two, act_two, grad_two, near, far, first, second, first_back, second_back, partial,
         so_far),
        results + outs,
        results + outs + (tile, tile, wide, wide, wide, wide, outer_stack, sums_shape),
        48 * 1024 * 1024, 10, (vmem, hbm), 9 * work, 1,
    )
    forward, rebuilt, passed = made[:3]
    halves = made[3:] if direct else split_blocks(made[3], count)
    total = reduce_blocks(halves, count, rows)
    return (
        forward.reshape((1,) + shape),
        rebuilt.reshape((1,) + shape),
        passed.reshape((1,) + shape),
        total[:rows][None],
        total[rows:][None],
    )


def solution(mesh):
    placed = (
        P("section", "space", None, None, None),
        P("section", "space", None, None, None),
        P("section", "space", None, None, None),
        P("space", None, None, None),
        P("space", None, None, None),
        P("section", None, None, None),
        P("section", None, None, None),
    )
    return jax.shard_map(
        shards,
        mesh=mesh,
        in_specs=placed,
        out_specs=(
            P("section", "space", None, None, None),
            P("section", "space", None, None, None),
            P("section", "space", None, None, None),
            P("section", "space", None),
            P("section", "space", None),
        ),
        check_vma=False,
    )
```

```python
import functools
import math

import jax
import jax.numpy as jnp
from jax import lax
from jax.experimental import pallas as pl
from jax.experimental.pallas import tpu as pltpu
from jax.sharding import PartitionSpec as P

F32 = jnp.float32
BF16 = jnp.bfloat16


class Copies:
    def __init__(self, sems):
        self.sems, self.used, self.open = sems, 0, {}

    def start(self, name, source, target):
        copy = pltpu.make_async_copy(source, target, self.sems.at[self.used])
        self.used += 1
        copy.start()
        self.open[name] = copy

    def need(self, *names):
        for name in names:
            if name in self.open:
                self.open.pop(name).wait()

    def finish(self):
        self.need(*list(self.open))


def half_erf(value):
    return 0.5 * (1.0 + lax.erf(value * 0.7071067811865476))


def smooth_gate(value):
    return value * half_erf(value)


def gate_slope(value, half):
    return half + value * jnp.exp(-0.5 * value * value) * 0.3989422804014327


def fill_shifts(stack, field, ydim, zdim):
    rows, width = field.shape
    cells = field.reshape(rows // zdim, zdim, width)
    depth = lax.broadcasted_iota(jnp.int32, cells.shape, 1)
    before = jnp.where(depth == 0, 0.0, pltpu.roll(cells, 1, 1))
    after = jnp.where(depth == zdim - 1, 0.0, pltpu.roll(cells, zdim - 1, 1))
    for across, moved in enumerate((before, cells, after)):
        moved = moved.reshape(rows // (ydim * zdim), ydim, zdim, width)
        blank = jnp.zeros_like(moved[:, :1])
        shifted = (
            jnp.concatenate([blank, moved[:, :-1]], axis=1),
            moved,
            jnp.concatenate([moved[:, 1:], blank], axis=1),
        )
        for down in range(3):
            at = (3 * down + across) * width
            stack[0:rows, at : at + width] = shifted[down].reshape(rows, width).astype(BF16)


def convolve(stack, weights, rows, plane):
    total = None
    for step in range(3):
        part = jnp.dot(
            stack[step * plane : step * plane + rows, :],
            weights[step],
            preferred_element_type=F32,
        )
        total = part if total is None else total + part
    return total


def pack_edges(odd, state, act, grad, near, far, plane):
    width = state.shape[1] // 2
    cells = state.shape[0]
    left, right = slice(0, width), slice(width, 2 * width)

    def put(at, size, source, half):
        low = source[0:size, half]
        high = source[cells - size : cells, half]
        near[at : at + size, :] = jnp.where(odd, low, high)
        far[at : at + size, :] = jnp.where(odd, high, low)

    for index, (source, half) in enumerate(((state, right), (act, left), (grad, right))):
        put(index * 2 * plane, 2 * plane, source, half)
    for index, (source, half) in enumerate(((state, left), (act, right), (grad, left))):
        put((6 + index) * plane, plane, source, half)


def edges_kernel(plane, state, act, grad, near_out, far_out, near, far, sems):
    width = state.shape[1] // 2
    cells = state.shape[0]
    left, right = pl.ds(0, width), pl.ds(width, width)
    moves = []
    for index, (source, half) in enumerate(((state, right), (act, left), (grad, right))):
        moves.append((source, half, 2 * plane, index * 2 * plane))
    for index, (source, half) in enumerate(((state, left), (act, right), (grad, left))):
        moves.append((source, half, plane, (6 + index) * plane))
    copies = Copies(sems)
    odd = lax.rem(lax.axis_index("space"), 2)
    for side, (out, high) in enumerate(((near, 1 - odd), (far, odd))):
        for index, (source, half, size, at) in enumerate(moves):
            start = pl.multiple_of(high * (cells - size), plane)
            copies.start((side, index), source.at[pl.ds(start, size), half], out.at[pl.ds(at, size), :])
    for side, (out, result) in enumerate(((near, near_out), (far, far_out))):
        copies.need(*[(side, index) for index in range(len(moves))])
        copies.start(side, out, result)
    copies.finish()


def join_kernel(plane, forward, lifted, lowered, fresh, target, state, act, grad, near, far):
    place = lax.axis_index("section")
    first_place, last_place = place == 0, place == lax.axis_size("section") - 1
    state[...] = jnp.where(first_place, fresh[...], lifted[0])
    own = forward[...]
    act[...] = jnp.where(last_place, own, lowered[0])
    error = (own.astype(F32) - target[...].astype(F32)).astype(BF16)
    grad[...] = jnp.where(last_place, error, lowered[1])
    pack_edges(lax.rem(lax.axis_index("space"), 2) == 1, state, act, grad, near, far, plane)


def own_kernel(ydim, zdim, state, act, grad, first, second, second_back, partial, stack):
    own_sums(ydim, zdim, gated_fields(state, act, grad), (first, second, second_back), partial, stack)


def flip_kernel(first, second, state_in, act_in, grad_in, first_back, second_back, state, act, grad):
    state[...] = state_in[...]
    act[...] = act_in[...]
    grad[...] = grad_in[...]
    offsets = first.shape[0]
    for source, out in ((first, first_back), (second, second_back)):
        for k in range(offsets):
            out[offsets - 1 - k] = jnp.transpose(source[k])


def own_sums(ydim, zdim, fields, weights, partial, stack):
    plane = ydim * zdim
    for index, (field, weight) in enumerate(zip(fields, weights)):
        fill_shifts(stack, field, ydim, zdim)
        cells = field.shape[0]
        partial[index] = jnp.zeros(partial.shape[1:], F32)
        for step in range(3):
            at = (2 - step) * plane
            partial[index, at : at + cells, :] += jnp.dot(
                stack[0:cells, :], weight[step], preferred_element_type=F32
            )


def gated_fields(state, act, grad):
    width = state.shape[1] // 2
    return (
        smooth_gate(state[:, width:].astype(F32)),
        smooth_gate(act[:, :width].astype(F32)),
        grad[:, width:].astype(F32),
    )


def halo_sums(index, partial, stack, weights, plane):
    total = partial[index]
    inner = total.shape[0]
    low = jnp.dot(stack[0 : 2 * plane, :], weights[0], preferred_element_type=F32)
    both = jnp.dot(stack[plane : 3 * plane, :], weights[1], preferred_element_type=F32)
    high = jnp.dot(stack[2 * plane : 4 * plane, :], weights[2], preferred_element_type=F32)
    return jnp.concatenate(
        [
            total[0:plane] + low[0:plane] + both[0:plane],
            total[plane : 2 * plane] + low[plane:],
            total[2 * plane : inner - 2 * plane],
            total[inner - 2 * plane : inner - plane] + high[0:plane],
            total[inner - plane :] + high[plane:] + both[plane:],
        ],
        axis=0,
    )


def first_kernel(ydim, zdim, copies, made, state, act, grad, near, far, first, second, second_back, partial,
                 new_one, back_two, mid, back, carry, gate, stack):
    plane = ydim * zdim
    cells, double = state.shape
    width = double // 2
    inner = cells + 2 * plane
    outer = cells + 4 * plane
    left, right = slice(0, width), slice(width, double)

    spot = lax.axis_index("space")
    odd = lax.rem(spot, 2) == 1

    def around(source, half, at, size):
        one_side, other_side = near[at : at + size, :], far[at : at + size, :]
        below = jnp.where(odd, one_side, other_side)
        above = jnp.where(odd, other_side, one_side)
        return jnp.concatenate([below, source[:, half], above], axis=0).astype(F32)

    def two(source, half, index):
        return around(source, half, index * 2 * plane, 2 * plane)

    def outside(field):
        return jnp.concatenate([field[0 : 2 * plane], field[2 * plane + cells :]], axis=0)

    def one(source, half, index):
        return around(source, half, (6 + index) * plane, plane)

    inside_low, inside_high = spot > 0, spot < lax.axis_size("space") - 1

    def store_masked(ref, value):
        blank = jnp.zeros((plane, width), BF16)
        ref[0:plane, :] = jnp.where(inside_low, value[0:plane], blank)
        ref[plane : plane + cells, :] = value[plane : plane + cells]
        ref[plane + cells : inner, :] = jnp.where(inside_high, value[plane + cells :], blank)

    core = slice(plane, plane + cells)
    copies.need("near", "far", "state")
    fill_shifts(stack, smooth_gate(outside(two(state, right, 0))), ydim, zdim)
    copies.need("first")
    f_one = (one(state, left, 0) + halo_sums(0, partial, stack, first, plane)).astype(BF16)
    new_one[...] = f_one[core]
    store_masked(mid, smooth_gate(f_one.astype(F32)).astype(BF16))

    made("new_one", "mid")

    copies.need("act")
    y_one = two(act, left, 1)
    half = half_erf(y_one)
    gated = y_one * half
    gate[...] = gated[plane : plane + inner].astype(BF16)
    fill_shifts(stack, outside(gated), ydim, zdim)
    copies.need("second")
    r_two = (one(act, right, 1) - halo_sums(1, partial, stack, second, plane)).astype(BF16)
    back_two[...] = r_two[core]
    store_masked(back, smooth_gate(r_two.astype(F32)).astype(BF16))

    made("gate", "back_two", "back")

    copies.need("grad")
    fill_shifts(stack, outside(two(grad, right, 2)), ydim, zdim)
    slope = gate_slope(y_one[plane : plane + inner], half[plane : plane + inner])
    copies.need("second_back")
    e_one = (one(grad, left, 2) + slope * halo_sums(2, partial, stack, second_back, plane)).astype(BF16)
    store_masked(carry, e_one)
    made("carry")


def second_kernel(ydim, zdim, copies, made, state, act, grad, new_one, back_two, mid, back, carry,
                  first, second, first_back, forward, rebuilt, passed, stack):
    plane = ydim * zdim
    cells, double = state.shape
    width = double // 2
    left, right = slice(0, width), slice(width, double)

    copies.need("back", "act", "back_two")
    fill_shifts(stack, back[...].astype(F32), ydim, zdim)
    rebuilt[:, right] = back_two[...]
    copies.need("first")
    rebuilt[:, left] = (
        act[:, left].astype(F32) - convolve(stack, first, cells, plane)
    ).astype(BF16)
    made("rebuilt")
    copies.need("carry", "grad")
    fill_shifts(stack, carry[...].astype(F32), ydim, zdim)
    passed[:, left] = carry[plane : plane + cells, :]
    r_two = back_two[...].astype(F32)
    copies.need("first_back")
    passed[:, right] = (
        grad[:, right].astype(F32)
        + gate_slope(r_two, half_erf(r_two)) * convolve(stack, first_back, cells, plane)
    ).astype(BF16)
    made("passed")
    copies.need("mid", "state", "new_one")
    fill_shifts(stack, mid[...].astype(F32), ydim, zdim)
    forward[:, left] = new_one[...]
    copies.need("second")
    forward[:, right] = (
        state[:, right].astype(F32) + convolve(stack, second, cells, plane)
    ).astype(BF16)
    made("forward")


def tick_kernel(ydim, zdim, paired, state, act, grad, near, far, first, second,
                first_back, second_back, partial, forward, sent, back, carry, gate, new_one, back_two, mid,
                rebuilt, stack):
    copies = Copies(None)
    ignore = lambda *names: None
    first_kernel(ydim, zdim, copies, ignore, state, act, grad, near, far, first, second,
                 second_back, partial, new_one, back_two, mid, back, carry, gate, stack)
    second_kernel(ydim, zdim, copies, ignore, state, act, grad, new_one, back_two, mid, back, carry,
                  first, second, first_back, forward, rebuilt, sent.at[1], stack)
    if paired:
        sent[0] = jnp.where(lax.axis_index("section") == 0, forward[...], rebuilt[...])
    else:
        sent[0] = rebuilt[...]


def correlate(stack, field, cotangent, ydim, zdim, emit):
    plane = ydim * zdim
    cells, width = cotangent.shape
    fill_shifts(stack, cotangent, ydim, zdim)
    for step in range(3):
        product = lax.dot_general(
            field[step * plane : step * plane + cells, :],
            stack[0:cells, :],
            (((0,), (0,)), ((), ())),
            preferred_element_type=F32,
        )
        for place in range(9):
            emit(9 * step + 8 - place, product[:, place * width : (place + 1) * width])


def both_grads(ydim, zdim, grad, back, carry, gate, stack, put):
    plane = ydim * zdim
    cells, double = grad.shape
    width = double // 2

    def store(which):
        return lambda k, block: put(which, slice(k * width, (k + 1) * width), block)

    own = carry[plane : plane + cells, :].astype(F32)
    correlate(stack, back, own, ydim, zdim, store(0))
    correlate(stack, gate, grad[:, width:].astype(F32), ydim, zdim, store(1))


def corr_kernel(ydim, zdim, grad, back, carry, gate, out, stack):
    def put(which, at, block):
        out[which, at, :] = block

    both_grads(ydim, zdim, grad, back, carry, gate, stack, put)


def ways_of(count, rows):
    bits = [1 << level for level in range(count.bit_length() - 1)]
    turning, last = bits[:-1], bits[-1:]
    ways = 3
    span = 2 * rows // ways
    orders = [turning[way % len(turning) :] + turning[: way % len(turning)] + last for way in range(ways)]
    return [(way * span, span, order) for way, order in enumerate(orders)]


def last_kernel(ydim, zdim, factor, count, direct, state, act, grad, near, far, first,
                second, first_back, second_back, partial, so_far, *args):
    n_outs = 6 if direct else 1
    results_out, args = args[:3], args[3:]
    final_outs, args = args[:n_outs], args[n_outs:]
    results, args = args[:3], args[3:]
    refs, args = args[:n_outs], args[n_outs:]
    new_one, back_two, mid, back, carry, gate, stack, sums, sems = args
    copies = Copies(sems)
    ignore = lambda *names: None
    first_kernel(ydim, zdim, copies, ignore, state, act, grad, near, far, first, second,
                 second_back, partial, new_one, back_two, mid, back, carry, gate, stack)

    def put(which, at, block):
        sums[which, at, :] = (block + so_far[which, at, :]) * factor

    both_grads(ydim, zdim, grad, back, carry, gate, stack, put)
    if not direct:
        refs[0][...] = sums[...].astype(BF16)
        copies.start("out", refs[0], final_outs[0])
    rows = sums.shape[1] // count
    for index, (start, span, order) in enumerate(ways_of(count, rows) if direct else ()):
        mine = lax.rem(lax.div(lax.axis_index("space"), order[0]), 2)
        for kept in (0, 1):
            side = mine if kept else 1 - mine
            out = refs[2 * index + (0 if kept else 1)]
            for j in range(count // 2):
                fixed = sum(
                    bit for level, bit in enumerate(order[1:]) if (j >> (len(order) - 2 - level)) & 1
                )
                block = fixed + side * order[0]
                pieces = []
                for which in range(2):
                    lower = max(start, which * rows)
                    upper = min(start + span, (which + 1) * rows)
                    if lower < upper:
                        at = pl.multiple_of(block * rows + (lower - which * rows), 8)
                        pieces.append(sums[which, pl.ds(at, upper - lower), :])
                value = pieces[0] if len(pieces) == 1 else jnp.concatenate(pieces, axis=0)
                out[j] = value.astype(BF16)
            at = 2 * index + (0 if kept else 1)
            copies.start(("half", at), out, final_outs[at])

    where = {"forward": 0, "rebuilt": 1, "passed": 2}

    def made(name):
        copies.start("out_" + name, results[where[name]], results_out[where[name]])

    second_kernel(ydim, zdim, copies, made, state, act, grad, new_one, back_two, mid, back, carry, first,
                  second, first_back, *results, stack)
    copies.finish()


def split_blocks(sums, count):
    blocks = jnp.concatenate([part.reshape(count, -1, part.shape[-1]) for part in sums], axis=1)
    spot = lax.axis_index("space")
    halves = []
    for start, span, order in ways_of(count, blocks.shape[1] // 2):
        part = blocks[:, start : start + span]
        part = part.reshape([2] * len(order) + list(part.shape[1:]))
        levels = [len(order) - bit.bit_length() for bit in order]
        part = jnp.transpose(part, levels + [len(order), len(order) + 1])
        part = part.reshape((2, count // 2) + part.shape[-2:])
        mine = (spot // order[0]) % 2
        for side in (mine, 1 - mine):
            halves.append(lax.dynamic_index_in_dim(part, side, 0, keepdims=False))
    return halves


def reduce_blocks(halves, count, rows):
    spot = lax.axis_index("space")
    ways = [
        (halves[2 * way], halves[2 * way + 1], order)
        for way, (_, _, order) in enumerate(ways_of(count, rows))
    ]
    def halved(total, bit):
        total = total.astype(BF16)
        total = total.reshape((2, total.shape[0] // 2) + total.shape[1:])
        mine = (spot // bit) % 2
        keep = lax.dynamic_index_in_dim(total, mine, 0, keepdims=False)
        return keep, lax.dynamic_index_in_dim(total, 1 - mine, 0, keepdims=False)

    def swapped(send, bit):
        return lax.ppermute(send, "space", [(i, i ^ bit) for i in range(count)]).astype(F32)

    depth = count.bit_length() - 1
    for step in range(depth - 1):
        later = []
        for keep, send, order in ways:
            total = keep.astype(F32) + swapped(send, order[step])
            later.append((*halved(total, order[step + 1]), order))
        ways = later
    keep = jnp.concatenate([keep[0] for keep, _, _ in ways], axis=0)
    send = jnp.concatenate([send[0] for _, send, _ in ways], axis=0)
    return keep.astype(F32) + swapped(send, ways[0][2][-1])


def shards(fwd_in, bwd_act, bwd_grad, fresh, target, w_first, w_second):
    width = w_first.shape[2]
    layers, ydim, zdim = fwd_in.shape[1:4]
    plane = ydim * zdim
    cells = layers * plane
    shape = fwd_in.shape[1:]
    flat = lambda block: block.reshape(cells, 2 * width)
    first = w_first[0].reshape(3, 9 * width, width)
    second = w_second[0].reshape(3, 9 * width, width)
    last_section = lax.axis_size("section") - 1
    place = lax.axis_index("section")
    count = lax.axis_size("space")
    beside = [(i, i ^ 1) for i in range(count) if i ^ 1 < count]
    across = [pair for i in range(1, count - 1, 2) for pair in ((i, i + 1), (i + 1, i))]
    array = jax.ShapeDtypeStruct
    edge = array((9 * plane, width), BF16)
    tile = array((cells, width), BF16)
    wide = array((cells + 2 * plane, width), BF16)
    state_shape = array((cells, 2 * width), BF16)
    offsets = 27 * width

    def exchange(near, far):
        far = lax.ppermute(far, "space", across)
        near = lax.ppermute(near, "space", beside)
        return near, far

    state, act, grad = flat(fwd_in), flat(bwd_act), flat(bwd_grad)
    hbm = pl.BlockSpec(memory_space=pltpu.HBM)
    outer_stack = array((cells + 4 * plane, 9 * width), BF16)
    small_stack = array((cells, 9 * width), BF16)
    weight = array((3, 9 * width, width), BF16)
    raw_weight = array((27, width, width), BF16)
    sums_shape = array((2, offsets, width), F32)

    vmem = pl.BlockSpec(memory_space=pltpu.VMEM)

    def call(kernel, name, inputs, outs, scratch, grant, copies=0, places=(vmem, vmem), flops=0,
             far=0):
        semaphores = [pltpu.SemaphoreType.DMA((copies,))] if copies else []
        return pl.pallas_call(
            kernel,
            out_shape=tuple(outs),
            in_specs=[places[0]] * (len(inputs) - far) + [hbm] * far,
            out_specs=(places[1],) * len(outs),
            scratch_shapes=[pltpu.VMEM(like.shape, like.dtype) for like in scratch] + semaphores,
            compiler_params=pltpu.CompilerParams(vmem_limit_bytes=grant),
            cost_estimate=pl.CostEstimate(
                flops=flops, bytes_accessed=sum(x.size * 2 for x in inputs), transcendentals=0
            ),
            name=name,
        )(*inputs)

    work = 2 * 27 * cells * width * width
    near, far = call(
        functools.partial(edges_kernel, plane), "edges", (state, act, grad), (edge,) * 2,
        (edge,) * 2, 65408 * 1024, 14, (hbm, hbm),
    )
    near, far = exchange(near, far)
    first_back, second_back, state, act, grad = call(
        flip_kernel, "flip", (w_first[0], w_second[0], state, act, grad),
        (raw_weight,) * 2 + (state_shape,) * 3, (), 16 * 1024 * 1024,
    )
    first_back, second_back = first_back.reshape(weight.shape), second_back.reshape(weight.shape)

    partial_shape = array((3, cells + 2 * plane, width), F32)

    def own(state, act, grad):
        (partial,) = call(
            functools.partial(own_kernel, ydim, zdim), "own_sums",
            (state, act, grad, first, second, second_back), (partial_shape,), (small_stack,),
            16 * 1024 * 1024, flops=2 * work,
        )
        return partial

    partial = own(state, act, grad)
    paired = last_section == 1
    pair_shape = array((2, cells, 2 * width), BF16)
    tick_outs = (state_shape, pair_shape, wide, wide, wide)
    forward, sent, back, carry, gate = call(
        functools.partial(tick_kernel, ydim, zdim, paired), "tick_one",
        (state, act, grad, near, far, first, second, first_back, second_back, partial), tick_outs,
        (tile, tile, wide, state_shape, outer_stack), 16 * 1024 * 1024, flops=8 * work,
    )
    if paired:
        lifted = lowered = lax.ppermute(sent, "section", [(0, 1), (1, 0)])
    else:
        lifted = lax.ppermute(forward[None], "section", [(s, s + 1) for s in range(last_section)])
        lowered = lax.ppermute(sent, "section", [(s + 1, s) for s in range(last_section)])

    join_outs = (state_shape,) * 3 + (edge, edge)
    state_two, act_two, grad_two, near, far = call(
        functools.partial(join_kernel, plane), "join",
        (forward, lifted, lowered, flat(fresh), flat(target)), join_outs,
        (), 16 * 1024 * 1024,
    )
    near, far = exchange(near, far)
    (so_far,) = call(
        functools.partial(corr_kernel, ydim, zdim), "weight_grads", (flat(bwd_grad), back, carry, gate),
        (sums_shape,), (small_stack,), 16 * 1024 * 1024, flops=2 * work,
    )

    partial = own(state_two, act_two, grad_two)
    rows = offsets // count
    direct = rows % 24 == 0
    if direct:
        span = 2 * rows // 3
        outs = (array((count // 2, span, width), BF16),) * 6
    else:
        outs = (array((2, offsets, width), BF16),)
    factor = 1.0 / math.sqrt(cells * count)
    results = (state_shape,) * 3
    made = call(
        functools.partial(last_kernel, ydim, zdim, factor, count, direct), "tick_two",
        (state_two, act_two, grad_two, near, far, first, second, first_back, second_back, partial,
         so_far),
        results + outs,
        results + outs + (tile, tile, wide, wide, wide, wide, outer_stack, sums_shape),
        32 * 1024 * 1024, 10, (vmem, hbm), 9 * work,
    )
    forward, rebuilt, passed = made[:3]
    halves = made[3:] if direct else split_blocks(made[3], count)
    total = reduce_blocks(halves, count, rows)
    return (
        forward.reshape((1,) + shape),
        rebuilt.reshape((1,) + shape),
        passed.reshape((1,) + shape),
        total[:rows][None],
        total[rows:][None],
    )


def solution(mesh):
    placed = (
        P("section", "space", None, None, None),
        P("section", "space", None, None, None),
        P("section", "space", None, None, None),
        P("space", None, None, None),
        P("space", None, None, None),
        P("section", None, None, None),
        P("section", None, None, None),
    )
    return jax.shard_map(
        shards,
        mesh=mesh,
        in_specs=placed,
        out_specs=(
            P("section", "space", None, None, None),
            P("section", "space", None, None, None),
            P("section", "space", None, None, None),
            P("section", "space", None),
            P("section", "space", None),
        ),
        check_vma=False,
    )
```

```python
import functools
import math

import jax
import jax.numpy as jnp
from jax import lax
from jax.experimental import pallas as pl
from jax.experimental.pallas import tpu as pltpu
from jax.sharding import PartitionSpec as P

F32 = jnp.float32
BF16 = jnp.bfloat16


class Copies:
    def __init__(self, sems):
        self.sems, self.used, self.open = sems, 0, {}

    def start(self, name, source, target):
        copy = pltpu.make_async_copy(source, target, self.sems.at[self.used])
        self.used += 1
        copy.start()
        self.open[name] = copy

    def need(self, *names):
        for name in names:
            if name in self.open:
                self.open.pop(name).wait()

    def finish(self):
        self.need(*list(self.open))


def half_erf(value):
    return 0.5 * (1.0 + lax.erf(value * 0.7071067811865476))


def smooth_gate(value):
    return value * half_erf(value)


def gate_slope(value, half):
    return half + value * jnp.exp(-0.5 * value * value) * 0.3989422804014327


def fill_shifts(stack, field, ydim, zdim):
    rows, width = field.shape
    cells = field.reshape(rows // zdim, zdim, width)
    depth = lax.broadcasted_iota(jnp.int32, cells.shape, 1)
    before = jnp.where(depth == 0, 0.0, pltpu.roll(cells, 1, 1))
    after = jnp.where(depth == zdim - 1, 0.0, pltpu.roll(cells, zdim - 1, 1))
    for across, moved in enumerate((before, cells, after)):
        moved = moved.reshape(rows // (ydim * zdim), ydim, zdim, width)
        blank = jnp.zeros_like(moved[:, :1])
        shifted = (
            jnp.concatenate([blank, moved[:, :-1]], axis=1),
            moved,
            jnp.concatenate([moved[:, 1:], blank], axis=1),
        )
        for down in range(3):
            at = (3 * down + across) * width
            stack[0:rows, at : at + width] = shifted[down].reshape(rows, width).astype(BF16)


def convolve(stack, weights, rows, plane):
    total = None
    for step in range(3):
        part = jnp.dot(
            stack[step * plane : step * plane + rows, :],
            weights[step],
            preferred_element_type=F32,
        )
        total = part if total is None else total + part
    return total


def pack_edges(odd, state, act, grad, near, far, plane):
    width = state.shape[1] // 2
    cells = state.shape[0]
    left, right = slice(0, width), slice(width, 2 * width)

    def put(at, size, source, half):
        low = source[0:size, half]
        high = source[cells - size : cells, half]
        near[at : at + size, :] = jnp.where(odd, low, high)
        far[at : at + size, :] = jnp.where(odd, high, low)

    for index, (source, half) in enumerate(((state, right), (act, left), (grad, right))):
        put(index * 2 * plane, 2 * plane, source, half)
    for index, (source, half) in enumerate(((state, left), (act, right), (grad, left))):
        put((6 + index) * plane, plane, source, half)


def edges_kernel(plane, state, act, grad, near_out, far_out, fields_out, near, far, fields,
                 sems):
    width = state.shape[1] // 2
    cells = state.shape[0]
    left, right = pl.ds(0, width), pl.ds(width, width)
    moves = []
    for index, (source, half) in enumerate(((state, right), (act, left), (grad, right))):
        moves.append((source, half, 2 * plane, index * 2 * plane))
    for index, (source, half) in enumerate(((state, left), (act, right), (grad, left))):
        moves.append((source, half, plane, (6 + index) * plane))
    copies = Copies(sems)
    odd = lax.rem(lax.axis_index("space"), 2)
    for side, (out, high) in enumerate(((near, 1 - odd), (far, odd))):
        for index, (source, half, size, at) in enumerate(moves):
            start = pl.multiple_of(high * (cells - size), plane)
            copies.start((side, index), source.at[pl.ds(start, size), half], out.at[pl.ds(at, size), :])
    for index, source in enumerate((state, act, grad)):
        copies.start(("field", index), source, fields.at[index])
    for side, (out, result) in enumerate(((near, near_out), (far, far_out))):
        copies.need(*[(side, index) for index in range(len(moves))])
        copies.start(side, out, result)
    copies.need(*[("field", index) for index in range(3)])
    copies.start("fields", fields, fields_out)
    copies.finish()


def join_kernel(plane, forward, lifted, lowered, fresh, target, state, act, grad, near, far):
    place = lax.axis_index("section")
    first_place, last_place = place == 0, place == lax.axis_size("section") - 1
    state[...] = jnp.where(first_place, fresh[...], lifted[0])
    own = forward[...]
    act[...] = jnp.where(last_place, own, lowered[0])
    error = (own.astype(F32) - target[...].astype(F32)).astype(BF16)
    grad[...] = jnp.where(last_place, error, lowered[1])
    pack_edges(lax.rem(lax.axis_index("space"), 2) == 1, state, act, grad, near, far, plane)


def own_kernel(ydim, zdim, state, act, grad, first, second, second_back, partial, stack):
    own_sums(ydim, zdim, gated_fields(state, act, grad), (first, second, second_back), partial, stack)


def flip_kernel(first, second, fields, first_out, second_out, first_back, second_back, state, act, grad):
    for index, out in enumerate((state, act, grad)):
        out[...] = fields[index]
    first_out[...] = first[...]
    second_out[...] = second[...]
    offsets = first.shape[0]
    for source, out in ((first, first_back), (second, second_back)):
        for k in range(offsets):
            out[offsets - 1 - k] = jnp.transpose(source[k])


def own_sums(ydim, zdim, fields, weights, partial, stack):
    plane = ydim * zdim
    for index, (field, weight) in enumerate(zip(fields, weights)):
        fill_shifts(stack, field, ydim, zdim)
        cells = field.shape[0]
        partial[index] = jnp.zeros(partial.shape[1:], F32)
        for step in range(3):
            at = (2 - step) * plane
            partial[index, at : at + cells, :] += jnp.dot(
                stack[0:cells, :], weight[step], preferred_element_type=F32
            )


def gated_fields(state, act, grad):
    width = state.shape[1] // 2
    return (
        smooth_gate(state[:, width:].astype(F32)),
        smooth_gate(act[:, :width].astype(F32)),
        grad[:, width:].astype(F32),
    )


def halo_sums(index, partial, stack, weights, plane):
    total = partial[index]
    inner = total.shape[0]
    low = jnp.dot(stack[0 : 2 * plane, :], weights[0], preferred_element_type=F32)
    both = jnp.dot(stack[plane : 3 * plane, :], weights[1], preferred_element_type=F32)
    high = jnp.dot(stack[2 * plane : 4 * plane, :], weights[2], preferred_element_type=F32)
    return jnp.concatenate(
        [
            total[0:plane] + low[0:plane] + both[0:plane],
            total[plane : 2 * plane] + low[plane:],
            total[2 * plane : inner - 2 * plane],
            total[inner - 2 * plane : inner - plane] + high[0:plane],
            total[inner - plane :] + high[plane:] + both[plane:],
        ],
        axis=0,
    )


def first_kernel(ydim, zdim, copies, made, state, act, grad, near, far, first, second, second_back, partial,
                 new_one, back_two, mid, back, carry, gate, stack):
    plane = ydim * zdim
    cells, double = state.shape
    width = double // 2
    inner = cells + 2 * plane
    outer = cells + 4 * plane
    left, right = slice(0, width), slice(width, double)

    spot = lax.axis_index("space")
    odd = lax.rem(spot, 2) == 1

    def around(source, half, at, size):
        one_side, other_side = near[at : at + size, :], far[at : at + size, :]
        below = jnp.where(odd, one_side, other_side)
        above = jnp.where(odd, other_side, one_side)
        return jnp.concatenate([below, source[:, half], above], axis=0).astype(F32)

    def two(source, half, index):
        return around(source, half, index * 2 * plane, 2 * plane)

    def outside(field):
        return jnp.concatenate([field[0 : 2 * plane], field[2 * plane + cells :]], axis=0)

    def one(source, half, index):
        return around(source, half, (6 + index) * plane, plane)

    inside_low, inside_high = spot > 0, spot < lax.axis_size("space") - 1

    def store_masked(ref, value):
        blank = jnp.zeros((plane, width), BF16)
        ref[0:plane, :] = jnp.where(inside_low, value[0:plane], blank)
        ref[plane : plane + cells, :] = value[plane : plane + cells]
        ref[plane + cells : inner, :] = jnp.where(inside_high, value[plane + cells :], blank)

    core = slice(plane, plane + cells)
    copies.need("near", "far", "state")
    fill_shifts(stack, smooth_gate(outside(two(state, right, 0))), ydim, zdim)
    copies.need("first")
    f_one = (one(state, left, 0) + halo_sums(0, partial, stack, first, plane)).astype(BF16)
    new_one[...] = f_one[core]
    store_masked(mid, smooth_gate(f_one.astype(F32)).astype(BF16))

    made("new_one", "mid")

    copies.need("act")
    y_one = two(act, left, 1)
    half = half_erf(y_one)
    gated = y_one * half
    gate[...] = gated[plane : plane + inner].astype(BF16)
    fill_shifts(stack, outside(gated), ydim, zdim)
    copies.need("second")
    r_two = (one(act, right, 1) - halo_sums(1, partial, stack, second, plane)).astype(BF16)
    back_two[...] = r_two[core]
    store_masked(back, smooth_gate(r_two.astype(F32)).astype(BF16))

    made("gate", "back_two", "back")

    copies.need("grad")
    fill_shifts(stack, outside(two(grad, right, 2)), ydim, zdim)
    slope = gate_slope(y_one[plane : plane + inner], half[plane : plane + inner])
    copies.need("second_back")
    e_one = (one(grad, left, 2) + slope * halo_sums(2, partial, stack, second_back, plane)).astype(BF16)
    store_masked(carry, e_one)
    made("carry")


def second_kernel(ydim, zdim, copies, made, state, act, grad, new_one, back_two, mid, back, carry,
                  first, second, first_back, forward, rebuilt, passed, stack):
    plane = ydim * zdim
    cells, double = state.shape
    width = double // 2
    left, right = slice(0, width), slice(width, double)

    copies.need("back", "act", "back_two")
    fill_shifts(stack, back[...].astype(F32), ydim, zdim)
    rebuilt[:, right] = back_two[...]
    copies.need("first")
    rebuilt[:, left] = (
        act[:, left].astype(F32) - convolve(stack, first, cells, plane)
    ).astype(BF16)
    made("rebuilt")
    copies.need("carry", "grad")
    fill_shifts(stack, carry[...].astype(F32), ydim, zdim)
    passed[:, left] = carry[plane : plane + cells, :]
    r_two = back_two[...].astype(F32)
    copies.need("first_back")
    passed[:, right] = (
        grad[:, right].astype(F32)
        + gate_slope(r_two, half_erf(r_two)) * convolve(stack, first_back, cells, plane)
    ).astype(BF16)
    made("passed")
    copies.need("mid", "state", "new_one")
    fill_shifts(stack, mid[...].astype(F32), ydim, zdim)
    forward[:, left] = new_one[...]
    copies.need("second")
    forward[:, right] = (
        state[:, right].astype(F32) + convolve(stack, second, cells, plane)
    ).astype(BF16)
    made("forward")


def tick_kernel(ydim, zdim, paired, state, act, grad, far, near, first, second,
                first_back, second_back, partial, forward, sent, back, carry, gate, new_one, back_two, mid,
                rebuilt, stack):
    copies = Copies(None)
    ignore = lambda *names: None
    first_kernel(ydim, zdim, copies, ignore, state, act, grad, near, far, first, second,
                 second_back, partial, new_one, back_two, mid, back, carry, gate, stack)
    second_kernel(ydim, zdim, copies, ignore, state, act, grad, new_one, back_two, mid, back, carry,
                  first, second, first_back, forward, rebuilt, sent.at[1], stack)
    if paired:
        sent[0] = jnp.where(lax.axis_index("section") == 0, forward[...], rebuilt[...])
    else:
        sent[0] = rebuilt[...]


def correlate(stack, field, cotangent, ydim, zdim, emit):
    plane = ydim * zdim
    cells, width = cotangent.shape
    fill_shifts(stack, cotangent, ydim, zdim)
    for step in range(3):
        product = lax.dot_general(
            field[step * plane : step * plane + cells, :],
            stack[0:cells, :],
            (((0,), (0,)), ((), ())),
            preferred_element_type=F32,
        )
        for place in range(9):
            emit(9 * step + 8 - place, product[:, place * width : (place + 1) * width])


def both_grads(ydim, zdim, grad, back, carry, gate, stack, put):
    plane = ydim * zdim
    cells, double = grad.shape
    width = double // 2

    def store(which):
        return lambda k, block: put(which, slice(k * width, (k + 1) * width), block)

    own = carry[plane : plane + cells, :].astype(F32)
    correlate(stack, back, own, ydim, zdim, store(0))
    correlate(stack, gate, grad[:, width:].astype(F32), ydim, zdim, store(1))


def corr_kernel(ydim, zdim, grad, back, carry, gate, out, stack):
    def put(which, at, block):
        out[which, at, :] = block

    both_grads(ydim, zdim, grad, back, carry, gate, stack, put)


def ways_of(count, rows):
    bits = [1 << level for level in range(count.bit_length() - 1)]
    turning, last = bits[:-1], bits[-1:]
    ways = 3
    span = 2 * rows // ways
    orders = [turning[way % len(turning) :] + turning[: way % len(turning)] + last for way in range(ways)]
    return [(way * span, span, order) for way, order in enumerate(orders)]


def last_kernel(ydim, zdim, factor, count, direct, state, act, grad, far, near, first,
                second, first_back, second_back, partial, so_far, *args):
    n_outs = 6 if direct else 1
    results_out, args = args[:3], args[3:]
    final_outs, args = args[:n_outs], args[n_outs:]
    results, args = args[:3], args[3:]
    refs, args = args[:n_outs], args[n_outs:]
    new_one, back_two, mid, back, carry, gate, stack, sums, sems = args
    copies = Copies(sems)
    ignore = lambda *names: None
    first_kernel(ydim, zdim, copies, ignore, state, act, grad, near, far, first, second,
                 second_back, partial, new_one, back_two, mid, back, carry, gate, stack)

    def put(which, at, block):
        sums[which, at, :] = (block + so_far[which, at, :]) * factor

    both_grads(ydim, zdim, grad, back, carry, gate, stack, put)
    if not direct:
        refs[0][...] = sums[...].astype(BF16)
        copies.start("out", refs[0], final_outs[0])
    rows = sums.shape[1] // count
    for index, (start, span, order) in enumerate(ways_of(count, rows) if direct else ()):
        mine = lax.rem(lax.div(lax.axis_index("space"), order[0]), 2)
        for kept in (0, 1):
            side = mine if kept else 1 - mine
            out = refs[2 * index + (0 if kept else 1)]
            for j in range(count // 2):
                fixed = sum(
                    bit for level, bit in enumerate(order[1:]) if (j >> (len(order) - 2 - level)) & 1
                )
                block = fixed + side * order[0]
                pieces = []
                for which in range(2):
                    lower = max(start, which * rows)
                    upper = min(start + span, (which + 1) * rows)
                    if lower < upper:
                        at = pl.multiple_of(block * rows + (lower - which * rows), 8)
                        pieces.append(sums[which, pl.ds(at, upper - lower), :])
                value = pieces[0] if len(pieces) == 1 else jnp.concatenate(pieces, axis=0)
                out[j] = value.astype(BF16)
            at = 2 * index + (0 if kept else 1)
            copies.start(("half", at), out, final_outs[at])

    where = {"forward": 0, "rebuilt": 1, "passed": 2}

    def made(name):
        copies.start("out_" + name, results[where[name]], results_out[where[name]])

    second_kernel(ydim, zdim, copies, made, state, act, grad, new_one, back_two, mid, back, carry, first,
                  second, first_back, *results, stack)
    copies.finish()


def split_blocks(sums, count):
    blocks = jnp.concatenate([part.reshape(count, -1, part.shape[-1]) for part in sums], axis=1)
    spot = lax.axis_index("space")
    halves = []
    for start, span, order in ways_of(count, blocks.shape[1] // 2):
        part = blocks[:, start : start + span]
        part = part.reshape([2] * len(order) + list(part.shape[1:]))
        levels = [len(order) - bit.bit_length() for bit in order]
        part = jnp.transpose(part, levels + [len(order), len(order) + 1])
        part = part.reshape((2, count // 2) + part.shape[-2:])
        mine = (spot // order[0]) % 2
        for side in (mine, 1 - mine):
            halves.append(lax.dynamic_index_in_dim(part, side, 0, keepdims=False))
    return halves


def reduce_blocks(halves, count, rows):
    spot = lax.axis_index("space")
    ways = [
        (halves[2 * way], halves[2 * way + 1], order)
        for way, (_, _, order) in enumerate(ways_of(count, rows))
    ]
    def halved(total, bit):
        total = total.astype(BF16)
        total = total.reshape((2, total.shape[0] // 2) + total.shape[1:])
        mine = (spot // bit) % 2
        keep = lax.dynamic_index_in_dim(total, mine, 0, keepdims=False)
        return keep, lax.dynamic_index_in_dim(total, 1 - mine, 0, keepdims=False)

    def swapped(send, bit):
        return lax.ppermute(send, "space", [(i, i ^ bit) for i in range(count)]).astype(F32)

    depth = count.bit_length() - 1
    for step in range(depth - 1):
        later = []
        for keep, send, order in ways:
            total = keep.astype(F32) + swapped(send, order[step])
            later.append((*halved(total, order[step + 1]), order))
        ways = later
    keep = jnp.concatenate([keep[0] for keep, _, _ in ways], axis=0)
    send = jnp.concatenate([send[0] for _, send, _ in ways], axis=0)
    return keep.astype(F32) + swapped(send, ways[0][2][-1])


def shards(fwd_in, bwd_act, bwd_grad, fresh, target, w_first, w_second):
    width = w_first.shape[2]
    layers, ydim, zdim = fwd_in.shape[1:4]
    plane = ydim * zdim
    cells = layers * plane
    shape = fwd_in.shape[1:]
    flat = lambda block: block.reshape(cells, 2 * width)
    first = w_first[0].reshape(3, 9 * width, width)
    second = w_second[0].reshape(3, 9 * width, width)
    last_section = lax.axis_size("section") - 1
    place = lax.axis_index("section")
    count = lax.axis_size("space")
    beside = [(i, i ^ 1) for i in range(count) if i ^ 1 < count]
    across = [pair for i in range(1, count - 1, 2) for pair in ((i, i + 1), (i + 1, i))]
    array = jax.ShapeDtypeStruct
    edge = array((9 * plane, width), BF16)
    tile = array((cells, width), BF16)
    wide = array((cells + 2 * plane, width), BF16)
    state_shape = array((cells, 2 * width), BF16)
    offsets = 27 * width

    def exchange(near, far):
        far = lax.ppermute(far, "space", across)
        near = lax.ppermute(near, "space", beside)
        return near, far

    state, act, grad = flat(fwd_in), flat(bwd_act), flat(bwd_grad)
    hbm = pl.BlockSpec(memory_space=pltpu.HBM)
    outer_stack = array((cells + 4 * plane, 9 * width), BF16)
    small_stack = array((cells, 9 * width), BF16)
    weight = array((3, 9 * width, width), BF16)
    raw_weight = array((27, width, width), BF16)
    sums_shape = array((2, offsets, width), F32)

    vmem = pl.BlockSpec(memory_space=pltpu.VMEM)

    def call(kernel, name, inputs, outs, scratch, grant, copies=0, places=(vmem, vmem), flops=0,
             far=0):
        semaphores = [pltpu.SemaphoreType.DMA((copies,))] if copies else []
        return pl.pallas_call(
            kernel,
            out_shape=tuple(outs),
            in_specs=[places[0]] * (len(inputs) - far) + [hbm] * far,
            out_specs=(places[1],) * len(outs),
            scratch_shapes=[pltpu.VMEM(like.shape, like.dtype) for like in scratch] + semaphores,
            compiler_params=pltpu.CompilerParams(vmem_limit_bytes=grant),
            cost_estimate=pl.CostEstimate(
                flops=flops, bytes_accessed=sum(x.size * 2 for x in inputs), transcendentals=0
            ),
            name=name,
        )(*inputs)

    work = 2 * 27 * cells * width * width
    fields_shape = array((3, cells, 2 * width), BF16)
    near, far, fields = call(
        functools.partial(edges_kernel, plane), "edges", (state, act, grad), (edge, edge, fields_shape),
        (edge, edge, fields_shape), 65408 * 1024, 18, (hbm, hbm),
    )
    near, far = exchange(near, far)
    held = call(
        flip_kernel, "flip", (w_first[0], w_second[0], fields),
        (raw_weight,) * 4 + (state_shape,) * 3, (), 16 * 1024 * 1024,
    )
    first_held, second_held, first_back, second_back = (part.reshape(weight.shape) for part in held[:4])
    state, act, grad = held[4:]

    partial_shape = array((3, cells + 2 * plane, width), F32)

    def own(state, act, grad, first, second):
        (partial,) = call(
            functools.partial(own_kernel, ydim, zdim), "own_sums",
            (state, act, grad, first, second, second_back), (partial_shape,), (small_stack,),
            16 * 1024 * 1024, flops=2 * work,
        )
        return partial

    partial = own(state, act, grad, first_held, second_held)
    paired = last_section == 1
    pair_shape = array((2, cells, 2 * width), BF16)
    tick_outs = (state_shape, pair_shape, wide, wide, wide)
    forward, sent, back, carry, gate = call(
        functools.partial(tick_kernel, ydim, zdim, paired), "tick_one",
        (state, act, grad, far, near, first_held, second_held, first_back, second_back, partial),
        tick_outs,
        (tile, tile, wide, state_shape, outer_stack), 16 * 1024 * 1024, flops=8 * work,
    )
    if paired:
        lifted = lowered = lax.ppermute(sent, "section", [(0, 1), (1, 0)])
    else:
        lifted = lax.ppermute(forward[None], "section", [(s, s + 1) for s in range(last_section)])
        lowered = lax.ppermute(sent, "section", [(s + 1, s) for s in range(last_section)])

    join_outs = (state_shape,) * 3 + (edge, edge)
    state_two, act_two, grad_two, near, far = call(
        functools.partial(join_kernel, plane), "join",
        (forward, lifted, lowered, flat(fresh), flat(target)), join_outs,
        (), 16 * 1024 * 1024,
    )
    near, far = exchange(near, far)
    (so_far,) = call(
        functools.partial(corr_kernel, ydim, zdim), "weight_grads", (flat(bwd_grad), back, carry, gate),
        (sums_shape,), (small_stack,), 16 * 1024 * 1024, flops=2 * work,
    )

    partial = own(state_two, act_two, grad_two, first, second)
    rows = offsets // count
    direct = rows % 24 == 0
    if direct:
        span = 2 * rows // 3
        outs = (array((count // 2, span, width), BF16),) * 6
    else:
        outs = (array((2, offsets, width), BF16),)
    factor = 1.0 / math.sqrt(cells * count)
    results = (state_shape,) * 3
    made = call(
        functools.partial(last_kernel, ydim, zdim, factor, count, direct), "tick_two",
        (state_two, act_two, grad_two, far, near, first, second, first_back, second_back, partial,
         so_far),
        results + outs,
        results + outs + (tile, tile, wide, wide, wide, wide, outer_stack, sums_shape),
        32 * 1024 * 1024, 10, (vmem, hbm), 9 * work,
    )
    forward, rebuilt, passed = made[:3]
    halves = made[3:] if direct else split_blocks(made[3], count)
    total = reduce_blocks(halves, count, rows)
    return (
        forward.reshape((1,) + shape),
        rebuilt.reshape((1,) + shape),
        passed.reshape((1,) + shape),
        total[:rows][None],
        total[rows:][None],
    )


def solution(mesh):
    placed = (
        P("section", "space", None, None, None),
        P("section", "space", None, None, None),
        P("section", "space", None, None, None),
        P("space", None, None, None),
        P("space", None, None, None),
        P("section", None, None, None),
        P("section", None, None, None),
    )
    return jax.shard_map(
        shards,
        mesh=mesh,
        in_specs=placed,
        out_specs=(
            P("section", "space", None, None, None),
            P("section", "space", None, None, None),
            P("section", "space", None, None, None),
            P("section", "space", None),
            P("section", "space", None),
        ),
        check_vma=False,
    )
```

```python
import functools
import math

import jax
import jax.numpy as jnp
from jax import lax
from jax.experimental import pallas as pl
from jax.experimental.pallas import tpu as pltpu
from jax.sharding import PartitionSpec as P

F32 = jnp.float32
BF16 = jnp.bfloat16


class Copies:
    def __init__(self, sems):
        self.sems, self.used, self.open = sems, 0, {}

    def start(self, name, source, target):
        copy = pltpu.make_async_copy(source, target, self.sems.at[self.used])
        self.used += 1
        copy.start()
        self.open[name] = copy

    def need(self, *names):
        for name in names:
            if name in self.open:
                self.open.pop(name).wait()

    def finish(self):
        self.need(*list(self.open))


def half_erf(value):
    return 0.5 * (1.0 + lax.erf(value * 0.7071067811865476))


def smooth_gate(value):
    return value * half_erf(value)


def gate_slope(value, half):
    return half + value * jnp.exp(-0.5 * value * value) * 0.3989422804014327


def fill_shifts(stack, field, ydim, zdim):
    rows, width = field.shape
    cells = field.reshape(rows // zdim, zdim, width)
    depth = lax.broadcasted_iota(jnp.int32, cells.shape, 1)
    before = jnp.where(depth == 0, 0.0, pltpu.roll(cells, 1, 1))
    after = jnp.where(depth == zdim - 1, 0.0, pltpu.roll(cells, zdim - 1, 1))
    for across, moved in enumerate((before, cells, after)):
        moved = moved.reshape(rows // (ydim * zdim), ydim, zdim, width)
        blank = jnp.zeros_like(moved[:, :1])
        shifted = (
            jnp.concatenate([blank, moved[:, :-1]], axis=1),
            moved,
            jnp.concatenate([moved[:, 1:], blank], axis=1),
        )
        for down in range(3):
            at = (3 * down + across) * width
            stack[0:rows, at : at + width] = shifted[down].reshape(rows, width).astype(BF16)


def convolve(stack, weights, rows, plane):
    total = None
    for step in range(3):
        part = jnp.dot(
            stack[step * plane : step * plane + rows, :],
            weights[step],
            preferred_element_type=F32,
        )
        total = part if total is None else total + part
    return total


def pack_edges(odd, state, act, grad, near, far, plane):
    width = state.shape[1] // 2
    cells = state.shape[0]
    left, right = slice(0, width), slice(width, 2 * width)

    def put(at, size, source, half):
        low = source[0:size, half]
        high = source[cells - size : cells, half]
        near[at : at + size, :] = jnp.where(odd, low, high)
        far[at : at + size, :] = jnp.where(odd, high, low)

    for index, (source, half) in enumerate(((state, right), (act, left), (grad, right))):
        put(index * 2 * plane, 2 * plane, source, half)
    for index, (source, half) in enumerate(((state, left), (act, right), (grad, left))):
        put((6 + index) * plane, plane, source, half)


def edges_kernel(plane, state, act, grad, near_out, far_out, fields_out, near, far, fields,
                 sems):
    width = state.shape[1] // 2
    cells = state.shape[0]
    left, right = pl.ds(0, width), pl.ds(width, width)
    moves = []
    for index, (source, half) in enumerate(((state, right), (act, left), (grad, right))):
        moves.append((source, half, 2 * plane, index * 2 * plane))
    for index, (source, half) in enumerate(((state, left), (act, right), (grad, left))):
        moves.append((source, half, plane, (6 + index) * plane))
    copies = Copies(sems)
    odd = lax.rem(lax.axis_index("space"), 2)
    for side, (out, high) in enumerate(((near, 1 - odd), (far, odd))):
        for index, (source, half, size, at) in enumerate(moves):
            start = pl.multiple_of(high * (cells - size), plane)
            copies.start((side, index), source.at[pl.ds(start, size), half], out.at[pl.ds(at, size), :])
    for index, source in enumerate((state, act, grad)):
        copies.start(("field", index), source, fields.at[index])
    for side, (out, result) in enumerate(((near, near_out), (far, far_out))):
        copies.need(*[(side, index) for index in range(len(moves))])
        copies.start(side, out, result)
    copies.need(*[("field", index) for index in range(3)])
    copies.start("fields", fields, fields_out)
    copies.finish()


def join_kernel(plane, forward, lifted, lowered, fresh, target, state, act, grad, near, far):
    place = lax.axis_index("section")
    first_place, last_place = place == 0, place == lax.axis_size("section") - 1
    state[...] = jnp.where(first_place, fresh[...], lifted[0])
    own = forward[...]
    act[...] = jnp.where(last_place, own, lowered[0])
    error = (own.astype(F32) - target[...].astype(F32)).astype(BF16)
    grad[...] = jnp.where(last_place, error, lowered[1])
    pack_edges(lax.rem(lax.axis_index("space"), 2) == 1, state, act, grad, near, far, plane)


def own_kernel(ydim, zdim, state, act, grad, first, second, second_back, partial, stack):
    own_sums(ydim, zdim, gated_fields(state, act, grad), (first, second, second_back), partial, stack)


def flip_kernel(first, second, fields, first_out, second_out, first_back, second_back, state, act, grad):
    for index, out in enumerate((state, act, grad)):
        out[...] = fields[index]
    first_out[...] = first[...]
    second_out[...] = second[...]
    offsets = first.shape[0]
    for source, out in ((first, first_back), (second, second_back)):
        for k in range(offsets):
            out[offsets - 1 - k] = jnp.transpose(source[k])


def own_sums(ydim, zdim, fields, weights, partial, stack):
    plane = ydim * zdim
    for index, (field, weight) in enumerate(zip(fields, weights)):
        fill_shifts(stack, field, ydim, zdim)
        cells = field.shape[0]
        partial[index] = jnp.zeros(partial.shape[1:], F32)
        for step in range(3):
            at = (2 - step) * plane
            partial[index, at : at + cells, :] += jnp.dot(
                stack[0:cells, :], weight[step], preferred_element_type=F32
            )


def gated_fields(state, act, grad):
    width = state.shape[1] // 2
    return (
        smooth_gate(state[:, width:].astype(F32)),
        smooth_gate(act[:, :width].astype(F32)),
        grad[:, width:].astype(F32),
    )


def halo_sums(index, partial, stack, weights, plane):
    total = partial[index]
    inner = total.shape[0]
    low = jnp.dot(stack[0 : 2 * plane, :], weights[0], preferred_element_type=F32)
    both = jnp.dot(stack[plane : 3 * plane, :], weights[1], preferred_element_type=F32)
    high = jnp.dot(stack[2 * plane : 4 * plane, :], weights[2], preferred_element_type=F32)
    return jnp.concatenate(
        [
            total[0:plane] + low[0:plane] + both[0:plane],
            total[plane : 2 * plane] + low[plane:],
            total[2 * plane : inner - 2 * plane],
            total[inner - 2 * plane : inner - plane] + high[0:plane],
            total[inner - plane :] + high[plane:] + both[plane:],
        ],
        axis=0,
    )


def first_kernel(ydim, zdim, copies, made, state, act, grad, near, far, first, second, second_back, partial,
                 new_one, back_two, mid, back, carry, gate, stack):
    plane = ydim * zdim
    cells, double = state.shape
    width = double // 2
    inner = cells + 2 * plane
    outer = cells + 4 * plane
    left, right = slice(0, width), slice(width, double)

    spot = lax.axis_index("space")
    odd = lax.rem(spot, 2) == 1

    def around(source, half, at, size):
        one_side, other_side = near[at : at + size, :], far[at : at + size, :]
        below = jnp.where(odd, one_side, other_side)
        above = jnp.where(odd, other_side, one_side)
        return jnp.concatenate([below, source[:, half], above], axis=0).astype(F32)

    def two(source, half, index):
        return around(source, half, index * 2 * plane, 2 * plane)

    def outside(field):
        return jnp.concatenate([field[0 : 2 * plane], field[2 * plane + cells :]], axis=0)

    def one(source, half, index):
        return around(source, half, (6 + index) * plane, plane)

    inside_low, inside_high = spot > 0, spot < lax.axis_size("space") - 1

    def store_masked(ref, value):
        blank = jnp.zeros((plane, width), BF16)
        ref[0:plane, :] = jnp.where(inside_low, value[0:plane], blank)
        ref[plane : plane + cells, :] = value[plane : plane + cells]
        ref[plane + cells : inner, :] = jnp.where(inside_high, value[plane + cells :], blank)

    core = slice(plane, plane + cells)
    copies.need("near", "far", "state")
    fill_shifts(stack, smooth_gate(outside(two(state, right, 0))), ydim, zdim)
    copies.need("first")
    f_one = (one(state, left, 0) + halo_sums(0, partial, stack, first, plane)).astype(BF16)
    new_one[...] = f_one[core]
    store_masked(mid, smooth_gate(f_one.astype(F32)).astype(BF16))

    made("new_one", "mid")

    copies.need("act")
    y_one = two(act, left, 1)
    half = half_erf(y_one)
    gated = y_one * half
    gate[...] = gated[plane : plane + inner].astype(BF16)
    fill_shifts(stack, outside(gated), ydim, zdim)
    copies.need("second")
    r_two = (one(act, right, 1) - halo_sums(1, partial, stack, second, plane)).astype(BF16)
    back_two[...] = r_two[core]
    store_masked(back, smooth_gate(r_two.astype(F32)).astype(BF16))

    made("gate", "back_two", "back")

    copies.need("grad")
    fill_shifts(stack, outside(two(grad, right, 2)), ydim, zdim)
    slope = gate_slope(y_one[plane : plane + inner], half[plane : plane + inner])
    copies.need("second_back")
    e_one = (one(grad, left, 2) + slope * halo_sums(2, partial, stack, second_back, plane)).astype(BF16)
    store_masked(carry, e_one)
    made("carry")


def second_kernel(ydim, zdim, copies, made, state, act, grad, new_one, back_two, mid, back, carry,
                  first, second, first_back, forward, rebuilt, passed, stack):
    plane = ydim * zdim
    cells, double = state.shape
    width = double // 2
    left, right = slice(0, width), slice(width, double)

    copies.need("back", "act", "back_two")
    fill_shifts(stack, back[...].astype(F32), ydim, zdim)
    rebuilt[:, right] = back_two[...]
    copies.need("first")
    rebuilt[:, left] = (
        act[:, left].astype(F32) - convolve(stack, first, cells, plane)
    ).astype(BF16)
    made("rebuilt")
    copies.need("carry", "grad")
    fill_shifts(stack, carry[...].astype(F32), ydim, zdim)
    passed[:, left] = carry[plane : plane + cells, :]
    r_two = back_two[...].astype(F32)
    copies.need("first_back")
    passed[:, right] = (
        grad[:, right].astype(F32)
        + gate_slope(r_two, half_erf(r_two)) * convolve(stack, first_back, cells, plane)
    ).astype(BF16)
    made("passed")
    copies.need("mid", "state", "new_one")
    fill_shifts(stack, mid[...].astype(F32), ydim, zdim)
    forward[:, left] = new_one[...]
    copies.need("second")
    forward[:, right] = (
        state[:, right].astype(F32) + convolve(stack, second, cells, plane)
    ).astype(BF16)
    made("forward")


def tick_kernel(ydim, zdim, paired, state, act, grad, near, far, first, second,
                first_back, second_back, partial, forward, sent, back, carry, gate, new_one, back_two, mid,
                rebuilt, stack):
    copies = Copies(None)
    ignore = lambda *names: None
    first_kernel(ydim, zdim, copies, ignore, state, act, grad, near, far, first, second,
                 second_back, partial, new_one, back_two, mid, back, carry, gate, stack)
    second_kernel(ydim, zdim, copies, ignore, state, act, grad, new_one, back_two, mid, back, carry,
                  first, second, first_back, forward, rebuilt, sent.at[1], stack)
    if paired:
        sent[0] = jnp.where(lax.axis_index("section") == 0, forward[...], rebuilt[...])
    else:
        sent[0] = rebuilt[...]


def correlate(stack, field, cotangent, ydim, zdim, emit):
    plane = ydim * zdim
    cells, width = cotangent.shape
    fill_shifts(stack, cotangent, ydim, zdim)
    for step in range(3):
        product = lax.dot_general(
            field[step * plane : step * plane + cells, :],
            stack[0:cells, :],
            (((0,), (0,)), ((), ())),
            preferred_element_type=F32,
        )
        for place in range(9):
            emit(9 * step + 8 - place, product[:, place * width : (place + 1) * width])


def both_grads(ydim, zdim, grad, back, carry, gate, stack, put):
    plane = ydim * zdim
    cells, double = grad.shape
    width = double // 2

    def store(which):
        return lambda k, block: put(which, slice(k * width, (k + 1) * width), block)

    own = carry[plane : plane + cells, :].astype(F32)
    correlate(stack, back, own, ydim, zdim, store(0))
    correlate(stack, gate, grad[:, width:].astype(F32), ydim, zdim, store(1))


def corr_kernel(ydim, zdim, grad, back, carry, gate, out, stack):
    def put(which, at, block):
        out[which, at, :] = block

    both_grads(ydim, zdim, grad, back, carry, gate, stack, put)


def ways_of(count, rows):
    bits = [1 << level for level in range(count.bit_length() - 1)]
    turning, last = bits[:-1], bits[-1:]
    ways = 3
    span = 2 * rows // ways
    orders = [turning[way % len(turning) :] + turning[: way % len(turning)] + last for way in range(ways)]
    return [(way * span, span, order) for way, order in enumerate(orders)]


def last_kernel(ydim, zdim, factor, count, direct, state, act, grad, near, far, first,
                second, first_back, second_back, partial, so_far, *args):
    n_outs = 6 if direct else 1
    results_out, args = args[:3], args[3:]
    final_outs, args = args[:n_outs], args[n_outs:]
    results, args = args[:3], args[3:]
    refs, args = args[:n_outs], args[n_outs:]
    new_one, back_two, mid, back, carry, gate, stack, sums, sems = args
    copies = Copies(sems)
    ignore = lambda *names: None
    first_kernel(ydim, zdim, copies, ignore, state, act, grad, near, far, first, second,
                 second_back, partial, new_one, back_two, mid, back, carry, gate, stack)

    def put(which, at, block):
        sums[which, at, :] = (block + so_far[which, at, :]) * factor

    both_grads(ydim, zdim, grad, back, carry, gate, stack, put)
    if not direct:
        refs[0][...] = sums[...].astype(BF16)
        copies.start("out", refs[0], final_outs[0])
    rows = sums.shape[1] // count
    for index, (start, span, order) in enumerate(ways_of(count, rows) if direct else ()):
        mine = lax.rem(lax.div(lax.axis_index("space"), order[0]), 2)
        for kept in (0, 1):
            side = mine if kept else 1 - mine
            out = refs[2 * index + (0 if kept else 1)]
            for j in range(count // 2):
                fixed = sum(
                    bit for level, bit in enumerate(order[1:]) if (j >> (len(order) - 2 - level)) & 1
                )
                block = fixed + side * order[0]
                pieces = []
                for which in range(2):
                    lower = max(start, which * rows)
                    upper = min(start + span, (which + 1) * rows)
                    if lower < upper:
                        at = pl.multiple_of(block * rows + (lower - which * rows), 8)
                        pieces.append(sums[which, pl.ds(at, upper - lower), :])
                value = pieces[0] if len(pieces) == 1 else jnp.concatenate(pieces, axis=0)
                out[j] = value.astype(BF16)
            at = 2 * index + (0 if kept else 1)
            copies.start(("half", at), out, final_outs[at])

    where = {"forward": 0, "rebuilt": 1, "passed": 2}

    def made(name):
        copies.start("out_" + name, results[where[name]], results_out[where[name]])

    second_kernel(ydim, zdim, copies, made, state, act, grad, new_one, back_two, mid, back, carry, first,
                  second, first_back, *results, stack)
    copies.finish()


def split_blocks(sums, count):
    blocks = jnp.concatenate([part.reshape(count, -1, part.shape[-1]) for part in sums], axis=1)
    spot = lax.axis_index("space")
    halves = []
    for start, span, order in ways_of(count, blocks.shape[1] // 2):
        part = blocks[:, start : start + span]
        part = part.reshape([2] * len(order) + list(part.shape[1:]))
        levels = [len(order) - bit.bit_length() for bit in order]
        part = jnp.transpose(part, levels + [len(order), len(order) + 1])
        part = part.reshape((2, count // 2) + part.shape[-2:])
        mine = (spot // order[0]) % 2
        for side in (mine, 1 - mine):
            halves.append(lax.dynamic_index_in_dim(part, side, 0, keepdims=False))
    return halves


def reduce_blocks(halves, count, rows):
    spot = lax.axis_index("space")
    ways = [
        (halves[2 * way], halves[2 * way + 1], order)
        for way, (_, _, order) in enumerate(ways_of(count, rows))
    ]
    def halved(total, bit):
        total = total.astype(BF16)
        total = total.reshape((2, total.shape[0] // 2) + total.shape[1:])
        mine = (spot // bit) % 2
        keep = lax.dynamic_index_in_dim(total, mine, 0, keepdims=False)
        return keep, lax.dynamic_index_in_dim(total, 1 - mine, 0, keepdims=False)

    def swapped(send, bit):
        return lax.ppermute(send, "space", [(i, i ^ bit) for i in range(count)]).astype(F32)

    depth = count.bit_length() - 1
    for step in range(depth - 1):
        later = []
        for keep, send, order in ways:
            total = keep.astype(F32) + swapped(send, order[step])
            later.append((*halved(total, order[step + 1]), order))
        ways = later
    keep = jnp.concatenate([keep[0] for keep, _, _ in ways], axis=0)
    send = jnp.concatenate([send[0] for _, send, _ in ways], axis=0)
    return keep.astype(F32) + swapped(send, ways[0][2][-1])


def shards(fwd_in, bwd_act, bwd_grad, fresh, target, w_first, w_second):
    width = w_first.shape[2]
    layers, ydim, zdim = fwd_in.shape[1:4]
    plane = ydim * zdim
    cells = layers * plane
    shape = fwd_in.shape[1:]
    flat = lambda block: block.reshape(cells, 2 * width)
    first = w_first[0].reshape(3, 9 * width, width)
    second = w_second[0].reshape(3, 9 * width, width)
    last_section = lax.axis_size("section") - 1
    place = lax.axis_index("section")
    count = lax.axis_size("space")
    beside = [(i, i ^ 1) for i in range(count) if i ^ 1 < count]
    across = [pair for i in range(1, count - 1, 2) for pair in ((i, i + 1), (i + 1, i))]
    array = jax.ShapeDtypeStruct
    edge = array((9 * plane, width), BF16)
    tile = array((cells, width), BF16)
    wide = array((cells + 2 * plane, width), BF16)
    state_shape = array((cells, 2 * width), BF16)
    offsets = 27 * width

    def exchange(near, far):
        far = lax.ppermute(far, "space", across)
        near = lax.ppermute(near, "space", beside)
        return near, far

    state, act, grad = flat(fwd_in), flat(bwd_act), flat(bwd_grad)
    hbm = pl.BlockSpec(memory_space=pltpu.HBM)
    outer_stack = array((cells + 4 * plane, 9 * width), BF16)
    small_stack = array((cells, 9 * width), BF16)
    weight = array((3, 9 * width, width), BF16)
    raw_weight = array((27, width, width), BF16)
    sums_shape = array((2, offsets, width), F32)

    vmem = pl.BlockSpec(memory_space=pltpu.VMEM)

    def call(kernel, name, inputs, outs, scratch, grant, copies=0, places=(vmem, vmem), flops=0,
             far=0):
        semaphores = [pltpu.SemaphoreType.DMA((copies,))] if copies else []
        return pl.pallas_call(
            kernel,
            out_shape=tuple(outs),
            in_specs=[places[0]] * (len(inputs) - far) + [hbm] * far,
            out_specs=(places[1],) * len(outs),
            scratch_shapes=[pltpu.VMEM(like.shape, like.dtype) for like in scratch] + semaphores,
            compiler_params=pltpu.CompilerParams(vmem_limit_bytes=grant),
            cost_estimate=pl.CostEstimate(
                flops=flops, bytes_accessed=sum(x.size * 2 for x in inputs), transcendentals=0
            ),
            name=name,
        )(*inputs)

    work = 2 * 27 * cells * width * width
    fields_shape = array((3, cells, 2 * width), BF16)
    near, far, fields = call(
        functools.partial(edges_kernel, plane), "edges", (state, act, grad), (edge, edge, fields_shape),
        (edge, edge, fields_shape), 65408 * 1024, 18, (hbm, hbm),
    )
    near, far = exchange(near, far)
    held = call(
        flip_kernel, "flip", (w_first[0], w_second[0], fields),
        (raw_weight,) * 4 + (state_shape,) * 3, (), 16 * 1024 * 1024,
    )
    first_held, second_held, first_back, second_back = (part.reshape(weight.shape) for part in held[:4])
    state, act, grad = held[4:]

    partial_shape = array((3, cells + 2 * plane, width), F32)

    def own(state, act, grad, first, second):
        (partial,) = call(
            functools.partial(own_kernel, ydim, zdim), "own_sums",
            (state, act, grad, first, second, second_back), (partial_shape,), (small_stack,),
            16 * 1024 * 1024, flops=2 * work,
        )
        return partial

    partial = own(state, act, grad, first_held, second_held)
    paired = last_section == 1
    pair_shape = array((2, cells, 2 * width), BF16)
    tick_outs = (state_shape, pair_shape, wide, wide, wide)
    forward, sent, back, carry, gate = call(
        functools.partial(tick_kernel, ydim, zdim, paired), "tick_one",
        (state, act, grad, near, far, first_held, second_held, first_back, second_back, partial),
        tick_outs,
        (tile, tile, wide, state_shape, outer_stack), 16 * 1024 * 1024, flops=8 * work,
    )
    if paired:
        lifted = lowered = lax.ppermute(sent, "section", [(0, 1), (1, 0)])
    else:
        lifted = lax.ppermute(forward[None], "section", [(s, s + 1) for s in range(last_section)])
        lowered = lax.ppermute(sent, "section", [(s + 1, s) for s in range(last_section)])

    join_outs = (state_shape,) * 3 + (edge, edge)
    state_two, act_two, grad_two, near, far = call(
        functools.partial(join_kernel, plane), "join",
        (forward, lifted, lowered, flat(fresh), flat(target)), join_outs,
        (), 16 * 1024 * 1024,
    )
    near, far = exchange(near, far)
    (so_far,) = call(
        functools.partial(corr_kernel, ydim, zdim), "weight_grads", (flat(bwd_grad), back, carry, gate),
        (sums_shape,), (small_stack,), 16 * 1024 * 1024, flops=2 * work,
    )

    partial = own(state_two, act_two, grad_two, first, second)
    rows = offsets // count
    direct = rows % 24 == 0
    if direct:
        span = 2 * rows // 3
        outs = (array((count // 2, span, width), BF16),) * 6
    else:
        outs = (array((2, offsets, width), BF16),)
    factor = 1.0 / math.sqrt(cells * count)
    results = (state_shape,) * 3
    made = call(
        functools.partial(last_kernel, ydim, zdim, factor, count, direct), "tick_two",
        (state_two, act_two, grad_two, near, far, first, second, first_back, second_back, partial,
         so_far),
        results + outs,
        results + outs + (tile, tile, wide, wide, wide, wide, outer_stack, sums_shape),
        32 * 1024 * 1024, 10, (vmem, hbm), 9 * work,
    )
    forward, rebuilt, passed = made[:3]
    halves = made[3:] if direct else split_blocks(made[3], count)
    total = reduce_blocks(halves, count, rows)
    return (
        forward.reshape((1,) + shape),
        rebuilt.reshape((1,) + shape),
        passed.reshape((1,) + shape),
        total[:rows][None],
        total[rows:][None],
    )


def solution(mesh):
    placed = (
        P("section", "space", None, None, None),
        P("section", "space", None, None, None),
        P("section", "space", None, None, None),
        P("space", None, None, None),
        P("space", None, None, None),
        P("section", None, None, None),
        P("section", None, None, None),
    )
    return jax.shard_map(
        shards,
        mesh=mesh,
        in_specs=placed,
        out_specs=(
            P("section", "space", None, None, None),
            P("section", "space", None, None, None),
            P("section", "space", None, None, None),
            P("section", "space", None),
            P("section", "space", None),
        ),
        check_vma=False,
    )
```

```python
import functools
import math

import jax
import jax.numpy as jnp
from jax import lax
from jax.experimental import pallas as pl
from jax.experimental.pallas import tpu as pltpu
from jax.sharding import PartitionSpec as P

F32 = jnp.float32
BF16 = jnp.bfloat16


class Copies:
    def __init__(self, sems):
        self.sems, self.used, self.open = sems, 0, {}

    def start(self, name, source, target):
        copy = pltpu.make_async_copy(source, target, self.sems.at[self.used])
        self.used += 1
        copy.start()
        self.open[name] = copy

    def need(self, *names):
        for name in names:
            if name in self.open:
                self.open.pop(name).wait()

    def finish(self):
        self.need(*list(self.open))


def half_erf(value):
    return 0.5 * (1.0 + lax.erf(value * 0.7071067811865476))


def smooth_gate(value):
    return value * half_erf(value)


def gate_slope(value, half):
    return half + value * jnp.exp(-0.5 * value * value) * 0.3989422804014327


def fill_shifts(stack, field, ydim, zdim):
    rows, width = field.shape
    cells = field.reshape(rows // zdim, zdim, width)
    depth = lax.broadcasted_iota(jnp.int32, cells.shape, 1)
    before = jnp.where(depth == 0, 0.0, pltpu.roll(cells, 1, 1))
    after = jnp.where(depth == zdim - 1, 0.0, pltpu.roll(cells, zdim - 1, 1))
    for across, moved in enumerate((before, cells, after)):
        moved = moved.reshape(rows // (ydim * zdim), ydim, zdim, width)
        blank = jnp.zeros_like(moved[:, :1])
        shifted = (
            jnp.concatenate([blank, moved[:, :-1]], axis=1),
            moved,
            jnp.concatenate([moved[:, 1:], blank], axis=1),
        )
        for down in range(3):
            at = (3 * down + across) * width
            stack[0:rows, at : at + width] = shifted[down].reshape(rows, width).astype(BF16)


def convolve(stack, weights, rows, plane):
    total = None
    for step in range(3):
        part = jnp.dot(
            stack[step * plane : step * plane + rows, :],
            weights[step],
            preferred_element_type=F32,
        )
        total = part if total is None else total + part
    return total


def pack_edges(odd, state, act, grad, near, far, plane):
    width = state.shape[1] // 2
    cells = state.shape[0]
    left, right = slice(0, width), slice(width, 2 * width)

    def put(at, size, source, half):
        low = source[0:size, half]
        high = source[cells - size : cells, half]
        near[at : at + size, :] = jnp.where(odd, low, high)
        far[at : at + size, :] = jnp.where(odd, high, low)

    for index, (source, half) in enumerate(((state, right), (act, left), (grad, right))):
        put(index * 2 * plane, 2 * plane, source, half)
    for index, (source, half) in enumerate(((state, left), (act, right), (grad, left))):
        put((6 + index) * plane, plane, source, half)


def edges_kernel(plane, state, act, grad, near_out, far_out, fields_out, near, far, fields, sems):
    copies = Copies(sems)
    for index, source in enumerate((state, act, grad)):
        copies.start(index, source, fields.at[index])
    copies.finish()
    odd = lax.rem(lax.axis_index("space"), 2) == 1
    copies.start("fields", fields, fields_out)
    pack_edges(odd, fields.at[0], fields.at[1], fields.at[2], near, far, plane)
    copies.start("near", near, near_out)
    copies.start("far", far, far_out)
    copies.finish()


def join_kernel(plane, forward, lifted, lowered, fresh, target, state, act, grad, near, far):
    place = lax.axis_index("section")
    first_place, last_place = place == 0, place == lax.axis_size("section") - 1
    state[...] = jnp.where(first_place, fresh[...], lifted[0])
    own = forward[...]
    act[...] = jnp.where(last_place, own, lowered[0])
    error = (own.astype(F32) - target[...].astype(F32)).astype(BF16)
    grad[...] = jnp.where(last_place, error, lowered[1])
    pack_edges(lax.rem(lax.axis_index("space"), 2) == 1, state, act, grad, near, far, plane)


def own_kernel(ydim, zdim, state, act, grad, first, second, second_back, partial, stack):
    own_sums(ydim, zdim, gated_fields(state, act, grad), (first, second, second_back), partial, stack)


def flip_kernel(first, second, fields, first_out, second_out, first_back, second_back, state, act, grad):
    for index, out in enumerate((state, act, grad)):
        out[...] = fields[index]
    first_out[...] = first[...]
    second_out[...] = second[...]
    offsets = first.shape[0]
    for source, out in ((first, first_back), (second, second_back)):
        for k in range(offsets):
            out[offsets - 1 - k] = jnp.transpose(source[k])


def own_sums(ydim, zdim, fields, weights, partial, stack):
    plane = ydim * zdim
    for index, (field, weight) in enumerate(zip(fields, weights)):
        fill_shifts(stack, field, ydim, zdim)
        cells = field.shape[0]
        partial[index] = jnp.zeros(partial.shape[1:], F32)
        for step in range(3):
            at = (2 - step) * plane
            partial[index, at : at + cells, :] += jnp.dot(
                stack[0:cells, :], weight[step], preferred_element_type=F32
            )


def gated_fields(state, act, grad):
    width = state.shape[1] // 2
    return (
        smooth_gate(state[:, width:].astype(F32)),
        smooth_gate(act[:, :width].astype(F32)),
        grad[:, width:].astype(F32),
    )


def halo_sums(index, partial, stack, weights, plane):
    total = partial[index]
    inner = total.shape[0]
    low = jnp.dot(stack[0 : 2 * plane, :], weights[0], preferred_element_type=F32)
    both = jnp.dot(stack[plane : 3 * plane, :], weights[1], preferred_element_type=F32)
    high = jnp.dot(stack[2 * plane : 4 * plane, :], weights[2], preferred_element_type=F32)
    return jnp.concatenate(
        [
            total[0:plane] + low[0:plane] + both[0:plane],
            total[plane : 2 * plane] + low[plane:],
            total[2 * plane : inner - 2 * plane],
            total[inner - 2 * plane : inner - plane] + high[0:plane],
            total[inner - plane :] + high[plane:] + both[plane:],
        ],
        axis=0,
    )


def first_kernel(ydim, zdim, copies, made, state, act, grad, near, far, first, second, second_back, partial,
                 new_one, back_two, mid, back, carry, gate, stack):
    plane = ydim * zdim
    cells, double = state.shape
    width = double // 2
    inner = cells + 2 * plane
    outer = cells + 4 * plane
    left, right = slice(0, width), slice(width, double)

    spot = lax.axis_index("space")
    odd = lax.rem(spot, 2) == 1

    def around(source, half, at, size):
        one_side, other_side = near[at : at + size, :], far[at : at + size, :]
        below = jnp.where(odd, one_side, other_side)
        above = jnp.where(odd, other_side, one_side)
        return jnp.concatenate([below, source[:, half], above], axis=0).astype(F32)

    def two(source, half, index):
        return around(source, half, index * 2 * plane, 2 * plane)

    def outside(field):
        return jnp.concatenate([field[0 : 2 * plane], field[2 * plane + cells :]], axis=0)

    def one(source, half, index):
        return around(source, half, (6 + index) * plane, plane)

    inside_low, inside_high = spot > 0, spot < lax.axis_size("space") - 1

    def store_masked(ref, value):
        blank = jnp.zeros((plane, width), BF16)
        ref[0:plane, :] = jnp.where(inside_low, value[0:plane], blank)
        ref[plane : plane + cells, :] = value[plane : plane + cells]
        ref[plane + cells : inner, :] = jnp.where(inside_high, value[plane + cells :], blank)

    core = slice(plane, plane + cells)
    copies.need("near", "far", "state")
    fill_shifts(stack, smooth_gate(outside(two(state, right, 0))), ydim, zdim)
    copies.need("first")
    f_one = (one(state, left, 0) + halo_sums(0, partial, stack, first, plane)).astype(BF16)
    new_one[...] = f_one[core]
    store_masked(mid, smooth_gate(f_one.astype(F32)).astype(BF16))

    made("new_one", "mid")

    copies.need("act")
    y_one = two(act, left, 1)
    half = half_erf(y_one)
    gated = y_one * half
    gate[...] = gated[plane : plane + inner].astype(BF16)
    fill_shifts(stack, outside(gated), ydim, zdim)
    copies.need("second")
    r_two = (one(act, right, 1) - halo_sums(1, partial, stack, second, plane)).astype(BF16)
    back_two[...] = r_two[core]
    store_masked(back, smooth_gate(r_two.astype(F32)).astype(BF16))

    made("gate", "back_two", "back")

    copies.need("grad")
    fill_shifts(stack, outside(two(grad, right, 2)), ydim, zdim)
    slope = gate_slope(y_one[plane : plane + inner], half[plane : plane + inner])
    copies.need("second_back")
    e_one = (one(grad, left, 2) + slope * halo_sums(2, partial, stack, second_back, plane)).astype(BF16)
    store_masked(carry, e_one)
    made("carry")


def second_kernel(ydim, zdim, copies, made, state, act, grad, new_one, back_two, mid, back, carry,
                  first, second, first_back, forward, rebuilt, passed, stack):
    plane = ydim * zdim
    cells, double = state.shape
    width = double // 2
    left, right = slice(0, width), slice(width, double)

    copies.need("back", "act", "back_two")
    fill_shifts(stack, back[...].astype(F32), ydim, zdim)
    rebuilt[:, right] = back_two[...]
    copies.need("first")
    rebuilt[:, left] = (
        act[:, left].astype(F32) - convolve(stack, first, cells, plane)
    ).astype(BF16)
    made("rebuilt")
    copies.need("carry", "grad")
    fill_shifts(stack, carry[...].astype(F32), ydim, zdim)
    passed[:, left] = carry[plane : plane + cells, :]
    r_two = back_two[...].astype(F32)
    copies.need("first_back")
    passed[:, right] = (
        grad[:, right].astype(F32)
        + gate_slope(r_two, half_erf(r_two)) * convolve(stack, first_back, cells, plane)
    ).astype(BF16)
    made("passed")
    copies.need("mid", "state", "new_one")
    fill_shifts(stack, mid[...].astype(F32), ydim, zdim)
    forward[:, left] = new_one[...]
    copies.need("second")
    forward[:, right] = (
        state[:, right].astype(F32) + convolve(stack, second, cells, plane)
    ).astype(BF16)
    made("forward")


def tick_kernel(ydim, zdim, paired, state, act, grad, near, far, first, second,
                first_back, second_back, partial, forward, sent, back, carry, gate, new_one, back_two, mid,
                rebuilt, stack):
    copies = Copies(None)
    ignore = lambda *names: None
    first_kernel(ydim, zdim, copies, ignore, state, act, grad, near, far, first, second,
                 second_back, partial, new_one, back_two, mid, back, carry, gate, stack)
    second_kernel(ydim, zdim, copies, ignore, state, act, grad, new_one, back_two, mid, back, carry,
                  first, second, first_back, forward, rebuilt, sent.at[1], stack)
    if paired:
        sent[0] = jnp.where(lax.axis_index("section") == 0, forward[...], rebuilt[...])
    else:
        sent[0] = rebuilt[...]


def correlate(stack, field, cotangent, ydim, zdim, emit):
    plane = ydim * zdim
    cells, width = cotangent.shape
    fill_shifts(stack, cotangent, ydim, zdim)
    for step in range(3):
        product = lax.dot_general(
            field[step * plane : step * plane + cells, :],
            stack[0:cells, :],
            (((0,), (0,)), ((), ())),
            preferred_element_type=F32,
        )
        for place in range(9):
            emit(9 * step + 8 - place, product[:, place * width : (place + 1) * width])


def both_grads(ydim, zdim, grad, back, carry, gate, stack, put):
    plane = ydim * zdim
    cells, double = grad.shape
    width = double // 2

    def store(which):
        return lambda k, block: put(which, slice(k * width, (k + 1) * width), block)

    own = carry[plane : plane + cells, :].astype(F32)
    correlate(stack, back, own, ydim, zdim, store(0))
    correlate(stack, gate, grad[:, width:].astype(F32), ydim, zdim, store(1))


def corr_kernel(ydim, zdim, grad, back, carry, gate, out, stack):
    def put(which, at, block):
        out[which, at, :] = block

    both_grads(ydim, zdim, grad, back, carry, gate, stack, put)


def ways_of(count, rows):
    bits = [1 << level for level in range(count.bit_length() - 1)]
    turning, last = bits[:-1], bits[-1:]
    ways = 3
    span = 2 * rows // ways
    orders = [turning[way % len(turning) :] + turning[: way % len(turning)] + last for way in range(ways)]
    return [(way * span, span, order) for way, order in enumerate(orders)]


def last_kernel(ydim, zdim, factor, count, direct, state, act, grad, near, far, first,
                second, first_back, second_back, partial, so_far, *args):
    n_outs = 6 if direct else 1
    results_out, args = args[:3], args[3:]
    final_outs, args = args[:n_outs], args[n_outs:]
    results, args = args[:3], args[3:]
    refs, args = args[:n_outs], args[n_outs:]
    new_one, back_two, mid, back, carry, gate, stack, sums, sems = args
    copies = Copies(sems)
    ignore = lambda *names: None
    first_kernel(ydim, zdim, copies, ignore, state, act, grad, near, far, first, second,
                 second_back, partial, new_one, back_two, mid, back, carry, gate, stack)

    def put(which, at, block):
        sums[which, at, :] = (block + so_far[which, at, :]) * factor

    both_grads(ydim, zdim, grad, back, carry, gate, stack, put)
    if not direct:
        refs[0][...] = sums[...].astype(BF16)
        copies.start("out", refs[0], final_outs[0])
    rows = sums.shape[1] // count
    for index, (start, span, order) in enumerate(ways_of(count, rows) if direct else ()):
        mine = lax.rem(lax.div(lax.axis_index("space"), order[0]), 2)
        for kept in (0, 1):
            side = mine if kept else 1 - mine
            out = refs[2 * index + (0 if kept else 1)]
            for j in range(count // 2):
                fixed = sum(
                    bit for level, bit in enumerate(order[1:]) if (j >> (len(order) - 2 - level)) & 1
                )
                block = fixed + side * order[0]
                pieces = []
                for which in range(2):
                    lower = max(start, which * rows)
                    upper = min(start + span, (which + 1) * rows)
                    if lower < upper:
                        at = pl.multiple_of(block * rows + (lower - which * rows), 8)
                        pieces.append(sums[which, pl.ds(at, upper - lower), :])
                value = pieces[0] if len(pieces) == 1 else jnp.concatenate(pieces, axis=0)
                out[j] = value.astype(BF16)
            at = 2 * index + (0 if kept else 1)
            copies.start(("half", at), out, final_outs[at])

    where = {"forward": 0, "rebuilt": 1, "passed": 2}

    def made(name):
        copies.start("out_" + name, results[where[name]], results_out[where[name]])

    second_kernel(ydim, zdim, copies, made, state, act, grad, new_one, back_two, mid, back, carry, first,
                  second, first_back, *results, stack)
    copies.finish()


def split_blocks(sums, count):
    blocks = jnp.concatenate([part.reshape(count, -1, part.shape[-1]) for part in sums], axis=1)
    spot = lax.axis_index("space")
    halves = []
    for start, span, order in ways_of(count, blocks.shape[1] // 2):
        part = blocks[:, start : start + span]
        part = part.reshape([2] * len(order) + list(part.shape[1:]))
        levels = [len(order) - bit.bit_length() for bit in order]
        part = jnp.transpose(part, levels + [len(order), len(order) + 1])
        part = part.reshape((2, count // 2) + part.shape[-2:])
        mine = (spot // order[0]) % 2
        for side in (mine, 1 - mine):
            halves.append(lax.dynamic_index_in_dim(part, side, 0, keepdims=False))
    return halves


def reduce_blocks(halves, count, rows):
    spot = lax.axis_index("space")
    ways = [
        (halves[2 * way], halves[2 * way + 1], order)
        for way, (_, _, order) in enumerate(ways_of(count, rows))
    ]
    def halved(total, bit):
        total = total.astype(BF16)
        total = total.reshape((2, total.shape[0] // 2) + total.shape[1:])
        mine = (spot // bit) % 2
        keep = lax.dynamic_index_in_dim(total, mine, 0, keepdims=False)
        return keep, lax.dynamic_index_in_dim(total, 1 - mine, 0, keepdims=False)

    def swapped(send, bit):
        return lax.ppermute(send, "space", [(i, i ^ bit) for i in range(count)]).astype(F32)

    depth = count.bit_length() - 1
    for step in range(depth - 1):
        later = []
        for keep, send, order in ways:
            total = keep.astype(F32) + swapped(send, order[step])
            later.append((*halved(total, order[step + 1]), order))
        ways = later
    keep = jnp.concatenate([keep[0] for keep, _, _ in ways], axis=0)
    send = jnp.concatenate([send[0] for _, send, _ in ways], axis=0)
    return keep.astype(F32) + swapped(send, ways[0][2][-1])


def shards(fwd_in, bwd_act, bwd_grad, fresh, target, w_first, w_second):
    width = w_first.shape[2]
    layers, ydim, zdim = fwd_in.shape[1:4]
    plane = ydim * zdim
    cells = layers * plane
    shape = fwd_in.shape[1:]
    flat = lambda block: block.reshape(cells, 2 * width)
    first = w_first[0].reshape(3, 9 * width, width)
    second = w_second[0].reshape(3, 9 * width, width)
    last_section = lax.axis_size("section") - 1
    place = lax.axis_index("section")
    count = lax.axis_size("space")
    beside = [(i, i ^ 1) for i in range(count) if i ^ 1 < count]
    across = [pair for i in range(1, count - 1, 2) for pair in ((i, i + 1), (i + 1, i))]
    array = jax.ShapeDtypeStruct
    edge = array((9 * plane, width), BF16)
    tile = array((cells, width), BF16)
    wide = array((cells + 2 * plane, width), BF16)
    state_shape = array((cells, 2 * width), BF16)
    offsets = 27 * width

    def exchange(near, far):
        far = lax.ppermute(far, "space", across)
        near = lax.ppermute(near, "space", beside)
        return near, far

    state, act, grad = flat(fwd_in), flat(bwd_act), flat(bwd_grad)
    hbm = pl.BlockSpec(memory_space=pltpu.HBM)
    outer_stack = array((cells + 4 * plane, 9 * width), BF16)
    small_stack = array((cells, 9 * width), BF16)
    weight = array((3, 9 * width, width), BF16)
    raw_weight = array((27, width, width), BF16)
    sums_shape = array((2, offsets, width), F32)

    vmem = pl.BlockSpec(memory_space=pltpu.VMEM)

    def call(kernel, name, inputs, outs, scratch, grant, copies=0, places=(vmem, vmem), flops=0,
             far=0):
        semaphores = [pltpu.SemaphoreType.DMA((copies,))] if copies else []
        return pl.pallas_call(
            kernel,
            out_shape=tuple(outs),
            in_specs=[places[0]] * (len(inputs) - far) + [hbm] * far,
            out_specs=(places[1],) * len(outs),
            scratch_shapes=[pltpu.VMEM(like.shape, like.dtype) for like in scratch] + semaphores,
            compiler_params=pltpu.CompilerParams(vmem_limit_bytes=grant),
            cost_estimate=pl.CostEstimate(
                flops=flops, bytes_accessed=sum(x.size * 2 for x in inputs), transcendentals=0
            ),
            name=name,
        )(*inputs)

    work = 2 * 27 * cells * width * width
    fields_shape = array((3, cells, 2 * width), BF16)
    near, far, fields = call(
        functools.partial(edges_kernel, plane), "edges", (state, act, grad), (edge, edge, fields_shape),
        (edge, edge, fields_shape), 65408 * 1024, 6, (hbm, hbm),
    )
    near, far = exchange(near, far)
    held = call(
        flip_kernel, "flip", (w_first[0], w_second[0], fields),
        (raw_weight,) * 4 + (state_shape,) * 3, (), 16 * 1024 * 1024,
    )
    first_held, second_held, first_back, second_back = (part.reshape(weight.shape) for part in held[:4])
    state, act, grad = held[4:]

    partial_shape = array((3, cells + 2 * plane, width), F32)

    def own(state, act, grad, first, second):
        (partial,) = call(
            functools.partial(own_kernel, ydim, zdim), "own_sums",
            (state, act, grad, first, second, second_back), (partial_shape,), (small_stack,),
            16 * 1024 * 1024, flops=2 * work,
        )
        return partial

    partial = own(state, act, grad, first_held, second_held)
    paired = last_section == 1
    pair_shape = array((2, cells, 2 * width), BF16)
    tick_outs = (state_shape, pair_shape, wide, wide, wide)
    forward, sent, back, carry, gate = call(
        functools.partial(tick_kernel, ydim, zdim, paired), "tick_one",
        (state, act, grad, near, far, first_held, second_held, first_back, second_back, partial),
        tick_outs,
        (tile, tile, wide, state_shape, outer_stack), 16 * 1024 * 1024, flops=8 * work,
    )
    if paired:
        lifted = lowered = lax.ppermute(sent, "section", [(0, 1), (1, 0)])
    else:
        lifted = lax.ppermute(forward[None], "section", [(s, s + 1) for s in range(last_section)])
        lowered = lax.ppermute(sent, "section", [(s + 1, s) for s in range(last_section)])

    join_outs = (state_shape,) * 3 + (edge, edge)
    state_two, act_two, grad_two, near, far = call(
        functools.partial(join_kernel, plane), "join",
        (forward, lifted, lowered, flat(fresh), flat(target)), join_outs,
        (), 16 * 1024 * 1024,
    )
    near, far = exchange(near, far)
    (so_far,) = call(
        functools.partial(corr_kernel, ydim, zdim), "weight_grads", (flat(bwd_grad), back, carry, gate),
        (sums_shape,), (small_stack,), 16 * 1024 * 1024, flops=2 * work,
    )

    partial = own(state_two, act_two, grad_two, first, second)
    rows = offsets // count
    direct = rows % 24 == 0
    if direct:
        span = 2 * rows // 3
        outs = (array((count // 2, span, width), BF16),) * 6
    else:
        outs = (array((2, offsets, width), BF16),)
    factor = 1.0 / math.sqrt(cells * count)
    results = (state_shape,) * 3
    made = call(
        functools.partial(last_kernel, ydim, zdim, factor, count, direct), "tick_two",
        (state_two, act_two, grad_two, near, far, first, second, first_back, second_back, partial,
         so_far),
        results + outs,
        results + outs + (tile, tile, wide, wide, wide, wide, outer_stack, sums_shape),
        32 * 1024 * 1024, 10, (vmem, hbm), 9 * work,
    )
    forward, rebuilt, passed = made[:3]
    halves = made[3:] if direct else split_blocks(made[3], count)
    total = reduce_blocks(halves, count, rows)
    return (
        forward.reshape((1,) + shape),
        rebuilt.reshape((1,) + shape),
        passed.reshape((1,) + shape),
        total[:rows][None],
        total[rows:][None],
    )


def solution(mesh):
    placed = (
        P("section", "space", None, None, None),
        P("section", "space", None, None, None),
        P("section", "space", None, None, None),
        P("space", None, None, None),
        P("space", None, None, None),
        P("section", None, None, None),
        P("section", None, None, None),
    )
    return jax.shard_map(
        shards,
        mesh=mesh,
        in_specs=placed,
        out_specs=(
            P("section", "space", None, None, None),
            P("section", "space", None, None, None),
            P("section", "space", None, None, None),
            P("section", "space", None),
            P("section", "space", None),
        ),
        check_vma=False,
    )
```

```python
import functools
import math

import jax
import jax.numpy as jnp
from jax import lax
from jax.experimental import pallas as pl
from jax.experimental.pallas import tpu as pltpu
from jax.sharding import PartitionSpec as P

F32 = jnp.float32
BF16 = jnp.bfloat16


class Copies:
    def __init__(self, sems):
        self.sems, self.used, self.open = sems, 0, {}

    def start(self, name, source, target):
        copy = pltpu.make_async_copy(source, target, self.sems.at[self.used])
        self.used += 1
        copy.start()
        self.open[name] = copy

    def need(self, *names):
        for name in names:
            if name in self.open:
                self.open.pop(name).wait()

    def finish(self):
        self.need(*list(self.open))


def half_erf(value):
    return 0.5 * (1.0 + lax.erf(value * 0.7071067811865476))


def smooth_gate(value):
    return value * half_erf(value)


def gate_slope(value, half):
    return half + value * jnp.exp(-0.5 * value * value) * 0.3989422804014327


def fill_shifts(stack, field, ydim, zdim):
    rows, width = field.shape
    cells = field.reshape(rows // zdim, zdim, width)
    depth = lax.broadcasted_iota(jnp.int32, cells.shape, 1)
    before = jnp.where(depth == 0, 0.0, pltpu.roll(cells, 1, 1))
    after = jnp.where(depth == zdim - 1, 0.0, pltpu.roll(cells, zdim - 1, 1))
    for across, moved in enumerate((before, cells, after)):
        moved = moved.reshape(rows // (ydim * zdim), ydim, zdim, width)
        blank = jnp.zeros_like(moved[:, :1])
        shifted = (
            jnp.concatenate([blank, moved[:, :-1]], axis=1),
            moved,
            jnp.concatenate([moved[:, 1:], blank], axis=1),
        )
        for down in range(3):
            at = (3 * down + across) * width
            stack[0:rows, at : at + width] = shifted[down].reshape(rows, width).astype(BF16)


def convolve(stack, weights, rows, plane):
    total = None
    for step in range(3):
        part = jnp.dot(
            stack[step * plane : step * plane + rows, :],
            weights[step],
            preferred_element_type=F32,
        )
        total = part if total is None else total + part
    return total


def pack_edges(odd, state, act, grad, near, far, plane):
    width = state.shape[1] // 2
    cells = state.shape[0]
    left, right = slice(0, width), slice(width, 2 * width)

    def put(at, size, source, half):
        low = source[0:size, half]
        high = source[cells - size : cells, half]
        near[at : at + size, :] = jnp.where(odd, low, high)
        far[at : at + size, :] = jnp.where(odd, high, low)

    for index, (source, half) in enumerate(((state, right), (act, left), (grad, right))):
        put(index * 2 * plane, 2 * plane, source, half)
    for index, (source, half) in enumerate(((state, left), (act, right), (grad, left))):
        put((6 + index) * plane, plane, source, half)


def edges_kernel(plane, state, act, grad, near_out, far_out, fields_out, near, far, fields, sems):
    copies = Copies(sems)
    for index, source in enumerate((state, act, grad)):
        copies.start(index, source, fields.at[index])
    copies.finish()
    odd = lax.rem(lax.axis_index("space"), 2) == 1
    copies.start("fields", fields, fields_out)
    pack_edges(odd, fields.at[0], fields.at[1], fields.at[2], near, far, plane)
    copies.start("near", near, near_out)
    copies.start("far", far, far_out)
    copies.finish()


def join_kernel(plane, forward, lifted, lowered, fresh, target, state, act, grad, near, far):
    place = lax.axis_index("section")
    first_place, last_place = place == 0, place == lax.axis_size("section") - 1
    state[...] = jnp.where(first_place, fresh[...], lifted[0])
    own = forward[...]
    act[...] = jnp.where(last_place, own, lowered[0])
    error = (own.astype(F32) - target[...].astype(F32)).astype(BF16)
    grad[...] = jnp.where(last_place, error, lowered[1])
    pack_edges(lax.rem(lax.axis_index("space"), 2) == 1, state, act, grad, near, far, plane)


def own_kernel(ydim, zdim, state, act, grad, first, second, second_back, partial, stack):
    own_sums(ydim, zdim, gated_fields(state, act, grad), (first, second, second_back), partial, stack)


def flip_kernel(first, second, fields, first_out, second_out, first_back, second_back, state, act, grad):
    for index, out in enumerate((state, act, grad)):
        out[...] = fields[index]
    first_out[...] = first[...]
    second_out[...] = second[...]
    offsets = first.shape[0]
    for source, out in ((first, first_back), (second, second_back)):
        for k in range(offsets):
            out[offsets - 1 - k] = jnp.transpose(source[k])


def own_sums(ydim, zdim, fields, weights, partial, stack):
    plane = ydim * zdim
    for index, (field, weight) in enumerate(zip(fields, weights)):
        fill_shifts(stack, field, ydim, zdim)
        cells = field.shape[0]
        ahead, level, behind = [
            jnp.dot(stack[0:cells, :], weight[step], preferred_element_type=F32) for step in range(3)
        ]
        end = cells - plane
        partial[index, 0:plane, :] = behind[0:plane]
        partial[index, plane : 2 * plane, :] = behind[plane : 2 * plane] + level[0:plane]
        partial[index, 2 * plane : cells, :] = (
            behind[2 * plane :] + level[plane:end] + ahead[0 : end - plane]
        )
        partial[index, cells : cells + plane, :] = level[end:] + ahead[end - plane : end]
        partial[index, cells + plane :, :] = ahead[end:]


def gated_fields(state, act, grad):
    width = state.shape[1] // 2
    return (
        smooth_gate(state[:, width:].astype(F32)),
        smooth_gate(act[:, :width].astype(F32)),
        grad[:, width:].astype(F32),
    )


def halo_sums(index, partial, stack, weights, plane):
    total = partial[index]
    inner = total.shape[0]
    low = jnp.dot(stack[0 : 2 * plane, :], weights[0], preferred_element_type=F32)
    both = jnp.dot(stack[plane : 3 * plane, :], weights[1], preferred_element_type=F32)
    high = jnp.dot(stack[2 * plane : 4 * plane, :], weights[2], preferred_element_type=F32)
    return jnp.concatenate(
        [
            total[0:plane] + low[0:plane] + both[0:plane],
            total[plane : 2 * plane] + low[plane:],
            total[2 * plane : inner - 2 * plane],
            total[inner - 2 * plane : inner - plane] + high[0:plane],
            total[inner - plane :] + high[plane:] + both[plane:],
        ],
        axis=0,
    )


def first_kernel(ydim, zdim, copies, made, state, act, grad, near, far, first, second, second_back, partial,
                 new_one, back_two, mid, back, carry, gate, stack):
    plane = ydim * zdim
    cells, double = state.shape
    width = double // 2
    inner = cells + 2 * plane
    outer = cells + 4 * plane
    left, right = slice(0, width), slice(width, double)

    spot = lax.axis_index("space")
    odd = lax.rem(spot, 2) == 1

    def around(source, half, at, size):
        one_side, other_side = near[at : at + size, :], far[at : at + size, :]
        below = jnp.where(odd, one_side, other_side)
        above = jnp.where(odd, other_side, one_side)
        return jnp.concatenate([below, source[:, half], above], axis=0).astype(F32)

    def two(source, half, index):
        return around(source, half, index * 2 * plane, 2 * plane)

    def outside(field):
        return jnp.concatenate([field[0 : 2 * plane], field[2 * plane + cells :]], axis=0)

    def one(source, half, index):
        return around(source, half, (6 + index) * plane, plane)

    inside_low, inside_high = spot > 0, spot < lax.axis_size("space") - 1

    def store_masked(ref, value):
        blank = jnp.zeros((plane, width), BF16)
        ref[0:plane, :] = jnp.where(inside_low, value[0:plane], blank)
        ref[plane : plane + cells, :] = value[plane : plane + cells]
        ref[plane + cells : inner, :] = jnp.where(inside_high, value[plane + cells :], blank)

    core = slice(plane, plane + cells)
    copies.need("near", "far", "state")
    fill_shifts(stack, smooth_gate(outside(two(state, right, 0))), ydim, zdim)
    copies.need("first")
    f_one = (one(state, left, 0) + halo_sums(0, partial, stack, first, plane)).astype(BF16)
    new_one[...] = f_one[core]
    store_masked(mid, smooth_gate(f_one.astype(F32)).astype(BF16))

    made("new_one", "mid")

    copies.need("act")
    y_one = two(act, left, 1)
    half = half_erf(y_one)
    gated = y_one * half
    gate[...] = gated[plane : plane + inner].astype(BF16)
    fill_shifts(stack, outside(gated), ydim, zdim)
    copies.need("second")
    r_two = (one(act, right, 1) - halo_sums(1, partial, stack, second, plane)).astype(BF16)
    back_two[...] = r_two[core]
    store_masked(back, smooth_gate(r_two.astype(F32)).astype(BF16))

    made("gate", "back_two", "back")

    copies.need("grad")
    fill_shifts(stack, outside(two(grad, right, 2)), ydim, zdim)
    slope = gate_slope(y_one[plane : plane + inner], half[plane : plane + inner])
    copies.need("second_back")
    e_one = (one(grad, left, 2) + slope * halo_sums(2, partial, stack, second_back, plane)).astype(BF16)
    store_masked(carry, e_one)
    made("carry")


def second_kernel(ydim, zdim, copies, made, state, act, grad, new_one, back_two, mid, back, carry,
                  first, second, first_back, forward, rebuilt, passed, stack):
    plane = ydim * zdim
    cells, double = state.shape
    width = double // 2
    left, right = slice(0, width), slice(width, double)

    copies.need("back", "act", "back_two")
    fill_shifts(stack, back[...].astype(F32), ydim, zdim)
    rebuilt[:, right] = back_two[...]
    copies.need("first")
    rebuilt[:, left] = (
        act[:, left].astype(F32) - convolve(stack, first, cells, plane)
    ).astype(BF16)
    made("rebuilt")
    copies.need("carry", "grad")
    fill_shifts(stack, carry[...].astype(F32), ydim, zdim)
    passed[:, left] = carry[plane : plane + cells, :]
    r_two = back_two[...].astype(F32)
    copies.need("first_back")
    passed[:, right] = (
        grad[:, right].astype(F32)
        + gate_slope(r_two, half_erf(r_two)) * convolve(stack, first_back, cells, plane)
    ).astype(BF16)
    made("passed")
    copies.need("mid", "state", "new_one")
    fill_shifts(stack, mid[...].astype(F32), ydim, zdim)
    forward[:, left] = new_one[...]
    copies.need("second")
    forward[:, right] = (
        state[:, right].astype(F32) + convolve(stack, second, cells, plane)
    ).astype(BF16)
    made("forward")


def tick_kernel(ydim, zdim, paired, state, act, grad, near, far, first, second,
                first_back, second_back, partial, forward, sent, back, carry, gate, new_one, back_two, mid,
                rebuilt, stack):
    copies = Copies(None)
    ignore = lambda *names: None
    first_kernel(ydim, zdim, copies, ignore, state, act, grad, near, far, first, second,
                 second_back, partial, new_one, back_two, mid, back, carry, gate, stack)
    second_kernel(ydim, zdim, copies, ignore, state, act, grad, new_one, back_two, mid, back, carry,
                  first, second, first_back, forward, rebuilt, sent.at[1], stack)
    if paired:
        sent[0] = jnp.where(lax.axis_index("section") == 0, forward[...], rebuilt[...])
    else:
        sent[0] = rebuilt[...]


def correlate(stack, field, cotangent, ydim, zdim, emit):
    plane = ydim * zdim
    cells, width = cotangent.shape
    fill_shifts(stack, cotangent, ydim, zdim)
    for step in range(3):
        product = lax.dot_general(
            field[step * plane : step * plane + cells, :],
            stack[0:cells, :],
            (((0,), (0,)), ((), ())),
            preferred_element_type=F32,
        )
        for place in range(9):
            emit(9 * step + 8 - place, product[:, place * width : (place + 1) * width])


def both_grads(ydim, zdim, grad, back, carry, gate, stack, put):
    plane = ydim * zdim
    cells, double = grad.shape
    width = double // 2

    def store(which):
        return lambda k, block: put(which, slice(k * width, (k + 1) * width), block)

    own = carry[plane : plane + cells, :].astype(F32)
    correlate(stack, back, own, ydim, zdim, store(0))
    correlate(stack, gate, grad[:, width:].astype(F32), ydim, zdim, store(1))


def corr_kernel(ydim, zdim, grad, back, carry, gate, out, stack):
    def put(which, at, block):
        out[which, at, :] = block

    both_grads(ydim, zdim, grad, back, carry, gate, stack, put)


def ways_of(count, rows):
    bits = [1 << level for level in range(count.bit_length() - 1)]
    turning, last = bits[:-1], bits[-1:]
    ways = 3
    span = 2 * rows // ways
    orders = [turning[way % len(turning) :] + turning[: way % len(turning)] + last for way in range(ways)]
    return [(way * span, span, order) for way, order in enumerate(orders)]


def last_kernel(ydim, zdim, factor, count, direct, state, act, grad, near, far, first,
                second, first_back, second_back, partial, so_far, *args):
    n_outs = 6 if direct else 1
    results_out, args = args[:3], args[3:]
    final_outs, args = args[:n_outs], args[n_outs:]
    results, args = args[:3], args[3:]
    refs, args = args[:n_outs], args[n_outs:]
    new_one, back_two, mid, back, carry, gate, stack, sums, sems = args
    copies = Copies(sems)
    ignore = lambda *names: None
    first_kernel(ydim, zdim, copies, ignore, state, act, grad, near, far, first, second,
                 second_back, partial, new_one, back_two, mid, back, carry, gate, stack)

    def put(which, at, block):
        sums[which, at, :] = (block + so_far[which, at, :]) * factor

    both_grads(ydim, zdim, grad, back, carry, gate, stack, put)
    if not direct:
        refs[0][...] = sums[...].astype(BF16)
        copies.start("out", refs[0], final_outs[0])
    rows = sums.shape[1] // count
    for index, (start, span, order) in enumerate(ways_of(count, rows) if direct else ()):
        mine = lax.rem(lax.div(lax.axis_index("space"), order[0]), 2)
        for kept in (0, 1):
            side = mine if kept else 1 - mine
            out = refs[2 * index + (0 if kept else 1)]
            for j in range(count // 2):
                fixed = sum(
                    bit for level, bit in enumerate(order[1:]) if (j >> (len(order) - 2 - level)) & 1
                )
                block = fixed + side * order[0]
                pieces = []
                for which in range(2):
                    lower = max(start, which * rows)
                    upper = min(start + span, (which + 1) * rows)
                    if lower < upper:
                        at = pl.multiple_of(block * rows + (lower - which * rows), 8)
                        pieces.append(sums[which, pl.ds(at, upper - lower), :])
                value = pieces[0] if len(pieces) == 1 else jnp.concatenate(pieces, axis=0)
                out[j] = value.astype(BF16)
            at = 2 * index + (0 if kept else 1)
            copies.start(("half", at), out, final_outs[at])

    where = {"forward": 0, "rebuilt": 1, "passed": 2}

    def made(name):
        copies.start("out_" + name, results[where[name]], results_out[where[name]])

    second_kernel(ydim, zdim, copies, made, state, act, grad, new_one, back_two, mid, back, carry, first,
                  second, first_back, *results, stack)
    copies.finish()


def split_blocks(sums, count):
    blocks = jnp.concatenate([part.reshape(count, -1, part.shape[-1]) for part in sums], axis=1)
    spot = lax.axis_index("space")
    halves = []
    for start, span, order in ways_of(count, blocks.shape[1] // 2):
        part = blocks[:, start : start + span]
        part = part.reshape([2] * len(order) + list(part.shape[1:]))
        levels = [len(order) - bit.bit_length() for bit in order]
        part = jnp.transpose(part, levels + [len(order), len(order) + 1])
        part = part.reshape((2, count // 2) + part.shape[-2:])
        mine = (spot // order[0]) % 2
        for side in (mine, 1 - mine):
            halves.append(lax.dynamic_index_in_dim(part, side, 0, keepdims=False))
    return halves


def reduce_blocks(halves, count, rows):
    spot = lax.axis_index("space")
    ways = [
        (halves[2 * way], halves[2 * way + 1], order)
        for way, (_, _, order) in enumerate(ways_of(count, rows))
    ]
    def halved(total, bit):
        total = total.astype(BF16)
        total = total.reshape((2, total.shape[0] // 2) + total.shape[1:])
        mine = (spot // bit) % 2
        keep = lax.dynamic_index_in_dim(total, mine, 0, keepdims=False)
        return keep, lax.dynamic_index_in_dim(total, 1 - mine, 0, keepdims=False)

    def swapped(send, bit):
        return lax.ppermute(send, "space", [(i, i ^ bit) for i in range(count)]).astype(F32)

    depth = count.bit_length() - 1
    for step in range(depth - 1):
        later = []
        for keep, send, order in ways:
            total = keep.astype(F32) + swapped(send, order[step])
            later.append((*halved(total, order[step + 1]), order))
        ways = later
    keep = jnp.concatenate([keep[0] for keep, _, _ in ways], axis=0)
    send = jnp.concatenate([send[0] for _, send, _ in ways], axis=0)
    return keep.astype(F32) + swapped(send, ways[0][2][-1])


def shards(fwd_in, bwd_act, bwd_grad, fresh, target, w_first, w_second):
    width = w_first.shape[2]
    layers, ydim, zdim = fwd_in.shape[1:4]
    plane = ydim * zdim
    cells = layers * plane
    shape = fwd_in.shape[1:]
    flat = lambda block: block.reshape(cells, 2 * width)
    first = w_first[0].reshape(3, 9 * width, width)
    second = w_second[0].reshape(3, 9 * width, width)
    last_section = lax.axis_size("section") - 1
    place = lax.axis_index("section")
    count = lax.axis_size("space")
    beside = [(i, i ^ 1) for i in range(count) if i ^ 1 < count]
    across = [pair for i in range(1, count - 1, 2) for pair in ((i, i + 1), (i + 1, i))]
    array = jax.ShapeDtypeStruct
    edge = array((9 * plane, width), BF16)
    tile = array((cells, width), BF16)
    wide = array((cells + 2 * plane, width), BF16)
    state_shape = array((cells, 2 * width), BF16)
    offsets = 27 * width

    def exchange(near, far):
        far = lax.ppermute(far, "space", across)
        near = lax.ppermute(near, "space", beside)
        return near, far

    state, act, grad = flat(fwd_in), flat(bwd_act), flat(bwd_grad)
    hbm = pl.BlockSpec(memory_space=pltpu.HBM)
    outer_stack = array((cells + 4 * plane, 9 * width), BF16)
    small_stack = array((cells, 9 * width), BF16)
    weight = array((3, 9 * width, width), BF16)
    raw_weight = array((27, width, width), BF16)
    sums_shape = array((2, offsets, width), F32)

    vmem = pl.BlockSpec(memory_space=pltpu.VMEM)

    def call(kernel, name, inputs, outs, scratch, grant, copies=0, places=(vmem, vmem), flops=0,
             far=0):
        semaphores = [pltpu.SemaphoreType.DMA((copies,))] if copies else []
        return pl.pallas_call(
            kernel,
            out_shape=tuple(outs),
            in_specs=[places[0]] * (len(inputs) - far) + [hbm] * far,
            out_specs=(places[1],) * len(outs),
            scratch_shapes=[pltpu.VMEM(like.shape, like.dtype) for like in scratch] + semaphores,
            compiler_params=pltpu.CompilerParams(vmem_limit_bytes=grant),
            cost_estimate=pl.CostEstimate(
                flops=flops, bytes_accessed=sum(x.size * 2 for x in inputs), transcendentals=0
            ),
            name=name,
        )(*inputs)

    work = 2 * 27 * cells * width * width
    fields_shape = array((3, cells, 2 * width), BF16)
    near, far, fields = call(
        functools.partial(edges_kernel, plane), "edges", (state, act, grad), (edge, edge, fields_shape),
        (edge, edge, fields_shape), 65408 * 1024, 6, (hbm, hbm),
    )
    near, far = exchange(near, far)
    held = call(
        flip_kernel, "flip", (w_first[0], w_second[0], fields),
        (raw_weight,) * 4 + (state_shape,) * 3, (), 16 * 1024 * 1024,
    )
    first_held, second_held, first_back, second_back = (part.reshape(weight.shape) for part in held[:4])
    state, act, grad = held[4:]

    partial_shape = array((3, cells + 2 * plane, width), F32)

    def own(state, act, grad, first, second):
        (partial,) = call(
            functools.partial(own_kernel, ydim, zdim), "own_sums",
            (state, act, grad, first, second, second_back), (partial_shape,), (small_stack,),
            16 * 1024 * 1024, flops=2 * work,
        )
        return partial

    partial = own(state, act, grad, first_held, second_held)
    paired = last_section == 1
    pair_shape = array((2, cells, 2 * width), BF16)
    tick_outs = (state_shape, pair_shape, wide, wide, wide)
    forward, sent, back, carry, gate = call(
        functools.partial(tick_kernel, ydim, zdim, paired), "tick_one",
        (state, act, grad, near, far, first_held, second_held, first_back, second_back, partial),
        tick_outs,
        (tile, tile, wide, state_shape, outer_stack), 16 * 1024 * 1024, flops=8 * work,
    )
    if paired:
        lifted = lowered = lax.ppermute(sent, "section", [(0, 1), (1, 0)])
    else:
        lifted = lax.ppermute(forward[None], "section", [(s, s + 1) for s in range(last_section)])
        lowered = lax.ppermute(sent, "section", [(s + 1, s) for s in range(last_section)])

    join_outs = (state_shape,) * 3 + (edge, edge)
    state_two, act_two, grad_two, near, far = call(
        functools.partial(join_kernel, plane), "join",
        (forward, lifted, lowered, flat(fresh), flat(target)), join_outs,
        (), 16 * 1024 * 1024,
    )
    near, far = exchange(near, far)
    (so_far,) = call(
        functools.partial(corr_kernel, ydim, zdim), "weight_grads", (flat(bwd_grad), back, carry, gate),
        (sums_shape,), (small_stack,), 16 * 1024 * 1024, flops=2 * work,
    )

    partial = own(state_two, act_two, grad_two, first, second)
    rows = offsets // count
    direct = rows % 24 == 0
    if direct:
        span = 2 * rows // 3
        outs = (array((count // 2, span, width), BF16),) * 6
    else:
        outs = (array((2, offsets, width), BF16),)
    factor = 1.0 / math.sqrt(cells * count)
    results = (state_shape,) * 3
    made = call(
        functools.partial(last_kernel, ydim, zdim, factor, count, direct), "tick_two",
        (state_two, act_two, grad_two, near, far, first, second, first_back, second_back, partial,
         so_far),
        results + outs,
        results + outs + (tile, tile, wide, wide, wide, wide, outer_stack, sums_shape),
        32 * 1024 * 1024, 10, (vmem, hbm), 9 * work,
    )
    forward, rebuilt, passed = made[:3]
    halves = made[3:] if direct else split_blocks(made[3], count)
    total = reduce_blocks(halves, count, rows)
    return (
        forward.reshape((1,) + shape),
        rebuilt.reshape((1,) + shape),
        passed.reshape((1,) + shape),
        total[:rows][None],
        total[rows:][None],
    )


def solution(mesh):
    placed = (
        P("section", "space", None, None, None),
        P("section", "space", None, None, None),
        P("section", "space", None, None, None),
        P("space", None, None, None),
        P("space", None, None, None),
        P("section", None, None, None),
        P("section", None, None, None),
    )
    return jax.shard_map(
        shards,
        mesh=mesh,
        in_specs=placed,
        out_specs=(
            P("section", "space", None, None, None),
            P("section", "space", None, None, None),
            P("section", "space", None, None, None),
            P("section", "space", None),
            P("section", "space", None),
        ),
        check_vma=False,
    )
```
